256 devices in a mesh: row: 8 (over x, y_lo), col: 32 (over y_hi, z, core).
Axes of the slice: x: 4, y: 4 (y_hi: 2, y_lo: 2; y = y_hi * 2 + y_lo), z: 8, core: 2. Of those that a mesh axis runs over, the one named last changes fastest.
Arguments:
- scores: float32 [65536, 256], P(('row', 'col')), may hold values from 0.2 to 2, as said below
- tile_values: bfloat16 [24576, 128, 128], P(('row', 'col')), as said below
- tile_rows: int32 [24576], P(('row', 'col')), may hold values from 0 to 511, as said below
- tile_cols: int32 [24576], P(('row', 'col')), may hold values from 0 to 511, as said below
- tile_count: int32 [256], P(('row', 'col')), may hold values from 48 to 96, as said below
- seed_ids: int32 [256, 1024], replicated, may hold values from 0 to 65535
Outputs:
- ranks: float32 [65536, 256], P(('row', 'col'))
The draws below stay inside these ranges and needn't reach their ends.
Inputs may be any that keep to these rules, and one draw needn't show every extreme that they name: Device d = r * 32 + c has its tiles in slots d * 96 to d * 96 + tile_count[d] - 1; some device has all 96 slots in use. Every slot of device (r, c) has (tile_rows // 2) % 32 == c; coordinates may repeat, and tiles at equal coordinates add. Every slot of device (r, c) has tile_cols // 64 == r; on each device the active slots are in nondecreasing order of tile_cols. `tile_values`: entries are positive. `scores`: entries are positive.
All inputs are finite; a program needn't handle non-finite values.
Results may differ from the reference program's by a relative error of at most 0.0004.
Values may be sent and summed in bfloat16 or wider, within the bound.
No kernel may reach another device: no remote copies, remote signals or barrier semaphores. Data moves between devices by JAX's collectives and lax.ppermute only.
A program may use at most 64 MiB of HBM per device.

```python
import math
import jax
import jax.numpy as jnp
from jax import lax

TILE = 128
S = 256
BT = 2
KCAP = 96
SEEDS = 1024
ITERS = 2
NT = 512
NV = 65536
N_ROW = 8
N_COL = 32
DEVICES = 256


def tile_layout(key):
    keys = jax.random.split(jax.random.fold_in(key, 71), 4)
    counts = jax.random.randint(keys[0], (DEVICES,), KCAP // 2, KCAP + 1)
    fullest = jax.random.randint(keys[1], (), 0, DEVICES)
    counts = jnp.where(jnp.arange(DEVICES) == fullest, KCAP, counts).astype(jnp.int32)
    positions = jnp.arange(DEVICES * KCAP, dtype=jnp.int32)
    owner = positions // KCAP
    slot_index = positions % KCAP
    grid_row = owner // N_COL
    grid_col = owner % N_COL
    dest_local = jax.random.randint(keys[2], (DEVICES * KCAP,), 0, N_ROW * BT)
    source_local = jax.random.randint(keys[3], (DEVICES * KCAP,), 0, N_COL * BT)
    rows_drawn = (dest_local // BT * N_COL + grid_col) * BT + dest_local % BT
    active = slot_index < counts[owner]
    sort_keys = owner * (2 * N_COL * BT) + jnp.where(active, 0, N_COL * BT) + source_local
    order = jnp.argsort(sort_keys, stable=True)
    rows_sorted = rows_drawn[order]
    source_sorted = source_local[order]
    cols_sorted = grid_row * (N_COL * BT) + source_sorted
    return (counts, rows_sorted.astype(jnp.int32), cols_sorted.astype(jnp.int32))


def draw_tile_count(key, part):
    return tile_layout(key)[0]


def draw_tile_rows(key, part):
    return tile_layout(key)[1]


def draw_tile_cols(key, part):
    return tile_layout(key)[2]


def draw_scores(key, part):
    key = jax.random.fold_in(key, 79)
    values = jnp.exp(jax.random.uniform(key, (NV, S), jnp.float32, math.log(0.2), math.log(2.0)))
    return jnp.clip(values, 0.2, 2.0).astype(jnp.float32)


def draw_tile_values(key, part):
    counts, rows_sorted, cols_sorted = tile_layout(key)
    keys = jax.random.split(jax.random.fold_in(key, 73), 4)
    owner = jnp.arange(DEVICES * KCAP, dtype=jnp.int32) // KCAP
    position = (owner % N_COL).astype(jnp.float32) / max(N_COL - 1, 1)
    multiplier = 2 * jax.random.randint(keys[2], (DEVICES * KCAP,), 0, max(TILE // 2, 1)) + 1
    offset = jax.random.randint(keys[3], (DEVICES * KCAP,), 0, TILE)
    lane = jnp.arange(TILE, dtype=jnp.int32)
    target = (lane[None, :] * multiplier[:, None] + offset[:, None]) % TILE
    dominant = (lane[None, None, :] == target[:, :, None]).astype(jnp.float32)
    device_scale = 3.0 ** position
    column_scale = jnp.exp(jax.random.uniform(keys[1], (NV,), jnp.float32, 0.0, math.log(10.0)))
    rough = jax.random.uniform(keys[0], (DEVICES * KCAP, TILE, TILE), jnp.float32, 0.25, 1.75)
    base = 0.7
    peak = 0.65
    page_ids = cols_sorted[:, None] * TILE + jnp.arange(TILE, dtype=jnp.int32)[None, :]
    scales = column_scale[page_ids]
    pattern = peak * dominant + (1.0 - peak) * rough / TILE
    values = base * BT / KCAP * device_scale[:, None, None] * scales[:, None, :] * pattern
    return values.astype(jnp.bfloat16)


def with_ends(result, stream_key, least, high):
    longest = result.shape.index(max(result.shape))
    spots = []
    for shift in (0, 1):
        where = [jax.random.randint(jax.random.fold_in(stream_key, axis), (), 0, length) for axis, length in enumerate(result.shape)]
        where[longest] = (where[longest] + shift) % result.shape[longest]
        spots.append(tuple(where))
    return result.at[spots[0]].set(least).at[spots[1]].set(high)


def setup_inputs(seed: int = 0) -> dict:
    key_list = jax.random.split(jax.random.key(seed), 7)
    return {
        "scores": draw_scores(jax.random.fold_in(key_list[6], 71), 0),
        "tile_values": draw_tile_values(jax.random.fold_in(key_list[6], 71), 0),
        "tile_rows": draw_tile_rows(jax.random.fold_in(key_list[6], 71), 0),
        "tile_cols": draw_tile_cols(jax.random.fold_in(key_list[6], 71), 0),
        "tile_count": draw_tile_count(jax.random.fold_in(key_list[6], 71), 0),
        "seed_ids": with_ends(jax.random.randint(key_list[5], (S, SEEDS), 0, NV), jax.random.fold_in(key_list[5], 1), 0, NV - 1).astype(jnp.int32),
    }


damping = 0.85
teleport = 0.15


def reference(scores, tile_values, tile_rows, tile_cols, tile_count, seed_ids):
    slot_owner = jnp.arange(DEVICES * KCAP, dtype=jnp.int32) // KCAP
    slot_index = jnp.arange(DEVICES * KCAP, dtype=jnp.int32) % KCAP
    active = slot_index < tile_count[slot_owner]
    tile_sums = jnp.sum(tile_values, axis=1, dtype=jnp.float32)
    tile_sums = jnp.where(active[:, None], tile_sums, jnp.float32(0.0))
    column_sums = jnp.zeros((NT, TILE), jnp.float32).at[tile_cols].add(tile_sums).reshape(NV)
    inverse = 1.0 / jnp.maximum(column_sums, jnp.float32(1.0))
    set_ids = jnp.broadcast_to(jnp.arange(S, dtype=jnp.int32)[:, None], seed_ids.shape)
    restart = jnp.zeros((NV, S), jnp.float32).at[seed_ids, set_ids].add(jnp.float32(1.0))
    tiles_grouped = tile_values.reshape(DEVICES, KCAP, TILE, TILE)
    rows_grouped = tile_rows.reshape(DEVICES, KCAP)
    cols_grouped = tile_cols.reshape(DEVICES, KCAP)
    active_grouped = active.reshape(DEVICES, KCAP)
    current = scores
    for sweep in range(ITERS):
        panels = (current * inverse[:, None]).astype(jnp.bfloat16).reshape(NT, TILE, S)

        def device_step(summed, group):
            block_tiles, rows_here, cols_here, active_here = group
            gathered = panels[cols_here].astype(jnp.float32)
            products = jnp.einsum("kab,kbs->kas", block_tiles.astype(jnp.float32), gathered)
            products = jnp.where(active_here[:, None, None], products, jnp.float32(0.0))
            return summed.at[rows_here].add(products), None

        summed, _ = lax.scan(device_step, jnp.zeros((NT, TILE, S), jnp.float32),
                             (tiles_grouped, rows_grouped, cols_grouped, active_grouped))
        current = damping * summed.reshape(NV, S) + teleport * restart
    return current
```

```python
import jax
import jax.numpy as jnp
from jax import lax
from jax.experimental import pallas as pl
from jax.experimental.pallas import tpu as pltpu
from jax.sharding import PartitionSpec as P

BT = 2
TILE = 128
LANES = 128
damping = 0.85
teleport = 0.15
LOW, HIGH = 0.2, 2.0
STEPS = 65535.0
HALF = 32768.0
FAR = 1 << 30
VMEM = pltpu.VMEM
SMEM = pltpu.SMEM


def vmem(*_):
    return pl.BlockSpec(memory_space=VMEM)


def smem(*_):
    return pl.BlockSpec(memory_space=SMEM)


def params():
    return pltpu.CompilerParams(vmem_limit_bytes=40 * 1024 * 1024)


def column_kernel(source_ref, count_ref, tiles_ref, sums_ref):
    sums_ref[...] = jnp.zeros_like(sums_ref)

    def slot(k, carry):
        column = jnp.sum(tiles_ref[k].astype(jnp.float32), axis=0, keepdims=True)
        sums_ref[pl.ds(source_ref[k], 1), :] += column
        return carry

    lax.fori_loop(0, count_ref[0], slot, 0)


def seed_kernel(first_ref, ids_ref, counts_ref):
    total, lanes = ids_ref.shape
    pages = counts_ref.shape[0]
    first = first_ref[0]
    chunk = 64
    counts_ref[...] = jnp.zeros_like(counts_ref)

    def above(low):
        def step(i, best):
            page = ids_ref[pl.ds(pl.multiple_of(i * chunk, chunk), chunk), :] - first
            found = jnp.where(page > low, page, FAR).reshape(chunk // 8, 8, lanes)
            return jnp.minimum(best, jnp.min(found, axis=0))

        best = lax.fori_loop(0, total // chunk, step, jnp.full((8, lanes), FAR, jnp.int32))
        return jnp.min(best, axis=0, keepdims=True)

    def more(carry):
        return carry[1] < pages

    def walk(carry):
        page_now, _ = carry

        def step(i, inner):
            best, seen = inner
            page = ids_ref[pl.ds(pl.multiple_of(i * chunk, chunk), chunk), :] - first
            found = jnp.where(page > page_now, page, FAR).reshape(chunk // 8, 8, lanes)
            same = jnp.where(page == page_now, 1.0, 0.0).reshape(chunk // 8, 8, lanes)
            return jnp.minimum(best, jnp.min(found, axis=0)), seen + jnp.sum(same, axis=0)

        best, seen = lax.fori_loop(
            0,
            total // chunk,
            step,
            (jnp.full((8, lanes), FAR, jnp.int32), jnp.zeros((8, lanes), jnp.float32)),
        )
        seen = jnp.sum(seen, axis=0, keepdims=True)

        def place(i, inner):
            rows = pl.ds(pl.multiple_of(i * chunk, chunk), chunk)
            here = lax.broadcasted_iota(jnp.int32, (chunk, lanes), 0) + i * chunk
            counts_ref[rows, :] += jnp.where(here == page_now, seen, 0.0)
            return inner

        lax.fori_loop(0, pages // chunk, place, 0)
        later = jnp.min(best, axis=0, keepdims=True)
        return later, jnp.min(later)

    start = above(jnp.full((1, lanes), -1, jnp.int32))
    lax.while_loop(more, walk, (start, jnp.min(start)))


def products(source_ref, target_ref, count_ref, tiles_refs, panel, total, out_ref):
    unroll = 8
    slots = tiles_refs[0].shape[0]
    total[...] = jnp.zeros_like(total)
    for which, tiles_ref in enumerate(tiles_refs):

        def group(g, carry, which=which, tiles_ref=tiles_ref):
            for u in range(unroll):
                k = g * unroll + u
                at = which * slots + k
                target = target_ref[at]
                total[target] += jnp.dot(
                    tiles_ref[k], panel[source_ref[at]], preferred_element_type=jnp.float32
                )
            return carry

        lax.fori_loop(0, (count_ref[which] + unroll - 1) // unroll, group, 0)
    receivers = out_ref.shape[0]
    per = (out_ref.shape[1] - 16) // TILE

    def send(r, carry):
        exponents = []
        for t in range(per):
            block = total[r * per + t]
            top = jnp.maximum(jnp.max(block, axis=0, keepdims=True), 1e-30)
            exponent = jnp.floor(jnp.log2(top)) + 1.0
            exponents.append(exponent)
            code = block * jnp.exp2(16.0 - exponent) + 0.5
            code = jnp.clip(code.astype(jnp.int32), 0, 65535) - 32768
            out_ref[r, t * TILE : (t + 1) * TILE, :] = code.astype(jnp.int16)
        rows = exponents + [jnp.zeros((16 - per, LANES), jnp.float32)]
        tail = jnp.concatenate(rows, axis=0).astype(jnp.int32).astype(jnp.int16)
        out_ref[r, per * TILE : per * TILE + 16, :] = tail
        return carry

    lax.fori_loop(0, receivers, send, 0)


def first_kernel(pieces, source_ref, target_ref, count_ref, chip_ref, sums_ref, own_ref, sib_ref, *refs):
    piece_refs = refs[:pieces]
    out_ref, inverse_ref, panel, total, ordered = refs[pieces:]
    per = piece_refs[0].shape[0] // TILE
    ordered[...] = jnp.zeros_like(ordered)
    for p in range(pieces):
        ordered[p * per : (p + 1) * per, :] = sums_ref[chip_ref[p]]
    inverse = (1.0 / jnp.maximum(ordered[...], 1.0)).T
    for p in range(pieces):
        for t in range(per):
            column = inverse[:, p * per + t : p * per + t + 1]
            code = piece_refs[p][t * TILE : (t + 1) * TILE, :].astype(jnp.float32)
            score = (code + HALF) * ((HIGH - LOW) / STEPS) + LOW
            panel[chip_ref[p] * per + t] = (score * column).astype(jnp.bfloat16)
            if p == 0:
                inverse_ref[t * TILE : (t + 1) * TILE, :] = jnp.broadcast_to(column, (TILE, LANES))
    products(source_ref, target_ref, count_ref, (own_ref, sib_ref), panel, total, out_ref)


def later_kernel(pieces, source_ref, target_ref, count_ref, chip_ref, own_ref, sib_ref, *refs):
    piece_refs = refs[:pieces]
    out_ref, panel, total = refs[pieces:]
    per = piece_refs[0].shape[0] // TILE
    for p in range(pieces):
        for t in range(per):
            panel[chip_ref[p] * per + t] = piece_refs[p][t * TILE : (t + 1) * TILE, :]
    products(source_ref, target_ref, count_ref, (own_ref, sib_ref), panel, total, out_ref)


def current_kernel(scaled, parts_ref, restart_ref, inverse_ref, out_ref):
    senders = parts_ref.shape[0]
    per = (parts_ref.shape[1] - 16) // TILE
    for t in range(per):
        rows = slice(t * TILE, (t + 1) * TILE)
        summed = jnp.zeros((TILE, LANES), jnp.float32)
        for r in range(senders):
            tail = parts_ref[r, per * TILE : per * TILE + 16, :].astype(jnp.float32)
            scale = jnp.exp2(tail[t : t + 1, :] - 16.0)
            summed += (parts_ref[r, rows, :].astype(jnp.float32) + HALF) * scale
        current = damping * summed + teleport * restart_ref[rows, :]
        if scaled:
            current = current * inverse_ref[rows, :]
        out_ref[rows, :] = current.astype(out_ref.dtype)


def per_device(scores, tile_values, tile_rows, tile_cols, tile_count, seed_ids):
    grid_rows = lax.axis_size("row")
    grid_cols = lax.axis_size("col")
    row_index = lax.axis_index("row")
    col_index = lax.axis_index("col")
    depth = grid_cols // 4
    high, z, core = col_index // (2 * depth), col_index // 2 % depth, col_index % 2
    own_rows = scores.shape[0]
    columns = scores.shape[1]
    slots = tile_values.shape[0]
    seed_total = seed_ids.shape[1]
    band_tiles = grid_cols * BT
    chips = grid_cols // 2
    per = 2 * BT

    def by_col(value, move):
        pairs = []
        for c in range(grid_cols):
            y, at, k = move(c // (2 * depth), c // 2 % depth, c % 2)
            pairs.append((c, (y * depth + at) * 2 + k))
        return lax.ppermute(value, "col", pairs)

    def sibling(value):
        return by_col(value, lambda y, at, k: (y, at, 1 - k))

    def along(value, step):
        return by_col(value, lambda y, at, k: (y, (at + step) % depth, k))

    def across(value):
        return by_col(value, lambda y, at, k: (1 - y, at, k))

    def gather(block):
        other = across(block)
        pieces = [block, other]
        names = [(0, 0), (1, 0)]
        a, b, c, d = block, block, other, other
        for step in range(1, depth // 2):
            a, b = along(a, 1), along(b, -1)
            c, d = along(c, 1), along(d, -1)
            pieces += [a, b, c, d]
            names += [(0, -step), (0, step), (1, -step), (1, step)]
        pieces += [along(a, 1), along(d, -1)]
        names += [(0, depth // 2), (1, depth // 2)]
        return pieces, names

    half = columns // 2
    code = ((scores - LOW) * (STEPS / (HIGH - LOW)) + 0.5).astype(jnp.int32)
    code = (jnp.clip(code, 0, 65535) - 32768).astype(jnp.int16)
    mine = lax.dynamic_slice_in_dim(code, core * half, half, 1)
    theirs = sibling(lax.dynamic_slice_in_dim(code, (1 - core) * half, half, 1))
    block = jnp.where(
        core == 0, jnp.concatenate([mine, theirs]), jnp.concatenate([theirs, mine])
    )
    sources = tile_cols - row_index * band_tiles
    targets = tile_rows // band_tiles * per + core * BT + tile_rows % BT
    targets = jnp.where(jnp.arange(slots) < tile_count[0], targets, grid_rows * per)
    facts = jnp.stack([sources, targets, jnp.broadcast_to(tile_count, (slots,))])
    sib_facts = sibling(facts)
    sib_tiles = sibling(tile_values)

    sums = pl.pallas_call(
        column_kernel,
        out_shape=jax.ShapeDtypeStruct((band_tiles, TILE), jnp.float32),
        in_specs=[smem(), smem(), vmem()],
        out_specs=vmem(),
        compiler_params=params(),
        name="column_sums",
    )(sources, tile_count, tile_values)
    sums = sums + sibling(sums)
    step = 1
    while step < depth:
        sums = sums + by_col(sums, lambda y, at, k, step=step: (y, at ^ step, k))
        step *= 2
    sums = sums + across(sums)

    first_page = (row_index * grid_cols + col_index - core) * own_rows
    ids = lax.dynamic_slice_in_dim(seed_ids, core * half, half, 0).T
    restart = pl.pallas_call(
        seed_kernel,
        out_shape=jax.ShapeDtypeStruct((2 * own_rows, half), jnp.float32),
        in_specs=[smem(), vmem()],
        out_specs=vmem(),
        compiler_params=params(),
        name="seed_counts",
    )(first_page.reshape(1), ids)

    slot_sources = jnp.concatenate([sources, sib_facts[0]])
    slot_targets = jnp.concatenate([targets, sib_facts[1]])
    counts = jnp.concatenate([tile_count, sib_facts[2, :1]])

    def multiply(pieces, names, sums):
        order = jnp.stack([(high ^ y) * depth + (z + d) % depth for y, d in names])
        n = len(pieces)
        parts = jax.ShapeDtypeStruct((grid_rows, per * TILE + 16, half), jnp.int16)
        scratch = [
            VMEM((band_tiles, TILE, half), jnp.bfloat16),
            VMEM((grid_rows * per + 1, TILE, half), jnp.float32),
        ]
        if sums is not None:
            return pl.pallas_call(
                lambda *refs: first_kernel(n, *refs),
                out_shape=(parts, jax.ShapeDtypeStruct((per * TILE, half), jnp.float32)),
                in_specs=[smem()] * 4 + [vmem()] * (3 + n),
                out_specs=(vmem(), vmem()),
                scratch_shapes=scratch + [VMEM((TILE, TILE), jnp.float32)],
                compiler_params=params(),
                name="first_products",
            )(
                slot_sources, slot_targets, counts, order,
                sums.reshape(chips, per, TILE), tile_values, sib_tiles, *pieces,
            )
        return pl.pallas_call(
            lambda *refs: later_kernel(n, *refs),
            out_shape=parts,
            in_specs=[smem()] * 4 + [vmem()] * (2 + n),
            out_specs=vmem(),
            scratch_shapes=scratch,
            compiler_params=params(),
            name="later_products",
        )(slot_sources, slot_targets, counts, order, tile_values, sib_tiles, *pieces)

    def update(parts, inverse, scaled):
        return pl.pallas_call(
            lambda *refs: current_kernel(scaled, *refs),
            out_shape=jax.ShapeDtypeStruct(
                (per * TILE, half), jnp.bfloat16 if scaled else jnp.float32
            ),
            in_specs=[vmem()] * 3,
            out_specs=vmem(),
            compiler_params=params(),
            name="current",
        )(parts, restart, inverse)

    pieces, names = gather(block)
    parts, inverse = multiply(pieces, names, sums)
    parts = lax.all_to_all(parts, "row", 0, 0, tiled=True)
    panel = update(parts, inverse, True)
    pieces, names = gather(panel)
    parts = multiply(pieces, names, None)
    parts = lax.all_to_all(parts, "row", 0, 0, tiled=True)
    current = update(parts, inverse, False)
    mine = lax.dynamic_slice_in_dim(current, core * own_rows, own_rows, 0)
    theirs = sibling(lax.dynamic_slice_in_dim(current, (1 - core) * own_rows, own_rows, 0))
    return jnp.where(
        core == 0,
        jnp.concatenate([mine, theirs], axis=1),
        jnp.concatenate([theirs, mine], axis=1),
    )


def solution(mesh):
    placed = (
        P(("row", "col"), None),
        P(("row", "col"), None, None),
        P(("row", "col")),
        P(("row", "col")),
        P(("row", "col")),
        P(),
    )
    return jax.shard_map(
        per_device, mesh=mesh, in_specs=placed, out_specs=P(("row", "col"), None), check_vma=False
    )
```

```python
import jax
import jax.numpy as jnp
from jax import lax
from jax.experimental import pallas as pl
from jax.experimental.pallas import tpu as pltpu
from jax.sharding import PartitionSpec as P

BT = 2
TILE = 128
LANES = 128
damping = 0.85
teleport = 0.15
LOW, HIGH = 0.2, 2.0
STEPS = 65535.0
HALF = 32768.0
FAR = 1 << 30
VMEM = pltpu.VMEM
SMEM = pltpu.SMEM


def vmem(*_):
    return pl.BlockSpec(memory_space=VMEM)


def smem(*_):
    return pl.BlockSpec(memory_space=SMEM)


def in_hbm(value):
    return pltpu.with_memory_space_constraint(value, pltpu.HBM)


def params():
    return pltpu.CompilerParams(vmem_limit_bytes=16 * 1024 * 1024)


def column_kernel(source_ref, count_ref, given_ref, sums_ref, tiles_ref, arrived):
    slots = given_ref.shape[0]
    chunk = slots // arrived.shape[0]
    copies = []
    for c in range(arrived.shape[0]):
        span = pl.ds(c * chunk, chunk)
        copies.append(
            pltpu.make_async_copy(given_ref.at[span], tiles_ref.at[span], arrived.at[c])
        )
        copies[c].start()
    sums_ref[...] = jnp.zeros_like(sums_ref)

    def slot(k, carry):
        column = jnp.sum(tiles_ref[k].astype(jnp.float32), axis=0, keepdims=True)
        sums_ref[pl.ds(source_ref[k], 1), :] += column
        return carry

    for c in range(arrived.shape[0]):
        copies[c].wait()
        lax.fori_loop(c * chunk, jnp.minimum((c + 1) * chunk, count_ref[0]), slot, 0)


def seed_kernel(first_ref, ids_ref, counts_ref):
    total, lanes = ids_ref.shape
    pages = counts_ref.shape[0]
    first = first_ref[0]
    chunk = 64
    counts_ref[...] = jnp.zeros_like(counts_ref)

    def above(low):
        def step(i, best):
            page = ids_ref[pl.ds(pl.multiple_of(i * chunk, chunk), chunk), :] - first
            found = jnp.where(page > low, page, FAR).reshape(chunk // 8, 8, lanes)
            return jnp.minimum(best, jnp.min(found, axis=0))

        best = lax.fori_loop(0, total // chunk, step, jnp.full((8, lanes), FAR, jnp.int32))
        return jnp.min(best, axis=0, keepdims=True)

    def more(carry):
        return carry[1] < pages

    def walk(carry):
        page_now, _ = carry

        def step(i, inner):
            best, seen = inner
            page = ids_ref[pl.ds(pl.multiple_of(i * chunk, chunk), chunk), :] - first
            found = jnp.where(page > page_now, page, FAR).reshape(chunk // 8, 8, lanes)
            same = jnp.where(page == page_now, 1.0, 0.0).reshape(chunk // 8, 8, lanes)
            return jnp.minimum(best, jnp.min(found, axis=0)), seen + jnp.sum(same, axis=0)

        best, seen = lax.fori_loop(
            0,
            total // chunk,
            step,
            (jnp.full((8, lanes), FAR, jnp.int32), jnp.zeros((8, lanes), jnp.float32)),
        )
        seen = jnp.sum(seen, axis=0, keepdims=True)

        def place(i, inner):
            rows = pl.ds(pl.multiple_of(i * chunk, chunk), chunk)
            here = lax.broadcasted_iota(jnp.int32, (chunk, lanes), 0) + i * chunk
            counts_ref[rows, :] += jnp.where(here == page_now, seen, 0.0)
            return inner

        lax.fori_loop(0, pages // chunk, place, 0)
        later = jnp.min(best, axis=0, keepdims=True)
        return later, jnp.min(later)

    start = above(jnp.full((1, lanes), -1, jnp.int32))
    lax.while_loop(more, walk, (start, jnp.min(start)))


UNROLL = 8


def fetch(group, first, facts_ref, own_ref, sib_ref, tiles, arrived):
    slots = own_ref.shape[0]
    side = group % 2
    for u in range(UNROLL):
        tile = facts_ref[0, jnp.minimum(first + group * UNROLL + u, 2 * slots - 1)]

        @pl.when(tile < slots)
        def _(tile=tile, u=u):
            pltpu.make_async_copy(own_ref.at[tile], tiles.at[side, u], arrived.at[side]).start()

        @pl.when(tile >= slots)
        def _(tile=tile, u=u):
            pltpu.make_async_copy(
                sib_ref.at[tile - slots], tiles.at[side, u], arrived.at[side]
            ).start()


def products(first, last, facts_ref, own_ref, sib_ref, panel, total, tiles, arrived):
    slots = own_ref.shape[0]
    dummy = total.shape[0] - 1
    groups = (last - first + UNROLL - 1) // UNROLL

    def step(g, carry):
        @pl.when(g + 1 < groups)
        def _():
            fetch(g + 1, first, facts_ref, own_ref, sib_ref, tiles, arrived)

        side = g % 2
        pltpu.make_async_copy(own_ref.at[pl.ds(0, UNROLL)], tiles.at[side], arrived.at[side]).wait()
        for u in range(UNROLL):
            wanted = first + g * UNROLL + u
            k = jnp.minimum(wanted, 2 * slots - 1)
            live = wanted < last
            target = jnp.where(live, facts_ref[2, k], dummy)
            source = jnp.where(live, facts_ref[1, k], 0)
            rows = pl.ds(pl.multiple_of(source * TILE, TILE), TILE)
            total[target] += jnp.dot(
                tiles[side, u], panel[rows, :], preferred_element_type=jnp.float32
            )
        return carry

    lax.fori_loop(0, groups, step, 0)


def encode(total, out_ref):
    per = (out_ref.shape[1] - 16) // TILE

    def send(r, carry):
        exponents = []
        for t in range(per):
            block = total[r * per + t]
            top = jnp.maximum(jnp.max(block, axis=0, keepdims=True), 1e-30)
            exponent = jnp.floor(jnp.log2(top)) + 1.0
            exponents.append(exponent)
            code = block * jnp.exp2(16.0 - exponent) + 0.5
            code = jnp.clip(code.astype(jnp.int32), 0, 65535) - 32768
            out_ref[r, t * TILE : (t + 1) * TILE, :] = code.astype(jnp.int16)
        rows = exponents + [jnp.zeros((16 - per, LANES), jnp.float32)]
        tail = jnp.concatenate(rows, axis=0).astype(jnp.int32).astype(jnp.int16)
        out_ref[r, per * TILE : per * TILE + 16, :] = tail
        return carry

    lax.fori_loop(0, out_ref.shape[0], send, 0)


def stage_kernel(stage, first, last, coded, counts, *refs):
    refs = list(refs)
    facts_ref, bound_ref, chip_ref = refs[:3]
    del refs[:3]
    sums_ref = refs.pop(0) if coded else None
    own_ref, sib_ref = refs[:2]
    del refs[:2]
    piece_refs = refs[: len(counts)]
    del refs[: len(counts)]
    if not first:
        before = refs.pop(0)
    out_ref = refs.pop(0)
    inverse_ref = refs.pop(0) if coded and first else None
    panel = refs.pop(0)
    ordered = refs.pop(0) if coded else None
    tiles, arrived = refs
    start, end = bound_ref[stage], bound_ref[stage + 1]

    @pl.when(end > start)
    def _():
        fetch(0, start, facts_ref, own_ref, sib_ref, tiles, arrived)

    total = before if last else out_ref
    if first:
        total[...] = jnp.zeros_like(total)
    per = piece_refs[0].shape[0] // TILE // counts[0]
    if coded:
        ordered[...] = jnp.zeros_like(ordered)
        for p in range(sum(counts)):
            ordered[p * per : (p + 1) * per, :] = sums_ref[chip_ref[p]]
        inverse = (1.0 / jnp.maximum(ordered[...], 1.0)).T
    at = 0
    for piece_ref in piece_refs:
        for t in range(piece_ref.shape[0] // TILE):
            rows = piece_ref[t * TILE : (t + 1) * TILE, :]
            if coded:
                column = inverse[:, at : at + 1]
                score = (rows.astype(jnp.float32) + HALF) * ((HIGH - LOW) / STEPS) + LOW
                rows = (score * column).astype(jnp.bfloat16)
                if first and at < per:
                    inverse_ref[at * TILE : (at + 1) * TILE, :] = jnp.broadcast_to(
                        column, (TILE, LANES)
                    )
            panel[at * TILE : (at + 1) * TILE, :] = rows
            at += 1
    products(start, end, facts_ref, own_ref, sib_ref, panel, total, tiles, arrived)
    if last:
        encode(total, out_ref)


def current_kernel(scaled, parts_ref, restart_ref, inverse_ref, out_ref):
    senders = parts_ref.shape[0]
    per = (parts_ref.shape[1] - 16) // TILE
    for t in range(per):
        rows = slice(t * TILE, (t + 1) * TILE)
        summed = jnp.zeros((TILE, LANES), jnp.float32)
        for r in range(senders):
            tail = parts_ref[r, per * TILE : per * TILE + 16, :].astype(jnp.float32)
            scale = jnp.exp2(tail[t : t + 1, :] - 16.0)
            summed += (parts_ref[r, rows, :].astype(jnp.float32) + HALF) * scale
        current = damping * summed + teleport * restart_ref[rows, :]
        if scaled:
            current = current * inverse_ref[rows, :]
        out_ref[rows, :] = current.astype(out_ref.dtype)


def per_device(scores, tile_values, tile_rows, tile_cols, tile_count, seed_ids):
    grid_rows = lax.axis_size("row")
    grid_cols = lax.axis_size("col")
    row_index = lax.axis_index("row")
    col_index = lax.axis_index("col")
    depth = grid_cols // 4
    high, z, core = col_index // (2 * depth), col_index // 2 % depth, col_index % 2
    own_rows = scores.shape[0]
    columns = scores.shape[1]
    slots = tile_values.shape[0]
    seed_total = seed_ids.shape[1]
    band_tiles = grid_cols * BT
    chips = grid_cols // 2
    per = 2 * BT

    def by_col(value, move):
        pairs = []
        for c in range(grid_cols):
            y, at, k = move(c // (2 * depth), c // 2 % depth, c % 2)
            pairs.append((c, (y * depth + at) * 2 + k))
        return lax.ppermute(value, "col", pairs)

    def sibling(value):
        return by_col(value, lambda y, at, k: (y, at, 1 - k))

    def along(value, step):
        return by_col(value, lambda y, at, k: (y, (at + step) % depth, k))

    def across(value):
        return by_col(value, lambda y, at, k: (1 - y, at, k))

    half = columns // 2
    code = ((scores - LOW) * (STEPS / (HIGH - LOW)) + 0.5).astype(jnp.int32)
    code = (jnp.clip(code, 0, 65535) - 32768).astype(jnp.int16)
    mine = lax.dynamic_slice_in_dim(code, core * half, half, 1)
    theirs = sibling(lax.dynamic_slice_in_dim(code, (1 - core) * half, half, 1))
    block = jnp.where(
        core == 0, jnp.concatenate([mine, theirs]), jnp.concatenate([theirs, mine])
    )
    sources = tile_cols - row_index * band_tiles
    targets = tile_rows // band_tiles * per + core * BT + tile_rows % BT
    targets = jnp.where(jnp.arange(slots) < tile_count[0], targets, grid_rows * per)
    facts = jnp.stack([sources, targets, jnp.broadcast_to(tile_count, (slots,))])
    sib_facts = sibling(facts)
    sib_tiles = sibling(tile_values)

    sums = pl.pallas_call(
        column_kernel,
        out_shape=jax.ShapeDtypeStruct((band_tiles, TILE), jnp.float32),
        in_specs=[smem(), smem(), pl.BlockSpec(memory_space=pl.ANY)],
        out_specs=vmem(),
        scratch_shapes=[VMEM(tile_values.shape, tile_values.dtype), pltpu.SemaphoreType.DMA((4,))],
        compiler_params=params(),
        name="column_sums",
    )(sources, tile_count, in_hbm(tile_values))
    sums = sums + sibling(sums)

    first_page = (row_index * grid_cols + col_index - core) * own_rows
    ids = lax.dynamic_slice_in_dim(seed_ids, core * half, half, 0).T
    restart = pl.pallas_call(
        seed_kernel,
        out_shape=jax.ShapeDtypeStruct((2 * own_rows, half), jnp.float32),
        in_specs=[smem(), vmem()],
        out_specs=vmem(),
        compiler_params=params(),
        name="seed_counts",
    )(first_page.reshape(1), ids)

    def stage_names():
        yield [(0, 0), (1, 0)]
        for step in range(1, depth // 2):
            yield [(0, -step), (1, -step), (0, step), (1, step)]
        yield [(0, depth // 2), (1, depth // 2)]

    chip_lists = [
        jnp.stack([(high ^ y) * depth + (z + d) % depth for y, d in names])
        for names in stage_names()
    ]
    stage_of = jnp.concatenate(
        [jnp.full((c.shape[0],), i, jnp.int32) for i, c in enumerate(chip_lists)]
    )
    place_of = jnp.concatenate([jnp.arange(c.shape[0], dtype=jnp.int32) for c in chip_lists])
    all_chips = jnp.concatenate(chip_lists)
    stage_total = len(chip_lists)
    slot_ids = jnp.arange(2 * slots, dtype=jnp.int32)
    source = jnp.concatenate([sources, sib_facts[0]])
    target = jnp.concatenate([targets, sib_facts[1]])
    hit = (source // per)[:, None] == all_chips[None, :]
    stage = jnp.sum(jnp.where(hit, stage_of[None, :], 0), axis=1)
    place = jnp.sum(jnp.where(hit, place_of[None, :], 0), axis=1) * per + source % per
    stage = jnp.where(target < grid_rows * per, stage, stage_total)
    key = stage * 2 * slots + slot_ids
    position = jnp.sum((key[None, :] < key[:, None]).astype(jnp.int32), axis=1)
    moved = position[:, None] == slot_ids[None, :]
    slot_facts = jnp.stack(
        [jnp.sum(jnp.where(moved, v[:, None], 0), axis=0) for v in (slot_ids, place, target)]
    )
    edges = jnp.arange(stage_total + 1, dtype=jnp.int32)
    bounds = jnp.sum((stage[:, None] < edges[None, :]).astype(jnp.int32), axis=0)

    parts_type = jax.ShapeDtypeStruct((grid_rows, per * TILE + 16, half), jnp.int16)
    total_type = jax.ShapeDtypeStruct((grid_rows * per + 1, TILE, half), jnp.float32)

    def multiply(i, pieces, total, sums):
        coded, first, last = sums is not None, i == 0, i + 1 == stage_total
        chip_list = chip_lists[i]
        each = chip_list.shape[0]
        counts = [each // len(pieces)] * len(pieces)
        args = [slot_facts, bounds, chip_list]
        specs = [smem()] * 3
        if coded:
            args.append(sums.reshape(chips, per, TILE))
        specs += [vmem()] * (len(args) - len(specs)) + [pl.BlockSpec(memory_space=pl.ANY)] * 2
        args += [in_hbm(tile_values), in_hbm(sib_tiles), *pieces]
        aliases = {}
        if not first:
            if not last:
                aliases = {len(args): 0}
            args.append(total)
        specs += [vmem()] * (len(args) - len(specs))
        outs = [parts_type if last else total_type]
        if coded and first:
            outs.append(jax.ShapeDtypeStruct((per * TILE, half), jnp.float32))
        scratch = [VMEM((each * per * TILE, half), jnp.bfloat16)]
        if coded:
            scratch.append(VMEM((TILE, TILE), jnp.float32))
        scratch.append(VMEM((2, UNROLL, TILE, TILE), tile_values.dtype))
        scratch.append(pltpu.SemaphoreType.DMA((2,)))
        results = pl.pallas_call(
            lambda *refs: stage_kernel(i, first, last, coded, counts, *refs),
            out_shape=tuple(outs),
            in_specs=specs,
            out_specs=tuple([vmem()] * len(outs)),
            scratch_shapes=scratch,
            input_output_aliases=aliases,
            compiler_params=params(),
            cost_estimate=pl.CostEstimate(
                flops=each * 9 * 2 * TILE * TILE * half,
                bytes_accessed=each * 9 * TILE * TILE * 2,
                transcendentals=0,
            ),
            name="products",
        )(*args)
        return results[0], results[1] if coded and first else None

    tie = lax.optimization_barrier

    def hop(sums, step):
        return sums + by_col(sums, lambda y, at, k: (y, at ^ step, k))

    def gather_and_multiply(block, sums):
        coded = sums is not None
        rows = block.shape[0]
        both = jnp.concatenate([block, across(block)])
        if coded:
            both, sums = tie((both, sums))
        arrived = [[both]]
        a, b = both, both
        total, inverse, done = None, None, 0
        hops = 1
        for step in range(1, depth // 2 + 1):
            if step < depth // 2:
                a, b = along(a, 1), along(b, -1)
            else:
                a, b = along(a[:rows], 1), along(b[rows:], -1)
            if coded and step <= 2:
                for _ in range(2):
                    sums = hop(sums, hops) if hops < depth else sums + across(sums)
                    hops *= 2
                a, b, sums = tie((a, b, sums))
            else:
                most = done + 2 if coded else step
                while done < min(most, step):
                    total, found = multiply(done, arrived[done], total, sums)
                    inverse = found if done == 0 else inverse
                    done += 1
                if step < depth // 2:
                    a, b, total = tie((a, b, total))
            arrived.append([a, b])
        while done < len(arrived):
            total, _ = multiply(done, arrived[done], total, sums)
            done += 1
        return total, inverse

    def update(parts, inverse, scaled):
        return pl.pallas_call(
            lambda *refs: current_kernel(scaled, *refs),
            out_shape=jax.ShapeDtypeStruct(
                (per * TILE, half), jnp.bfloat16 if scaled else jnp.float32
            ),
            in_specs=[vmem()] * 3,
            out_specs=vmem(),
            compiler_params=params(),
            name="current",
        )(parts, restart, inverse)

    parts, inverse = gather_and_multiply(block, sums)
    parts = lax.all_to_all(parts, "row", 0, 0, tiled=True)
    panel = update(parts, inverse, True)
    parts, _ = gather_and_multiply(panel, None)
    parts = lax.all_to_all(parts, "row", 0, 0, tiled=True)
    current = update(parts, inverse, False)
    mine = lax.dynamic_slice_in_dim(current, core * own_rows, own_rows, 0)
    theirs = sibling(lax.dynamic_slice_in_dim(current, (1 - core) * own_rows, own_rows, 0))
    return jnp.where(
        core == 0,
        jnp.concatenate([mine, theirs], axis=1),
        jnp.concatenate([theirs, mine], axis=1),
    )


def solution(mesh):
    placed = (
        P(("row", "col"), None),
        P(("row", "col"), None, None),
        P(("row", "col")),
        P(("row", "col")),
        P(("row", "col")),
        P(),
    )
    return jax.shard_map(
        per_device, mesh=mesh, in_specs=placed, out_specs=P(("row", "col"), None), check_vma=False
    )
```

```python
import jax
import jax.numpy as jnp
from jax import lax
from jax.experimental import pallas as pl
from jax.experimental.pallas import tpu as pltpu
from jax.sharding import PartitionSpec as P

BT = 2
TILE = 128
LANES = 128
damping = 0.85
teleport = 0.15
LOW, HIGH = 0.2, 2.0
STEPS = 65535.0
HALF = 32768.0
FAR = 1 << 30
VMEM = pltpu.VMEM
SMEM = pltpu.SMEM


def vmem(*_):
    return pl.BlockSpec(memory_space=VMEM)


def smem(*_):
    return pl.BlockSpec(memory_space=SMEM)


def anywhere(*_):
    return pl.BlockSpec(memory_space=pl.ANY)


def in_hbm(value):
    return pltpu.with_memory_space_constraint(value, pltpu.HBM)


def params():
    return pltpu.CompilerParams(vmem_limit_bytes=24 * 1024 * 1024)


def column_kernel(source_ref, count_ref, given_ref, sums_ref, tiles_ref, arrived):
    slots = given_ref.shape[0]
    chunk = slots // arrived.shape[0]
    copies = []
    for c in range(arrived.shape[0]):
        span = pl.ds(c * chunk, chunk)
        copies.append(
            pltpu.make_async_copy(given_ref.at[span], tiles_ref.at[span], arrived.at[c])
        )
        copies[c].start()
    sums_ref[...] = jnp.zeros_like(sums_ref)

    def slot(k, carry):
        column = jnp.sum(tiles_ref[k].astype(jnp.float32), axis=0, keepdims=True)
        sums_ref[pl.ds(source_ref[k], 1), :] += column
        return carry

    for c in range(arrived.shape[0]):
        copies[c].wait()
        lax.fori_loop(c * chunk, jnp.minimum((c + 1) * chunk, count_ref[0]), slot, 0)


def total_kernel(rows, *refs):
    *piece_refs, out_ref = refs
    each = out_ref.shape[0]
    total = jnp.zeros(out_ref.shape, jnp.float32)
    for piece_ref in piece_refs:
        code = piece_ref[rows : rows + 3 * each, :].astype(jnp.float32)
        mantissa = code[each : 2 * each] * 4096.0 + code[2 * each :]
        total += mantissa * jnp.exp2(code[:each] - 24.0)
    out_ref[...] = total


def seed_kernel(first_ref, ids_ref, counts_ref):
    total, lanes = ids_ref.shape
    pages = counts_ref.shape[0]
    first = first_ref[0]
    chunk = 64
    counts_ref[...] = jnp.zeros_like(counts_ref)

    def above(low):
        def step(i, best):
            page = ids_ref[pl.ds(pl.multiple_of(i * chunk, chunk), chunk), :] - first
            found = jnp.where(page > low, page, FAR).reshape(chunk // 8, 8, lanes)
            return jnp.minimum(best, jnp.min(found, axis=0))

        best = lax.fori_loop(0, total // chunk, step, jnp.full((8, lanes), FAR, jnp.int32))
        return jnp.min(best, axis=0, keepdims=True)

    def more(carry):
        return carry[1] < pages

    def walk(carry):
        page_now, _ = carry

        def step(i, inner):
            best, seen = inner
            page = ids_ref[pl.ds(pl.multiple_of(i * chunk, chunk), chunk), :] - first
            found = jnp.where(page > page_now, page, FAR).reshape(chunk // 8, 8, lanes)
            same = jnp.where(page == page_now, 1.0, 0.0).reshape(chunk // 8, 8, lanes)
            return jnp.minimum(best, jnp.min(found, axis=0)), seen + jnp.sum(same, axis=0)

        best, seen = lax.fori_loop(
            0,
            total // chunk,
            step,
            (jnp.full((8, lanes), FAR, jnp.int32), jnp.zeros((8, lanes), jnp.float32)),
        )
        seen = jnp.sum(seen, axis=0, keepdims=True)

        def place(i, inner):
            rows = pl.ds(pl.multiple_of(i * chunk, chunk), chunk)
            here = lax.broadcasted_iota(jnp.int32, (chunk, lanes), 0) + i * chunk
            counts_ref[rows, :] += jnp.where(here == page_now, seen, 0.0)
            return inner

        lax.fori_loop(0, pages // chunk, place, 0)
        later = jnp.min(best, axis=0, keepdims=True)
        return later, jnp.min(later)

    start = above(jnp.full((1, lanes), -1, jnp.int32))
    lax.while_loop(more, walk, (start, jnp.min(start)))


def fetch(own_ref, sib_ref, tiles, arrived):
    slots = own_ref.shape[0]
    copies = [
        pltpu.make_async_copy(own_ref, tiles.at[pl.ds(0, slots)], arrived.at[0]),
        pltpu.make_async_copy(sib_ref, tiles.at[pl.ds(slots, slots)], arrived.at[1]),
    ]
    for copy in copies:
        copy.start()
    return copies


def products(facts_refs, copies, tiles, panel, total, out_ref):
    unroll = 4
    slots = tiles.shape[0] // 2
    dummy = total.shape[0] - 1
    for which, facts_ref in enumerate(facts_refs):
        copies[which].wait()
        pairs = facts_ref[3, 0]

        def group(g, carry, base=which * slots, facts_ref=facts_ref, pairs=pairs):
            for u in range(unroll):
                pair = g * unroll + u
                at = 2 * pair
                target = jnp.where(pair < pairs, facts_ref[2, at], dummy)
                left = jnp.concatenate(
                    [tiles[base + facts_ref[0, at]], tiles[base + facts_ref[0, at + 1]]], axis=1
                )
                right = jnp.concatenate(
                    [panel[facts_ref[1, at]], panel[facts_ref[1, at + 1]]], axis=0
                )
                total[target] += jnp.dot(left, right, preferred_element_type=jnp.float32)
            return carry

        lax.fori_loop(0, (pairs + unroll - 1) // unroll, group, 0)
    receivers = out_ref.shape[0]
    per = (out_ref.shape[1] - 16) // TILE

    def send(r, carry):
        exponents = []
        for t in range(per):
            block = total[r * per + t]
            top = jnp.maximum(jnp.max(block, axis=0, keepdims=True), 1e-30)
            exponent = jnp.floor(jnp.log2(top)) + 1.0
            exponents.append(exponent)
            code = block * jnp.exp2(16.0 - exponent) + 0.5
            code = jnp.clip(code.astype(jnp.int32), 0, 65535) - 32768
            out_ref[r, t * TILE : (t + 1) * TILE, :] = code.astype(jnp.int16)
        rows = exponents + [jnp.zeros((16 - per, LANES), jnp.float32)]
        tail = jnp.concatenate(rows, axis=0).astype(jnp.int32).astype(jnp.int16)
        out_ref[r, per * TILE : per * TILE + 16, :] = tail
        return carry

    lax.fori_loop(0, receivers, send, 0)


def first_kernel(pieces, rows, own_facts, sib_facts, chip_ref, sums_ref, own_ref, sib_ref, *refs):
    piece_refs = refs[:pieces]
    out_ref, inverse_ref, panel, total, tiles, arrived, ordered = refs[pieces:]
    copies = fetch(own_ref, sib_ref, tiles, arrived)
    total[...] = jnp.zeros_like(total)
    per = rows // TILE
    ordered[...] = jnp.zeros_like(ordered)
    for p in range(pieces):
        ordered[p * per : (p + 1) * per, :] = sums_ref[chip_ref[p]]
    inverse = (1.0 / jnp.maximum(ordered[...], 1.0)).T
    for p in range(pieces):
        for t in range(per):
            column = inverse[:, p * per + t : p * per + t + 1]
            code = piece_refs[p][t * TILE : (t + 1) * TILE, :].astype(jnp.float32)
            score = (code + HALF) * ((HIGH - LOW) / STEPS) + LOW
            panel[chip_ref[p] * per + t] = (score * column).astype(jnp.bfloat16)
            if p == 0:
                inverse_ref[t * TILE : (t + 1) * TILE, :] = jnp.broadcast_to(column, (TILE, LANES))
    panel[pieces * per] = jnp.zeros((TILE, LANES), jnp.bfloat16)
    products((own_facts, sib_facts), copies, tiles, panel, total, out_ref)


def later_kernel(pieces, rows, own_facts, sib_facts, chip_ref, own_ref, sib_ref, *refs):
    piece_refs = refs[:pieces]
    out_ref, panel, total, tiles, arrived = refs[pieces:]
    copies = fetch(own_ref, sib_ref, tiles, arrived)
    total[...] = jnp.zeros_like(total)
    per = rows // TILE
    for p in range(pieces):
        for t in range(per):
            panel[chip_ref[p] * per + t] = piece_refs[p][t * TILE : (t + 1) * TILE, :]
    panel[pieces * per] = jnp.zeros((TILE, LANES), jnp.bfloat16)
    products((own_facts, sib_facts), copies, tiles, panel, total, out_ref)


def current_kernel(scaled, parts_ref, restart_ref, inverse_ref, out_ref):
    senders = parts_ref.shape[0]
    per = (parts_ref.shape[1] - 16) // TILE
    for t in range(per):
        rows = slice(t * TILE, (t + 1) * TILE)
        summed = jnp.zeros((TILE, LANES), jnp.float32)
        for r in range(senders):
            tail = parts_ref[r, per * TILE : per * TILE + 16, :].astype(jnp.float32)
            scale = jnp.exp2(tail[t : t + 1, :] - 16.0)
            summed += (parts_ref[r, rows, :].astype(jnp.float32) + HALF) * scale
        current = damping * summed + teleport * restart_ref[rows, :]
        if scaled:
            current = current * inverse_ref[rows, :]
        out_ref[rows, :] = current.astype(out_ref.dtype)


def per_device(scores, tile_values, tile_rows, tile_cols, tile_count, seed_ids):
    grid_rows = lax.axis_size("row")
    grid_cols = lax.axis_size("col")
    row_index = lax.axis_index("row")
    col_index = lax.axis_index("col")
    depth = grid_cols // 4
    high, z, core = col_index // (2 * depth), col_index // 2 % depth, col_index % 2
    own_rows = scores.shape[0]
    columns = scores.shape[1]
    slots = tile_values.shape[0]
    seed_total = seed_ids.shape[1]
    band_tiles = grid_cols * BT
    chips = grid_cols // 2
    per = 2 * BT

    def by_col(value, move):
        pairs = []
        for c in range(grid_cols):
            y, at, k = move(c // (2 * depth), c // 2 % depth, c % 2)
            pairs.append((c, (y * depth + at) * 2 + k))
        return lax.ppermute(value, "col", pairs)

    def sibling(value):
        return by_col(value, lambda y, at, k: (y, at, 1 - k))

    def along(value, step):
        return by_col(value, lambda y, at, k: (y, (at + step) % depth, k))

    def across(value):
        return by_col(value, lambda y, at, k: (1 - y, at, k))

    def gather(block):
        other = across(block)
        pieces = [block, other]
        names = [(0, 0), (1, 0)]
        a, b, c, d = block, block, other, other
        for step in range(1, depth // 2):
            a, b = along(a, 1), along(b, -1)
            c, d = along(c, 1), along(d, -1)
            pieces += [a, b, c, d]
            names += [(0, -step), (0, step), (1, -step), (1, step)]
        pieces += [along(a, 1), along(d, -1)]
        names += [(0, depth // 2), (1, depth // 2)]
        return pieces, names

    half = columns // 2
    code = ((scores - LOW) * (STEPS / (HIGH - LOW)) + 0.5).astype(jnp.int32)
    code = (jnp.clip(code, 0, 65535) - 32768).astype(jnp.int16)
    mine = lax.dynamic_slice_in_dim(code, core * half, half, 1)
    theirs = sibling(lax.dynamic_slice_in_dim(code, (1 - core) * half, half, 1))
    block = jnp.where(
        core == 0, jnp.concatenate([mine, theirs]), jnp.concatenate([theirs, mine])
    )
    sib_tiles = sibling(tile_values)
    sources = tile_cols - row_index * band_tiles
    sums = pl.pallas_call(
        column_kernel,
        out_shape=jax.ShapeDtypeStruct((band_tiles, TILE), jnp.float32),
        in_specs=[smem(), smem(), anywhere()],
        out_specs=vmem(),
        scratch_shapes=[VMEM(tile_values.shape, tile_values.dtype), pltpu.SemaphoreType.DMA((4,))],
        compiler_params=params(),
        name="column_sums",
    )(sources, tile_count, in_hbm(tile_values))

    part = band_tiles // 2
    given = sibling(lax.dynamic_slice_in_dim(sums, (1 - core) * part, part, 0))
    given = given + lax.dynamic_slice_in_dim(sums, core * part, part, 0)
    exponent = jnp.floor(jnp.log2(jnp.maximum(given, 1e-30))) + 1.0
    mantissa = (given * jnp.exp2(24.0 - exponent) + 0.5).astype(jnp.int32)
    tail = jnp.concatenate([exponent.astype(jnp.int32), mantissa >> 12, mantissa & 4095])
    block = jnp.concatenate([block, tail.astype(jnp.int16)])

    targets = tile_rows // band_tiles * per + core * BT + tile_rows % BT
    live = jnp.arange(slots) < tile_count[0]
    target_total = grid_rows * per
    target_ids = jnp.arange(target_total, dtype=jnp.int32)
    at_target = (targets[:, None] == target_ids[None, :]) & live[:, None]
    filled = (jnp.sum(at_target.astype(jnp.int32), axis=0) + 1) // 2 * 2
    start = jnp.sum(jnp.where(target_ids[:, None] < target_ids[None, :], filled[:, None], 0), axis=0)
    slot_ids = jnp.arange(slots, dtype=jnp.int32)
    alike = (targets[:, None] == targets[None, :]) & (slot_ids[None, :] < slot_ids[:, None])
    place = jnp.sum(alike.astype(jnp.int32), axis=1)
    place = place + jnp.sum(jnp.where(at_target, start[None, :], 0), axis=1)
    long = slots + target_total
    moved = (place[:, None] == jnp.arange(long)[None, :]) & live[:, None]

    def spread(value):
        return jnp.sum(jnp.where(moved, value[:, None], 0), axis=0)

    facts = jnp.stack(
        [
            spread(slot_ids),
            spread(sources - band_tiles) + band_tiles,
            spread(targets),
            jnp.broadcast_to(jnp.sum(filled) // 2, (long,)),
        ]
    )
    sib_facts = sibling(facts)

    first_page = (row_index * grid_cols + col_index - core) * own_rows
    ids = lax.dynamic_slice_in_dim(seed_ids, core * half, half, 0).T
    restart = pl.pallas_call(
        seed_kernel,
        out_shape=jax.ShapeDtypeStruct((2 * own_rows, half), jnp.float32),
        in_specs=[smem(), vmem()],
        out_specs=vmem(),
        compiler_params=params(),
        name="seed_counts",
    )(first_page.reshape(1), ids)

    def multiply(pieces, names, sums):
        order = jnp.stack([(high ^ y) * depth + (z + d) % depth for y, d in names])
        n = len(pieces)
        rows = per * TILE
        parts = jax.ShapeDtypeStruct((grid_rows, rows + 16, half), jnp.int16)
        scratch = [
            VMEM((band_tiles + 1, TILE, half), jnp.bfloat16),
            VMEM((target_total + 1, TILE, half), jnp.float32),
            VMEM((2 * slots, TILE, TILE), tile_values.dtype),
            pltpu.SemaphoreType.DMA((2,)),
        ]
        tiles = (in_hbm(tile_values), in_hbm(sib_tiles))
        if sums is not None:
            return pl.pallas_call(
                lambda *refs: first_kernel(n, rows, *refs),
                out_shape=(parts, jax.ShapeDtypeStruct((rows, half), jnp.float32)),
                in_specs=[smem()] * 3 + [vmem()] + [anywhere()] * 2 + [vmem()] * n,
                out_specs=(vmem(), vmem()),
                scratch_shapes=scratch + [VMEM((TILE, TILE), jnp.float32)],
                compiler_params=params(),
                name="first_products",
            )(facts, sib_facts, order, sums.reshape(chips, per, TILE), *tiles, *pieces)
        return pl.pallas_call(
            lambda *refs: later_kernel(n, rows, *refs),
            out_shape=parts,
            in_specs=[smem()] * 3 + [anywhere()] * 2 + [vmem()] * n,
            out_specs=vmem(),
            scratch_shapes=scratch,
            compiler_params=params(),
            name="later_products",
        )(facts, sib_facts, order, *tiles, *pieces)

    def update(parts, inverse, scaled):
        return pl.pallas_call(
            lambda *refs: current_kernel(scaled, *refs),
            out_shape=jax.ShapeDtypeStruct(
                (per * TILE, half), jnp.bfloat16 if scaled else jnp.float32
            ),
            in_specs=[vmem()] * 3,
            out_specs=vmem(),
            compiler_params=params(),
            name="current",
        )(parts, restart, inverse)

    pieces, names = gather(block)
    found = pl.pallas_call(
        lambda *refs: total_kernel(per * TILE, *refs),
        out_shape=jax.ShapeDtypeStruct((part, TILE), jnp.float32),
        in_specs=[vmem()] * len(pieces),
        out_specs=vmem(),
        compiler_params=params(),
        name="column_totals",
    )(*pieces)
    other = sibling(found)
    sums = jnp.where(
        core == 0, jnp.concatenate([found, other]), jnp.concatenate([other, found])
    )
    parts, inverse = multiply(pieces, names, sums)
    parts = lax.all_to_all(parts, "row", 0, 0, tiled=True)
    panel = update(parts, inverse, True)
    pieces, names = gather(panel)
    parts = multiply(pieces, names, None)
    parts = lax.all_to_all(parts, "row", 0, 0, tiled=True)
    current = update(parts, inverse, False)
    mine = lax.dynamic_slice_in_dim(current, core * own_rows, own_rows, 0)
    theirs = sibling(lax.dynamic_slice_in_dim(current, (1 - core) * own_rows, own_rows, 0))
    return jnp.where(
        core == 0,
        jnp.concatenate([mine, theirs], axis=1),
        jnp.concatenate([theirs, mine], axis=1),
    )


def solution(mesh):
    placed = (
        P(("row", "col"), None),
        P(("row", "col"), None, None),
        P(("row", "col")),
        P(("row", "col")),
        P(("row", "col")),
        P(),
    )
    return jax.shard_map(
        per_device, mesh=mesh, in_specs=placed, out_specs=P(("row", "col"), None), check_vma=False
    )
```

```python
import jax
import jax.numpy as jnp
from jax import lax
from jax.experimental import pallas as pl
from jax.experimental.pallas import tpu as pltpu
from jax.sharding import PartitionSpec as P

BT = 2
TILE = 128
LANES = 128
damping = 0.85
teleport = 0.15
LOW, HIGH = 0.2, 2.0
STEPS = 65535.0
HALF = 32768.0
FAR = 1 << 30
VMEM = pltpu.VMEM
SMEM = pltpu.SMEM


def vmem(*_):
    return pl.BlockSpec(memory_space=VMEM)


def smem(*_):
    return pl.BlockSpec(memory_space=SMEM)


def anywhere(*_):
    return pl.BlockSpec(memory_space=pl.ANY)


def in_hbm(value):
    return pltpu.with_memory_space_constraint(value, pltpu.HBM)


def params(mebibytes):
    return pltpu.CompilerParams(vmem_limit_bytes=mebibytes * 1024 * 1024)


def column_kernel(source_ref, count_ref, given_ref, sums_ref, tiles_ref, arrived):
    slots = given_ref.shape[0]
    chunk = slots // arrived.shape[0]
    copies = []
    for c in range(arrived.shape[0]):
        span = pl.ds(c * chunk, chunk)
        copies.append(
            pltpu.make_async_copy(given_ref.at[span], tiles_ref.at[span], arrived.at[c])
        )
        copies[c].start()
    sums_ref[...] = jnp.zeros_like(sums_ref)

    def group(g, carry):
        columns = [
            jnp.sum(tiles_ref[8 * g + u].astype(jnp.float32), axis=0, keepdims=True) for u in range(8)
        ]
        for u in range(8):
            k = 8 * g + u
            live = jnp.where(k < count_ref[0], 1.0, 0.0)
            sums_ref[pl.ds(source_ref[k], 1), :] += columns[u] * live
        return carry

    for c in range(arrived.shape[0]):
        copies[c].wait()
        last = jnp.minimum((c + 1) * chunk, count_ref[0])
        lax.fori_loop(c * chunk // 8, (last + 7) // 8, group, 0)


def column_totals(rows, piece_refs, sums_ref):
    groups, per, lanes = sums_ref.shape
    each = groups * per
    total = jnp.zeros((each, lanes), jnp.float32)
    for piece_ref in piece_refs:
        code = piece_ref[rows : rows + 2 * each, :].astype(jnp.int32) + 32768
        upper, lower = code[:each], code[each:]
        exponent = (upper >> 8) - 127
        mantissa = ((upper & 255) * 65536 + lower).astype(jnp.float32)
        total += mantissa * jnp.exp2((exponent - 24).astype(jnp.float32))
    for g in range(groups):
        sums_ref[g] = total[g * per : (g + 1) * per]


def seed_kernel(first_ref, ids_ref, counts_ref):
    total, lanes = ids_ref.shape
    pages = counts_ref.shape[0]
    first = first_ref[0]
    chunk = 64
    counts_ref[...] = jnp.zeros_like(counts_ref)

    def above(low):
        def step(i, best):
            page = ids_ref[pl.ds(pl.multiple_of(i * chunk, chunk), chunk), :] - first
            found = jnp.where(page > low, page, FAR).reshape(chunk // 8, 8, lanes)
            return jnp.minimum(best, jnp.min(found, axis=0))

        best = lax.fori_loop(0, total // chunk, step, jnp.full((8, lanes), FAR, jnp.int32))
        return jnp.min(best, axis=0, keepdims=True)

    def more(carry):
        return carry[1] < pages

    def walk(carry):
        page_now, _ = carry

        def step(i, inner):
            best, seen = inner
            page = ids_ref[pl.ds(pl.multiple_of(i * chunk, chunk), chunk), :] - first
            found = jnp.where(page > page_now, page, FAR).reshape(chunk // 8, 8, lanes)
            same = jnp.where(page == page_now, 1.0, 0.0).reshape(chunk // 8, 8, lanes)
            return jnp.minimum(best, jnp.min(found, axis=0)), seen + jnp.sum(same, axis=0)

        best, seen = lax.fori_loop(
            0,
            total // chunk,
            step,
            (jnp.full((8, lanes), FAR, jnp.int32), jnp.zeros((8, lanes), jnp.float32)),
        )
        seen = jnp.sum(seen, axis=0, keepdims=True)

        def place(i, inner):
            rows = pl.ds(pl.multiple_of(i * chunk, chunk), chunk)
            here = lax.broadcasted_iota(jnp.int32, (chunk, lanes), 0) + i * chunk
            counts_ref[rows, :] += jnp.where(here == page_now, seen, 0.0)
            return inner

        lax.fori_loop(0, pages // chunk, place, 0)
        later = jnp.min(best, axis=0, keepdims=True)
        return later, jnp.min(later)

    start = above(jnp.full((1, lanes), -1, jnp.int32))
    lax.while_loop(more, walk, (start, jnp.min(start)))


def fetch(own_ref, sib_ref, tiles, arrived):
    slots = own_ref.shape[0]
    copies = [
        pltpu.make_async_copy(own_ref, tiles.at[pl.ds(0, slots)], arrived.at[0]),
        pltpu.make_async_copy(sib_ref, tiles.at[pl.ds(slots, slots)], arrived.at[1]),
    ]
    for copy in copies:
        copy.start()
    return copies


def products(facts_refs, copies, tiles, panel, total, out_ref):
    unroll = 16
    slots = tiles.shape[0] // 2
    dummy = total.shape[0] - 1
    for which, facts_ref in enumerate(facts_refs):
        copies[which].wait()
        pairs = facts_ref[3, 0]

        def group(g, carry, base=which * slots, facts_ref=facts_ref, pairs=pairs):
            for u in range(unroll):
                pair = g * unroll + u
                at = 2 * pair
                target = jnp.where(pair < pairs, facts_ref[2, at], dummy)
                left = jnp.concatenate(
                    [tiles[base + facts_ref[0, at]], tiles[base + facts_ref[0, at + 1]]], axis=1
                )
                right = jnp.concatenate(
                    [panel[facts_ref[1, at]], panel[facts_ref[1, at + 1]]], axis=0
                )
                total[target] += jnp.dot(left, right, preferred_element_type=jnp.float32)
            return carry

        lax.fori_loop(0, (pairs + unroll - 1) // unroll, group, 0)
    receivers = out_ref.shape[0]
    per = (out_ref.shape[1] - 16) // TILE

    def send(r, carry):
        exponents = []
        for t in range(per):
            block = total[r * per + t]
            top = jnp.maximum(jnp.max(block, axis=0, keepdims=True), 1e-30)
            exponent = jnp.floor(jnp.log2(top)) + 1.0
            exponents.append(exponent)
            code = block * jnp.exp2(16.0 - exponent) + 0.5
            code = jnp.clip(code.astype(jnp.int32), 0, 65535) - 32768
            out_ref[r, t * TILE : (t + 1) * TILE, :] = code.astype(jnp.int16)
        rows = exponents + [jnp.zeros((16 - per, LANES), jnp.float32)]
        tail = jnp.concatenate(rows, axis=0).astype(jnp.int32).astype(jnp.int16)
        out_ref[r, per * TILE : per * TILE + 16, :] = tail
        return carry

    lax.fori_loop(0, receivers, send, 0)


def first_kernel(pieces, rows, own_facts, sib_facts, chip_ref, own_ref, sib_ref, *refs):
    piece_refs = refs[:pieces]
    out_ref, inverse_ref, panel, total, tiles, arrived, sums_ref, ordered = refs[pieces:]
    copies = fetch(own_ref, sib_ref, tiles, arrived)
    column_totals(rows, piece_refs, sums_ref)
    total[...] = jnp.zeros_like(total)
    per = rows // TILE
    ordered[...] = jnp.zeros_like(ordered)
    for p in range(pieces):
        ordered[p * per : (p + 1) * per, :] = sums_ref[chip_ref[p]]
    inverse = (1.0 / jnp.maximum(ordered[...], 1.0)).T
    for p in range(pieces):
        for t in range(per):
            column = inverse[:, p * per + t : p * per + t + 1]
            code = piece_refs[p][t * TILE : (t + 1) * TILE, :].astype(jnp.float32)
            score = (code + HALF) * ((HIGH - LOW) / STEPS) + LOW
            panel[chip_ref[p] * per + t] = (score * column).astype(jnp.bfloat16)
            if p == 0:
                inverse_ref[t * TILE : (t + 1) * TILE, :] = jnp.broadcast_to(column, (TILE, LANES))
    panel[pieces * per] = jnp.zeros((TILE, LANES), jnp.bfloat16)
    products((own_facts, sib_facts), copies, tiles, panel, total, out_ref)


def later_kernel(pieces, rows, own_facts, sib_facts, chip_ref, own_ref, sib_ref, *refs):
    piece_refs = refs[:pieces]
    out_ref, panel, total, tiles, arrived = refs[pieces:]
    copies = fetch(own_ref, sib_ref, tiles, arrived)
    total[...] = jnp.zeros_like(total)
    per = rows // TILE
    for p in range(pieces):
        for t in range(per):
            panel[chip_ref[p] * per + t] = piece_refs[p][t * TILE : (t + 1) * TILE, :]
    panel[pieces * per] = jnp.zeros((TILE, LANES), jnp.bfloat16)
    products((own_facts, sib_facts), copies, tiles, panel, total, out_ref)


def current_kernel(scaled, parts_ref, restart_ref, inverse_ref, out_ref):
    senders = parts_ref.shape[0]
    per = (parts_ref.shape[1] - 16) // TILE
    for t in range(per):
        rows = slice(t * TILE, (t + 1) * TILE)
        summed = jnp.zeros((TILE, LANES), jnp.float32)
        for r in range(senders):
            tail = parts_ref[r, per * TILE : per * TILE + 16, :].astype(jnp.float32)
            scale = jnp.exp2(tail[t : t + 1, :] - 16.0)
            summed += (parts_ref[r, rows, :].astype(jnp.float32) + HALF) * scale
        current = damping * summed + teleport * restart_ref[rows, :]
        if scaled:
            current = current * inverse_ref[rows, :]
        out_ref[rows, :] = current.astype(out_ref.dtype)


def per_device(scores, tile_values, tile_rows, tile_cols, tile_count, seed_ids):
    grid_rows = lax.axis_size("row")
    grid_cols = lax.axis_size("col")
    row_index = lax.axis_index("row")
    col_index = lax.axis_index("col")
    depth = grid_cols // 4
    high, z, core = col_index // (2 * depth), col_index // 2 % depth, col_index % 2
    own_rows = scores.shape[0]
    columns = scores.shape[1]
    slots = tile_values.shape[0]
    seed_total = seed_ids.shape[1]
    band_tiles = grid_cols * BT
    chips = grid_cols // 2
    per = 2 * BT

    def by_col(value, move):
        pairs = []
        for c in range(grid_cols):
            y, at, k = move(c // (2 * depth), c // 2 % depth, c % 2)
            pairs.append((c, (y * depth + at) * 2 + k))
        return lax.ppermute(value, "col", pairs)

    def sibling(value):
        return by_col(value, lambda y, at, k: (y, at, 1 - k))

    def along(value, step):
        return by_col(value, lambda y, at, k: (y, (at + step) % depth, k))

    def across(value):
        return by_col(value, lambda y, at, k: (1 - y, at, k))

    def gather(block, beside=None):
        other = across(block)
        pieces = [block, other]
        names = [(0, 0), (1, 0)]
        a, b, c, d = block, block, other, other
        for step in range(1, depth // 2):
            a, b = along(a, 1), along(b, -1)
            c, d = along(c, 1), along(d, -1)
            pieces += [a, b, c, d]
            names += [(0, -step), (0, step), (1, -step), (1, step)]
            if step == 1 and beside is not None:
                a, beside = lax.optimization_barrier((a, beside))
        pieces += [along(a, 1), along(d, -1)]
        names += [(0, depth // 2), (1, depth // 2)]
        return pieces, names, beside

    half = columns // 2
    code = ((scores - LOW) * (STEPS / (HIGH - LOW)) + 0.5).astype(jnp.int32)
    code = (jnp.clip(code, 0, 65535) - 32768).astype(jnp.int16)
    mine = lax.dynamic_slice_in_dim(code, core * half, half, 1)
    theirs = sibling(lax.dynamic_slice_in_dim(code, (1 - core) * half, half, 1))
    block = jnp.where(
        core == 0, jnp.concatenate([mine, theirs]), jnp.concatenate([theirs, mine])
    )
    sib_tiles = sibling(tile_values)
    sources = tile_cols - row_index * band_tiles
    sums = pl.pallas_call(
        column_kernel,
        out_shape=jax.ShapeDtypeStruct((band_tiles, TILE), jnp.float32),
        in_specs=[smem(), smem(), anywhere()],
        out_specs=vmem(),
        scratch_shapes=[VMEM(tile_values.shape, tile_values.dtype), pltpu.SemaphoreType.DMA((4,))],
        compiler_params=params(8),
        name="column_sums",
    )(sources, tile_count, in_hbm(tile_values))

    given = sums + sibling(sums)
    exponent = jnp.floor(jnp.log2(jnp.maximum(given, 1e-30))) + 1.0
    mantissa = jnp.minimum((given * jnp.exp2(24.0 - exponent) + 0.5).astype(jnp.int32), (1 << 24) - 1)
    upper = (exponent.astype(jnp.int32) + 127) * 256 + (mantissa >> 16)
    tail = jnp.concatenate([upper, mantissa & 65535]) - 32768
    block = jnp.concatenate([block, tail.astype(jnp.int16)])

    targets = tile_rows // band_tiles * per + core * BT + tile_rows % BT
    live = jnp.arange(slots) < tile_count[0]
    target_total = grid_rows * per
    target_ids = jnp.arange(target_total, dtype=jnp.int32)
    at_target = (targets[:, None] == target_ids[None, :]) & live[:, None]
    filled = (jnp.sum(at_target.astype(jnp.int32), axis=0) + 1) // 2 * 2
    start = jnp.sum(jnp.where(target_ids[:, None] < target_ids[None, :], filled[:, None], 0), axis=0)
    slot_ids = jnp.arange(slots, dtype=jnp.int32)
    alike = (targets[:, None] == targets[None, :]) & (slot_ids[None, :] < slot_ids[:, None])
    place = jnp.sum(alike.astype(jnp.int32), axis=1)
    place = place + jnp.sum(jnp.where(at_target, start[None, :], 0), axis=1)
    long = slots + target_total
    moved = (place[:, None] == jnp.arange(long)[None, :]) & live[:, None]

    def spread(value):
        return jnp.sum(jnp.where(moved, value[:, None], 0), axis=0)

    facts = jnp.stack(
        [
            spread(slot_ids),
            spread(sources - band_tiles) + band_tiles,
            spread(targets),
            jnp.broadcast_to(jnp.sum(filled) // 2, (long,)),
        ]
    )
    sib_facts = sibling(facts)

    first_page = (row_index * grid_cols + col_index - core) * own_rows
    ids = lax.dynamic_slice_in_dim(seed_ids, core * half, half, 0).T
    restart = pl.pallas_call(
        seed_kernel,
        out_shape=jax.ShapeDtypeStruct((2 * own_rows, half), jnp.float32),
        in_specs=[smem(), vmem()],
        out_specs=vmem(),
        compiler_params=params(4),
        name="seed_counts",
    )(first_page.reshape(1), ids)

    def multiply(pieces, names, coded):
        order = jnp.stack([(high ^ y) * depth + (z + d) % depth for y, d in names])
        n = len(pieces)
        rows = per * TILE
        parts = jax.ShapeDtypeStruct((grid_rows, rows + 16, half), jnp.int16)
        scratch = [
            VMEM((band_tiles + 1, TILE, half), jnp.bfloat16),
            VMEM((target_total + 1, TILE, half), jnp.float32),
            VMEM((2 * slots, TILE, TILE), tile_values.dtype),
            pltpu.SemaphoreType.DMA((2,)),
        ]
        tiles = (in_hbm(tile_values), in_hbm(sib_tiles))
        if coded:
            return pl.pallas_call(
                lambda *refs: first_kernel(n, rows, *refs),
                out_shape=(parts, jax.ShapeDtypeStruct((rows, half), jnp.float32)),
                in_specs=[smem()] * 3 + [anywhere()] * 2 + [vmem()] * n,
                out_specs=(vmem(), vmem()),
                scratch_shapes=scratch
                + [VMEM((chips, per, TILE), jnp.float32), VMEM((TILE, TILE), jnp.float32)],
                compiler_params=params(20),
                name="first_products",
            )(facts, sib_facts, order, *tiles, *pieces)
        return pl.pallas_call(
            lambda *refs: later_kernel(n, rows, *refs),
            out_shape=parts,
            in_specs=[smem()] * 3 + [anywhere()] * 2 + [vmem()] * n,
            out_specs=vmem(),
            scratch_shapes=scratch,
            compiler_params=params(20),
            name="later_products",
        )(facts, sib_facts, order, *tiles, *pieces)

    def update(parts, inverse, scaled):
        return pl.pallas_call(
            lambda *refs: current_kernel(scaled, *refs),
            out_shape=jax.ShapeDtypeStruct(
                (per * TILE, half), jnp.bfloat16 if scaled else jnp.float32
            ),
            in_specs=[vmem()] * 3,
            out_specs=vmem(),
            compiler_params=params(6),
            name="current",
        )(parts, restart, inverse)

    pieces, names, (sib_facts, sib_tiles) = gather(block, (sib_facts, sib_tiles))
    parts, inverse = multiply(pieces, names, True)
    parts = lax.all_to_all(parts, "row", 0, 0, tiled=True)
    panel = update(parts, inverse, True)
    pieces, names, _ = gather(panel)
    parts = multiply(pieces, names, False)
    parts = lax.all_to_all(parts, "row", 0, 0, tiled=True)
    current = update(parts, inverse, False)
    mine = lax.dynamic_slice_in_dim(current, core * own_rows, own_rows, 0)
    theirs = sibling(lax.dynamic_slice_in_dim(current, (1 - core) * own_rows, own_rows, 0))
    return jnp.where(
        core == 0,
        jnp.concatenate([mine, theirs], axis=1),
        jnp.concatenate([theirs, mine], axis=1),
    )


def solution(mesh):
    placed = (
        P(("row", "col"), None),
        P(("row", "col"), None, None),
        P(("row", "col")),
        P(("row", "col")),
        P(("row", "col")),
        P(),
    )
    return jax.shard_map(
        per_device, mesh=mesh, in_specs=placed, out_specs=P(("row", "col"), None), check_vma=False
    )
```

```python
import jax
import jax.numpy as jnp
from jax import lax
from jax.experimental import pallas as pl
from jax.experimental.pallas import tpu as pltpu
from jax.sharding import PartitionSpec as P

BT = 2
TILE = 128
LANES = 128
damping = 0.85
teleport = 0.15
LOW, HIGH = 0.2, 2.0
STEPS = 65535.0
HALF = 32768.0
FAR = 1 << 30
VMEM = pltpu.VMEM
SMEM = pltpu.SMEM


def vmem(*_):
    return pl.BlockSpec(memory_space=VMEM)


def smem(*_):
    return pl.BlockSpec(memory_space=SMEM)


def anywhere(*_):
    return pl.BlockSpec(memory_space=pl.ANY)


def in_hbm(value):
    return pltpu.with_memory_space_constraint(value, pltpu.HBM)


def params(mebibytes):
    return pltpu.CompilerParams(vmem_limit_bytes=mebibytes * 1024 * 1024)


def column_kernel(source_ref, count_ref, given_ref, sums_ref, tiles_ref, arrived):
    slots = given_ref.shape[0]
    chunk = slots // arrived.shape[0]
    copies = []
    for c in range(arrived.shape[0]):
        span = pl.ds(c * chunk, chunk)
        copies.append(
            pltpu.make_async_copy(given_ref.at[span], tiles_ref.at[span], arrived.at[c])
        )
        copies[c].start()
    sums_ref[...] = jnp.zeros_like(sums_ref)

    def group(g, carry):
        columns = [
            jnp.sum(tiles_ref[8 * g + u].astype(jnp.float32), axis=0, keepdims=True) for u in range(8)
        ]
        for u in range(8):
            k = 8 * g + u
            live = jnp.where(k < count_ref[0], 1.0, 0.0)
            sums_ref[pl.ds(source_ref[k] % sums_ref.shape[0], 1), :] += columns[u] * live
        return carry

    for c in range(arrived.shape[0]):
        copies[c].wait()
        last = jnp.minimum((c + 1) * chunk, count_ref[0])
        lax.fori_loop(c * chunk // 8, (last + 7) // 8, group, 0)


def encode(value):
    exponent = jnp.floor(jnp.log2(jnp.maximum(value, 1e-30))) + 1.0
    mantissa = (value * jnp.exp2(24.0 - exponent) + 0.5).astype(jnp.int32)
    mantissa = jnp.minimum(mantissa, (1 << 24) - 1)
    upper = (exponent.astype(jnp.int32) + 127) * 256 + (mantissa >> 16)
    return (jnp.concatenate([upper, mantissa & 65535]) - 32768).astype(jnp.int16)


def decode(code):
    code = code.astype(jnp.int32) + 32768
    each = code.shape[0] // 2
    upper, lower = code[:each], code[each:]
    mantissa = ((upper & 255) * 65536 + lower).astype(jnp.float32)
    return mantissa * jnp.exp2(((upper >> 8) - (127 + 24)).astype(jnp.float32))


def column_totals(rows, piece_refs, sums_ref):
    groups, per, lanes = sums_ref.shape
    each = groups * per
    total = jnp.zeros((each, lanes), jnp.float32)
    for piece_ref in piece_refs:
        if piece_ref.shape[0] > rows:
            total += decode(piece_ref[rows : rows + 2 * each, :])
    for g in range(groups):
        sums_ref[g] = total[g * per : (g + 1) * per]


def seed_kernel(first_ref, ids_ref, counts_ref):
    total, lanes = ids_ref.shape
    pages = counts_ref.shape[0]
    first = first_ref[0]
    chunk = 64
    counts_ref[...] = jnp.zeros_like(counts_ref)

    def above(low):
        def step(i, best):
            page = ids_ref[pl.ds(pl.multiple_of(i * chunk, chunk), chunk), :] - first
            found = jnp.where(page > low, page, FAR).reshape(chunk // 8, 8, lanes)
            return jnp.minimum(best, jnp.min(found, axis=0))

        best = lax.fori_loop(0, total // chunk, step, jnp.full((8, lanes), FAR, jnp.int32))
        return jnp.min(best, axis=0, keepdims=True)

    def more(carry):
        return carry[1] < pages

    def walk(carry):
        page_now, _ = carry

        def step(i, inner):
            best, seen = inner
            page = ids_ref[pl.ds(pl.multiple_of(i * chunk, chunk), chunk), :] - first
            found = jnp.where(page > page_now, page, FAR).reshape(chunk // 8, 8, lanes)
            same = jnp.where(page == page_now, 1.0, 0.0).reshape(chunk // 8, 8, lanes)
            return jnp.minimum(best, jnp.min(found, axis=0)), seen + jnp.sum(same, axis=0)

        best, seen = lax.fori_loop(
            0,
            total // chunk,
            step,
            (jnp.full((8, lanes), FAR, jnp.int32), jnp.zeros((8, lanes), jnp.float32)),
        )
        seen = jnp.sum(seen, axis=0, keepdims=True)

        def place(i, inner):
            rows = pl.ds(pl.multiple_of(i * chunk, chunk), chunk)
            here = lax.broadcasted_iota(jnp.int32, (chunk, lanes), 0) + i * chunk
            counts_ref[rows, :] += jnp.where(here == page_now, seen, 0.0)
            return inner

        lax.fori_loop(0, pages // chunk, place, 0)
        later = jnp.min(best, axis=0, keepdims=True)
        return later, jnp.min(later)

    start = above(jnp.full((1, lanes), -1, jnp.int32))
    lax.while_loop(more, walk, (start, jnp.min(start)))


def fetch(own_ref, sib_ref, tiles, arrived):
    slots = own_ref.shape[0]
    copies = [
        pltpu.make_async_copy(own_ref, tiles.at[pl.ds(0, slots)], arrived.at[0]),
        pltpu.make_async_copy(sib_ref, tiles.at[pl.ds(slots, slots)], arrived.at[1]),
    ]
    for copy in copies:
        copy.start()
    return copies


def products(facts_refs, copies, tiles, panel, total, out_ref):
    unroll = 16
    slots = tiles.shape[0] // 2
    dummy = total.shape[0] - 1
    for which, facts_ref in enumerate(facts_refs):
        copies[which].wait()
        pairs = facts_ref[3, 0]

        def group(g, carry, base=which * slots, facts_ref=facts_ref, pairs=pairs):
            for u in range(unroll):
                pair = g * unroll + u
                at = 2 * pair
                target = jnp.where(pair < pairs, facts_ref[2, at], dummy)
                left = jnp.concatenate(
                    [tiles[base + facts_ref[0, at]], tiles[base + facts_ref[0, at + 1]]], axis=1
                )
                right = jnp.concatenate(
                    [panel[facts_ref[1, at]], panel[facts_ref[1, at + 1]]], axis=0
                )
                total[target] += jnp.dot(left, right, preferred_element_type=jnp.float32)
            return carry

        lax.fori_loop(0, (pairs + unroll - 1) // unroll, group, 0)
    receivers = out_ref.shape[0]
    per = (out_ref.shape[1] - 16) // TILE

    def send(r, carry):
        exponents = []
        for t in range(per):
            block = total[r * per + t]
            top = jnp.maximum(jnp.max(block, axis=0, keepdims=True), 1e-30)
            exponent = jnp.floor(jnp.log2(top)) + 1.0
            exponents.append(exponent)
            code = block * jnp.exp2(16.0 - exponent) + 0.5
            code = jnp.clip(code.astype(jnp.int32), 0, 65535) - 32768
            out_ref[r, t * TILE : (t + 1) * TILE, :] = code.astype(jnp.int16)
        rows = exponents + [jnp.zeros((16 - per, LANES), jnp.float32)]
        tail = jnp.concatenate(rows, axis=0).astype(jnp.int32).astype(jnp.int16)
        out_ref[r, per * TILE : per * TILE + 16, :] = tail
        return carry

    lax.fori_loop(0, receivers, send, 0)


def first_kernel(pieces, rows, own_facts, sib_facts, chip_ref, own_ref, sib_ref, *refs):
    piece_refs = refs[:pieces]
    out_ref, inverse_ref, panel, total, tiles, arrived, sums_ref, ordered = refs[pieces:]
    copies = fetch(own_ref, sib_ref, tiles, arrived)
    column_totals(rows, piece_refs, sums_ref)
    total[...] = jnp.zeros_like(total)
    per = rows // TILE
    ordered[...] = jnp.zeros_like(ordered)
    for p in range(pieces):
        ordered[p * per : (p + 1) * per, :] = sums_ref[chip_ref[p]]
    inverse = (1.0 / jnp.maximum(ordered[...], 1.0)).T
    for p in range(pieces):
        for t in range(per):
            column = inverse[:, p * per + t : p * per + t + 1]
            code = piece_refs[p][t * TILE : (t + 1) * TILE, :].astype(jnp.float32)
            score = (code + HALF) * ((HIGH - LOW) / STEPS) + LOW
            panel[chip_ref[p] * per + t] = (score * column).astype(jnp.bfloat16)
            if p == 0:
                inverse_ref[t * TILE : (t + 1) * TILE, :] = jnp.broadcast_to(column, (TILE, LANES))
    panel[pieces * per] = jnp.zeros((TILE, LANES), jnp.bfloat16)
    products((own_facts, sib_facts), copies, tiles, panel, total, out_ref)


def later_kernel(pieces, rows, own_facts, sib_facts, chip_ref, own_ref, sib_ref, *refs):
    piece_refs = refs[:pieces]
    out_ref, panel, total, tiles, arrived = refs[pieces:]
    copies = fetch(own_ref, sib_ref, tiles, arrived)
    total[...] = jnp.zeros_like(total)
    per = rows // TILE
    for p in range(pieces):
        for t in range(per):
            panel[chip_ref[p] * per + t] = piece_refs[p][t * TILE : (t + 1) * TILE, :]
    panel[pieces * per] = jnp.zeros((TILE, LANES), jnp.bfloat16)
    products((own_facts, sib_facts), copies, tiles, panel, total, out_ref)


def current_kernel(scaled, parts_ref, restart_ref, inverse_ref, out_ref):
    senders = parts_ref.shape[0]
    per = (parts_ref.shape[1] - 16) // TILE
    for t in range(per):
        rows = slice(t * TILE, (t + 1) * TILE)
        summed = jnp.zeros((TILE, LANES), jnp.float32)
        for r in range(senders):
            tail = parts_ref[r, per * TILE : per * TILE + 16, :].astype(jnp.float32)
            scale = jnp.exp2(tail[t : t + 1, :] - 16.0)
            summed += (parts_ref[r, rows, :].astype(jnp.float32) + HALF) * scale
        current = damping * summed + teleport * restart_ref[rows, :]
        if scaled:
            current = current * inverse_ref[rows, :]
        out_ref[rows, :] = current.astype(out_ref.dtype)


def per_device(scores, tile_values, tile_rows, tile_cols, tile_count, seed_ids):
    grid_rows = lax.axis_size("row")
    grid_cols = lax.axis_size("col")
    row_index = lax.axis_index("row")
    col_index = lax.axis_index("col")
    depth = grid_cols // 4
    high, z, core = col_index // (2 * depth), col_index // 2 % depth, col_index % 2
    own_rows = scores.shape[0]
    columns = scores.shape[1]
    slots = tile_values.shape[0]
    seed_total = seed_ids.shape[1]
    band_tiles = grid_cols * BT
    chips = grid_cols // 2
    per = 2 * BT

    def by_col(value, move):
        pairs = []
        for c in range(grid_cols):
            y, at, k = move(c // (2 * depth), c // 2 % depth, c % 2)
            pairs.append((c, (y * depth + at) * 2 + k))
        return lax.ppermute(value, "col", pairs)

    def sibling(value):
        return by_col(value, lambda y, at, k: (y, at, 1 - k))

    def along(value, step):
        return by_col(value, lambda y, at, k: (y, (at + step) % depth, k))

    def across(value):
        return by_col(value, lambda y, at, k: (1 - y, at, k))

    tie = lax.optimization_barrier

    def gather(block, sums=None, later=None):
        rows = block.shape[0]
        a, b = along(block, 1), along(block, -1)
        if sums is None:
            other = across(block)
        else:
            other = across(jnp.concatenate([block, encode(sums)]))
            sums = sums + decode(other[rows:])
            other = jnp.concatenate([other[:rows], encode(sums)])
        pieces, names, beside = [block, other], [(0, 0), (1, 0)], None
        c, d = other, other
        for step in range(1, depth // 2):
            if step > 1:
                a, b = along(a, 1), along(b, -1)
            c, d = along(c, 1), along(d, -1)
            if later is not None and step == 1:
                a, raw = tie((a, (tile_rows, tile_cols, tile_count)))
                beside = later(*raw)
            if later is not None and step == 2:
                a, beside = tie((a, beside))
            pieces += [a, b, c, d]
            names += [(0, -step), (0, step), (1, -step), (1, step)]
        pieces += [along(a, 1), along(d, -1)]
        names += [(0, depth // 2), (1, depth // 2)]
        return pieces, names, beside

    half = columns // 2
    code = ((scores - LOW) * (STEPS / (HIGH - LOW)) + 0.5).astype(jnp.int32)
    code = (jnp.clip(code, 0, 65535) - 32768).astype(jnp.int16)
    mine = lax.dynamic_slice_in_dim(code, core * half, half, 1)
    theirs = sibling(lax.dynamic_slice_in_dim(code, (1 - core) * half, half, 1))
    block = jnp.where(
        core == 0, jnp.concatenate([mine, theirs]), jnp.concatenate([theirs, mine])
    )
    sib_tiles = sibling(tile_values)
    sums = pl.pallas_call(
        column_kernel,
        out_shape=jax.ShapeDtypeStruct((band_tiles, TILE), jnp.float32),
        in_specs=[smem(), smem(), anywhere()],
        out_specs=vmem(),
        scratch_shapes=[VMEM(tile_values.shape, tile_values.dtype), pltpu.SemaphoreType.DMA((4,))],
        compiler_params=params(8),
        name="column_sums",
    )(tile_cols, tile_count, in_hbm(tile_values))

    sums = sums + sibling(sums)

    target_total = grid_rows * per

    def order_tiles(tile_rows, tile_cols, tile_count):
        sources = tile_cols - row_index * band_tiles
        targets = tile_rows // band_tiles * per + core * BT + tile_rows % BT
        slot_ids = jnp.arange(slots, dtype=jnp.int32)
        live = slot_ids < tile_count[0]
        target_ids = jnp.arange(target_total, dtype=jnp.int32)
        at_target = (targets[:, None] == target_ids[None, :]) & live[:, None]
        filled = (jnp.sum(at_target.astype(jnp.int32), axis=0) + 1) // 2 * 2
        before = target_ids[:, None] < target_ids[None, :]
        start = jnp.sum(jnp.where(before, filled[:, None], 0), axis=0)
        alike = (targets[:, None] == targets[None, :]) & (slot_ids[None, :] < slot_ids[:, None])
        place = jnp.sum(alike.astype(jnp.int32), axis=1)
        place = place + jnp.sum(jnp.where(at_target, start[None, :], 0), axis=1)
        long = slots + target_total
        moved = (place[:, None] == jnp.arange(long)[None, :]) & live[:, None]

        def spread(value):
            return jnp.sum(jnp.where(moved, value[:, None], 0), axis=0)

        facts = jnp.stack(
            [
                spread(slot_ids),
                spread(sources - band_tiles) + band_tiles,
                spread(targets),
                jnp.broadcast_to(jnp.sum(filled) // 2, (long,)),
            ]
        )
        return facts, sibling(facts), sib_tiles

    first_page = (row_index * grid_cols + col_index - core) * own_rows
    ids = lax.dynamic_slice_in_dim(seed_ids, core * half, half, 0).T
    restart = pl.pallas_call(
        seed_kernel,
        out_shape=jax.ShapeDtypeStruct((2 * own_rows, half), jnp.float32),
        in_specs=[smem(), vmem()],
        out_specs=vmem(),
        compiler_params=params(4),
        name="seed_counts",
    )(first_page.reshape(1), ids)

    def multiply(pieces, names, coded, facts, sib_facts, sib_tiles):
        order = jnp.stack([(high ^ y) * depth + (z + d) % depth for y, d in names])
        n = len(pieces)
        rows = per * TILE
        parts = jax.ShapeDtypeStruct((grid_rows, rows + 16, half), jnp.int16)
        scratch = [
            VMEM((band_tiles + 1, TILE, half), jnp.bfloat16),
            VMEM((target_total + 1, TILE, half), jnp.float32),
            VMEM((2 * slots, TILE, TILE), tile_values.dtype),
            pltpu.SemaphoreType.DMA((2,)),
        ]
        tiles = (in_hbm(tile_values), in_hbm(sib_tiles))
        if coded:
            return pl.pallas_call(
                lambda *refs: first_kernel(n, rows, *refs),
                out_shape=(parts, jax.ShapeDtypeStruct((rows, half), jnp.float32)),
                in_specs=[smem()] * 3 + [anywhere()] * 2 + [vmem()] * n,
                out_specs=(vmem(), vmem()),
                scratch_shapes=scratch
                + [VMEM((chips, per, TILE), jnp.float32), VMEM((TILE, TILE), jnp.float32)],
                compiler_params=params(20),
                name="first_products",
            )(facts, sib_facts, order, *tiles, *pieces)
        return pl.pallas_call(
            lambda *refs: later_kernel(n, rows, *refs),
            out_shape=parts,
            in_specs=[smem()] * 3 + [anywhere()] * 2 + [vmem()] * n,
            out_specs=vmem(),
            scratch_shapes=scratch,
            compiler_params=params(20),
            name="later_products",
        )(facts, sib_facts, order, *tiles, *pieces)

    def update(parts, inverse, scaled):
        return pl.pallas_call(
            lambda *refs: current_kernel(scaled, *refs),
            out_shape=jax.ShapeDtypeStruct(
                (per * TILE, half), jnp.bfloat16 if scaled else jnp.float32
            ),
            in_specs=[vmem()] * 3,
            out_specs=vmem(),
            compiler_params=params(6),
            name="current",
        )(parts, restart, inverse)

    pieces, names, tile_facts = gather(block, sums, order_tiles)
    parts, inverse = multiply(pieces, names, True, *tile_facts)
    parts = lax.all_to_all(parts, "row", 0, 0, tiled=True)
    panel = update(parts, inverse, True)
    pieces, names, _ = gather(panel)
    parts = multiply(pieces, names, False, *tile_facts)
    parts = lax.all_to_all(parts, "row", 0, 0, tiled=True)
    current = update(parts, inverse, False)
    mine = lax.dynamic_slice_in_dim(current, core * own_rows, own_rows, 0)
    theirs = sibling(lax.dynamic_slice_in_dim(current, (1 - core) * own_rows, own_rows, 0))
    return jnp.where(
        core == 0,
        jnp.concatenate([mine, theirs], axis=1),
        jnp.concatenate([theirs, mine], axis=1),
    )


def solution(mesh):
    placed = (
        P(("row", "col"), None),
        P(("row", "col"), None, None),
        P(("row", "col")),
        P(("row", "col")),
        P(("row", "col")),
        P(),
    )
    return jax.shard_map(
        per_device, mesh=mesh, in_specs=placed, out_specs=P(("row", "col"), None), check_vma=False
    )
```

```python
import jax
import jax.numpy as jnp
from jax import lax
from jax.experimental import pallas as pl
from jax.experimental.pallas import tpu as pltpu
from jax.sharding import PartitionSpec as P

BT = 2
TILE = 128
LANES = 128
damping = 0.85
teleport = 0.15
LOW, HIGH = 0.2, 2.0
STEPS = 65535.0
HALF = 32768.0
FAR = 1 << 30
VMEM = pltpu.VMEM
SMEM = pltpu.SMEM


def vmem(*_):
    return pl.BlockSpec(memory_space=VMEM)


def smem(*_):
    return pl.BlockSpec(memory_space=SMEM)


def anywhere(*_):
    return pl.BlockSpec(memory_space=pl.ANY)


def in_hbm(value):
    return pltpu.with_memory_space_constraint(value, pltpu.HBM)


def params(mebibytes):
    return pltpu.CompilerParams(vmem_limit_bytes=mebibytes * 1024 * 1024)


def column_kernel(source_ref, count_ref, given_ref, sums_ref, tiles_ref, arrived):
    slots = given_ref.shape[0]
    chunk = slots // arrived.shape[0]
    copies = []
    for c in range(arrived.shape[0]):
        span = pl.ds(c * chunk, chunk)
        copies.append(
            pltpu.make_async_copy(given_ref.at[span], tiles_ref.at[span], arrived.at[c])
        )
        copies[c].start()
    sums_ref[...] = jnp.zeros_like(sums_ref)

    def group(g, carry):
        columns = [
            jnp.sum(tiles_ref[8 * g + u].astype(jnp.float32), axis=0, keepdims=True) for u in range(8)
        ]
        for u in range(8):
            k = 8 * g + u
            live = jnp.where(k < count_ref[0], 1.0, 0.0)
            sums_ref[pl.ds(source_ref[k] % sums_ref.shape[0], 1), :] += columns[u] * live
        return carry

    for c in range(arrived.shape[0]):
        copies[c].wait()
        last = jnp.minimum((c + 1) * chunk, count_ref[0])
        lax.fori_loop(c * chunk // 8, (last + 7) // 8, group, 0)


def encode(value):
    exponent = jnp.floor(jnp.log2(jnp.maximum(value, 1e-30))) + 1.0
    mantissa = (value * jnp.exp2(24.0 - exponent) + 0.5).astype(jnp.int32)
    mantissa = jnp.minimum(mantissa, (1 << 24) - 1)
    upper = (exponent.astype(jnp.int32) + 127) * 256 + (mantissa >> 16)
    return (jnp.concatenate([upper, mantissa & 65535]) - 32768).astype(jnp.int16)


def decode(code):
    code = code.astype(jnp.int32) + 32768
    each = code.shape[0] // 2
    upper, lower = code[:each], code[each:]
    mantissa = ((upper & 255) * 65536 + lower).astype(jnp.float32)
    return mantissa * jnp.exp2(((upper >> 8) - (127 + 24)).astype(jnp.float32))


def column_totals(rows, each, piece_refs):
    total = jnp.zeros((each, LANES), jnp.float32)
    for piece_ref in piece_refs:
        if piece_ref.shape[0] > rows:
            total += decode(piece_ref[rows : rows + 2 * each, :])
    return total


def seed_kernel(first_ref, ids_ref, counts_ref, pages_ref):
    total, lanes = ids_ref.shape
    pages = counts_ref.shape[0]
    first = first_ref[0]
    chunk = 256
    counts_ref[...] = jnp.zeros_like(counts_ref)

    def fold(value, reduce):
        parts = [value[i : i + 8] for i in range(0, value.shape[0], 8)]
        while len(parts) > 1:
            parts = [reduce(p, q) for p, q in zip(parts[::2], parts[1::2])]
        return parts[0]

    def rows(i):
        return pl.ds(pl.multiple_of(i * chunk, chunk), chunk)

    def prepare(i, best):
        page = ids_ref[rows(i), :] - first
        page = jnp.where((page >= 0) & (page < pages), page, FAR)
        pages_ref[rows(i), :] = page
        return jnp.minimum(best, fold(page, jnp.minimum))

    def more(carry):
        return carry[1] < pages

    def walk(carry):
        page_now, _ = carry

        def step(i, inner):
            best, seen = inner
            page = pages_ref[rows(i), :]
            found = jnp.where(page > page_now, page, FAR)
            same = jnp.where(page == page_now, 1.0, 0.0)
            return jnp.minimum(best, fold(found, jnp.minimum)), seen + fold(same, jnp.add)

        best, seen = lax.fori_loop(0, total // chunk, step, (far, jnp.zeros((8, lanes), jnp.float32)))
        seen = jnp.sum(seen, axis=0, keepdims=True)

        def place(i, inner):
            here = lax.broadcasted_iota(jnp.int32, (chunk, lanes), 0) + i * chunk
            counts_ref[rows(i), :] += jnp.where(here == page_now, seen, 0.0)
            return inner

        lax.fori_loop(0, pages // chunk, place, 0)
        later = jnp.min(best, axis=0, keepdims=True)
        return later, jnp.min(later)

    far = jnp.full((8, lanes), FAR, jnp.int32)
    best = lax.fori_loop(0, total // chunk, prepare, far)
    start = jnp.min(best, axis=0, keepdims=True)
    lax.while_loop(more, walk, (start, jnp.min(start)))


def fetch(own_ref, sib_ref, tiles, arrived):
    slots = own_ref.shape[0]
    copies = [
        pltpu.make_async_copy(own_ref, tiles.at[pl.ds(0, slots)], arrived.at[0]),
        pltpu.make_async_copy(sib_ref, tiles.at[pl.ds(slots, slots)], arrived.at[1]),
    ]
    for copy in copies:
        copy.start()
    return copies


def products(facts_refs, copies, tiles, panel, total, out_ref):
    unroll = 16
    slots = tiles.shape[0] // 2
    dummy = total.shape[0] - 1
    for which, facts_ref in enumerate(facts_refs):
        copies[which].wait()
        pairs = facts_ref[3, 0]

        def group(g, carry, base=which * slots, facts_ref=facts_ref, pairs=pairs):
            for u in range(unroll):
                pair = g * unroll + u
                at = 2 * pair
                target = jnp.where(pair < pairs, facts_ref[2, at], dummy)
                left = jnp.concatenate(
                    [tiles[base + facts_ref[0, at]], tiles[base + facts_ref[0, at + 1]]], axis=1
                )
                right = jnp.concatenate(
                    [panel[facts_ref[1, at]], panel[facts_ref[1, at + 1]]], axis=0
                )
                total[target] += jnp.dot(left, right, preferred_element_type=jnp.float32)
            return carry

        lax.fori_loop(0, (pairs + unroll - 1) // unroll, group, 0)
    receivers = out_ref.shape[0]
    per = (out_ref.shape[1] - 16) // TILE

    def send(r, carry):
        exponents = []
        for t in range(per):
            block = total[r * per + t]
            top = jnp.maximum(jnp.max(block, axis=0, keepdims=True), 1e-30)
            exponent = jnp.floor(jnp.log2(top)) + 1.0
            exponents.append(exponent)
            code = block * jnp.exp2(16.0 - exponent) + 0.5
            code = jnp.clip(code.astype(jnp.int32), 0, 65535) - 32768
            out_ref[r, t * TILE : (t + 1) * TILE, :] = code.astype(jnp.int16)
        rows = exponents + [jnp.zeros((16 - per, LANES), jnp.float32)]
        tail = jnp.concatenate(rows, axis=0).astype(jnp.int32).astype(jnp.int16)
        out_ref[r, per * TILE : per * TILE + 16, :] = tail
        return carry

    lax.fori_loop(0, receivers, send, 0)


def first_kernel(pieces, far, rows, own_facts, sib_facts, chip_ref, own_ref, sib_ref, *refs):
    piece_refs = list(refs[:pieces])
    out_ref, inverse_ref, panel, total, tiles, arrived, sums_ref, ordered, brought, near = refs[pieces:]
    brings = []
    for i, piece_ref in enumerate(piece_refs[pieces - far :]):
        inside = brought.at[i, pl.ds(0, piece_ref.shape[0])]
        brings.append(pltpu.make_async_copy(piece_ref, inside, near.at[i]))
        brings[i].start()
        piece_refs[pieces - far + i] = inside
    copies = fetch(own_ref, sib_ref, tiles, arrived)
    total[...] = jnp.zeros_like(total)
    groups, per, _ = sums_ref.shape
    sums = column_totals(rows, groups * per, piece_refs[: pieces - far])
    for bring in brings:
        bring.wait()
    sums = sums + column_totals(rows, groups * per, piece_refs[pieces - far :])
    for g in range(groups):
        sums_ref[g] = sums[g * per : (g + 1) * per]
    ordered[...] = jnp.zeros_like(ordered)
    for p in range(pieces):
        ordered[p * per : (p + 1) * per, :] = sums_ref[chip_ref[p]]
    inverse = (1.0 / jnp.maximum(ordered[...], 1.0)).T
    for p in range(pieces):
        for t in range(per):
            column = inverse[:, p * per + t : p * per + t + 1]
            code = piece_refs[p][t * TILE : (t + 1) * TILE, :].astype(jnp.float32)
            score = (code + HALF) * ((HIGH - LOW) / STEPS) + LOW
            panel[chip_ref[p] * per + t] = (score * column).astype(jnp.bfloat16)
            if p == 0:
                inverse_ref[t * TILE : (t + 1) * TILE, :] = jnp.broadcast_to(column, (TILE, LANES))
    panel[pieces * per] = jnp.zeros((TILE, LANES), jnp.bfloat16)
    products((own_facts, sib_facts), copies, tiles, panel, total, out_ref)


def later_kernel(pieces, rows, own_facts, sib_facts, chip_ref, own_ref, sib_ref, *refs):
    piece_refs = refs[:pieces]
    out_ref, panel, total, tiles, arrived = refs[pieces:]
    copies = fetch(own_ref, sib_ref, tiles, arrived)
    total[...] = jnp.zeros_like(total)
    per = rows // TILE
    for p in range(pieces):
        for t in range(per):
            panel[chip_ref[p] * per + t] = piece_refs[p][t * TILE : (t + 1) * TILE, :]
    panel[pieces * per] = jnp.zeros((TILE, LANES), jnp.bfloat16)
    products((own_facts, sib_facts), copies, tiles, panel, total, out_ref)


def current_kernel(scaled, parts_ref, restart_ref, inverse_ref, out_ref):
    senders = parts_ref.shape[0]
    per = (parts_ref.shape[1] - 16) // TILE
    for t in range(per):
        rows = slice(t * TILE, (t + 1) * TILE)
        summed = jnp.zeros((TILE, LANES), jnp.float32)
        for r in range(senders):
            tail = parts_ref[r, per * TILE : per * TILE + 16, :].astype(jnp.float32)
            scale = jnp.exp2(tail[t : t + 1, :] - 16.0)
            summed += (parts_ref[r, rows, :].astype(jnp.float32) + HALF) * scale
        current = damping * summed + teleport * restart_ref[rows, :]
        if scaled:
            current = current * inverse_ref[rows, :]
        out_ref[rows, :] = current.astype(out_ref.dtype)


def per_device(scores, tile_values, tile_rows, tile_cols, tile_count, seed_ids):
    grid_rows = lax.axis_size("row")
    grid_cols = lax.axis_size("col")
    row_index = lax.axis_index("row")
    col_index = lax.axis_index("col")
    depth = grid_cols // 4
    high, z, core = col_index // (2 * depth), col_index // 2 % depth, col_index % 2
    own_rows = scores.shape[0]
    columns = scores.shape[1]
    slots = tile_values.shape[0]
    seed_total = seed_ids.shape[1]
    band_tiles = grid_cols * BT
    chips = grid_cols // 2
    per = 2 * BT

    def by_col(value, move):
        pairs = []
        for c in range(grid_cols):
            y, at, k = move(c // (2 * depth), c // 2 % depth, c % 2)
            pairs.append((c, (y * depth + at) * 2 + k))
        return lax.ppermute(value, "col", pairs)

    def sibling(value):
        return by_col(value, lambda y, at, k: (y, at, 1 - k))

    def along(value, step):
        return by_col(value, lambda y, at, k: (y, (at + step) % depth, k))

    def across(value):
        return by_col(value, lambda y, at, k: (1 - y, at, k))

    tie = lax.optimization_barrier

    def gather(block, sums=None, later=None):
        rows = block.shape[0]
        a, b = along(block, 1), along(block, -1)
        if sums is None:
            other = across(block)
        else:
            other = across(jnp.concatenate([block, encode(sums)]))
            a, b, other = tie((a, b, other))
            sums = sums + decode(other[rows:])
            other = jnp.concatenate([other[:rows], encode(sums)])
        pieces, names, beside = [block, other], [(0, 0), (1, 0)], None
        c, d = other, other
        for step in range(1, depth // 2):
            if step > 1:
                a, b = along(a, 1), along(b, -1)
            c, d = along(c, 1), along(d, -1)
            if later is not None and step == depth // 2 - 1:
                c, raw = tie((c, (tile_rows, tile_cols, tile_count)))
                beside = later(*raw)
            pieces += [a, b, c, d]
            names += [(0, -step), (0, step), (1, -step), (1, step)]
        pieces += [along(a, 1), along(d, -1)]
        names += [(0, depth // 2), (1, depth // 2)]
        return pieces, names, beside

    half = columns // 2
    code = ((scores - LOW) * (STEPS / (HIGH - LOW)) + 0.5).astype(jnp.int32)
    code = (jnp.clip(code, 0, 65535) - 32768).astype(jnp.int16)
    code, count = tie((code, tile_count))
    mine = lax.dynamic_slice_in_dim(code, core * half, half, 1)
    theirs = sibling(lax.dynamic_slice_in_dim(code, (1 - core) * half, half, 1))
    block = jnp.where(
        core == 0, jnp.concatenate([mine, theirs]), jnp.concatenate([theirs, mine])
    )
    sib_tiles = sibling(tile_values)
    sums = pl.pallas_call(
        column_kernel,
        out_shape=jax.ShapeDtypeStruct((band_tiles, TILE), jnp.float32),
        in_specs=[smem(), smem(), anywhere()],
        out_specs=vmem(),
        scratch_shapes=[VMEM(tile_values.shape, tile_values.dtype), pltpu.SemaphoreType.DMA((4,))],
        compiler_params=params(8),
        name="column_sums",
    )(tile_cols, count, in_hbm(tile_values))

    sums = sums + sibling(sums)

    target_total = grid_rows * per

    def order_tiles(tile_rows, tile_cols, tile_count):
        sources = tile_cols - row_index * band_tiles
        targets = tile_rows // band_tiles * per + core * BT + tile_rows % BT
        slot_ids = jnp.arange(slots, dtype=jnp.int32)
        live = slot_ids < tile_count[0]
        target_ids = jnp.arange(target_total, dtype=jnp.int32)
        at_target = (targets[:, None] == target_ids[None, :]) & live[:, None]
        filled = (jnp.sum(at_target.astype(jnp.int32), axis=0) + 1) // 2 * 2
        before = target_ids[:, None] < target_ids[None, :]
        start = jnp.sum(jnp.where(before, filled[:, None], 0), axis=0)
        alike = (targets[:, None] == targets[None, :]) & (slot_ids[None, :] < slot_ids[:, None])
        place = jnp.sum(alike.astype(jnp.int32), axis=1)
        place = place + jnp.sum(jnp.where(at_target, start[None, :], 0), axis=1)
        long = slots + target_total
        moved = (place[:, None] == jnp.arange(long)[None, :]) & live[:, None]

        def spread(value):
            return jnp.sum(jnp.where(moved, value[:, None], 0), axis=0)

        facts = jnp.stack(
            [
                spread(slot_ids),
                spread(sources - band_tiles) + band_tiles,
                spread(targets),
                jnp.broadcast_to(jnp.sum(filled) // 2, (long,)),
            ]
        )
        return facts, sibling(facts), sib_tiles

    first_page = (row_index * grid_cols + col_index - core) * own_rows
    ids = lax.dynamic_slice_in_dim(seed_ids, core * half, half, 0).T
    restart = pl.pallas_call(
        seed_kernel,
        out_shape=jax.ShapeDtypeStruct((2 * own_rows, half), jnp.float32),
        in_specs=[smem(), vmem()],
        out_specs=vmem(),
        scratch_shapes=[VMEM(ids.shape, jnp.int32)],
        compiler_params=params(4),
        name="seed_counts",
    )(first_page.reshape(1), ids)

    def multiply(pieces, names, coded, facts, sib_facts, sib_tiles):
        order = jnp.stack([(high ^ y) * depth + (z + d) % depth for y, d in names])
        n = len(pieces)
        rows = per * TILE
        parts = jax.ShapeDtypeStruct((grid_rows, rows + 16, half), jnp.int16)
        scratch = [
            VMEM((band_tiles + 1, TILE, half), jnp.bfloat16),
            VMEM((target_total + 1, TILE, half), jnp.float32),
            VMEM((2 * slots, TILE, TILE), tile_values.dtype),
            pltpu.SemaphoreType.DMA((2,)),
        ]
        tiles = (in_hbm(tile_values), in_hbm(sib_tiles))
        if coded:
            far = 6
            pieces = pieces[: n - far] + [in_hbm(piece) for piece in pieces[n - far :]]
            longest = max(piece.shape[0] for piece in pieces)
            return pl.pallas_call(
                lambda *refs: first_kernel(n, far, rows, *refs),
                out_shape=(parts, jax.ShapeDtypeStruct((rows, half), jnp.float32)),
                in_specs=[smem()] * 3
                + [anywhere()] * 2
                + [vmem()] * (n - far)
                + [anywhere()] * far,
                out_specs=(vmem(), vmem()),
                scratch_shapes=scratch
                + [
                    VMEM((chips, per, TILE), jnp.float32),
                    VMEM((TILE, TILE), jnp.float32),
                    VMEM((far, longest, half), jnp.int16),
                    pltpu.SemaphoreType.DMA((far,)),
                ],
                compiler_params=params(20),
                name="first_products",
            )(facts, sib_facts, order, *tiles, *pieces)
        return pl.pallas_call(
            lambda *refs: later_kernel(n, rows, *refs),
            out_shape=parts,
            in_specs=[smem()] * 3 + [anywhere()] * 2 + [vmem()] * n,
            out_specs=vmem(),
            scratch_shapes=scratch,
            compiler_params=params(20),
            name="later_products",
        )(facts, sib_facts, order, *tiles, *pieces)

    def update(parts, inverse, scaled):
        return pl.pallas_call(
            lambda *refs: current_kernel(scaled, *refs),
            out_shape=jax.ShapeDtypeStruct(
                (per * TILE, half), jnp.bfloat16 if scaled else jnp.float32
            ),
            in_specs=[vmem()] * 3,
            out_specs=vmem(),
            compiler_params=params(6),
            name="current",
        )(parts, restart, inverse)

    pieces, names, tile_facts = gather(block, sums, order_tiles)
    parts, inverse = multiply(pieces, names, True, *tile_facts)
    parts = lax.all_to_all(parts, "row", 0, 0, tiled=True)
    panel = update(parts, inverse, True)
    pieces, names, _ = gather(panel)
    parts = multiply(pieces, names, False, *tile_facts)
    parts = lax.all_to_all(parts, "row", 0, 0, tiled=True)
    current = update(parts, inverse, False)
    mine = lax.dynamic_slice_in_dim(current, core * own_rows, own_rows, 0)
    theirs = sibling(lax.dynamic_slice_in_dim(current, (1 - core) * own_rows, own_rows, 0))
    return jnp.where(
        core == 0,
        jnp.concatenate([mine, theirs], axis=1),
        jnp.concatenate([theirs, mine], axis=1),
    )


def solution(mesh):
    placed = (
        P(("row", "col"), None),
        P(("row", "col"), None, None),
        P(("row", "col")),
        P(("row", "col")),
        P(("row", "col")),
        P(),
    )
    return jax.shard_map(
        per_device, mesh=mesh, in_specs=placed, out_specs=P(("row", "col"), None), check_vma=False
    )
```

```python
import jax
import jax.numpy as jnp
from jax import lax
from jax.experimental import pallas as pl
from jax.experimental.pallas import tpu as pltpu
from jax.sharding import PartitionSpec as P

BT = 2
TILE = 128
LANES = 128
damping = 0.85
teleport = 0.15
LOW, HIGH = 0.2, 2.0
STEPS = 65535.0
HALF = 32768.0
FAR = 1 << 30
VMEM = pltpu.VMEM
SMEM = pltpu.SMEM


def vmem(*_):
    return pl.BlockSpec(memory_space=VMEM)


def smem(*_):
    return pl.BlockSpec(memory_space=SMEM)


def anywhere(*_):
    return pl.BlockSpec(memory_space=pl.ANY)


def in_hbm(value):
    return pltpu.with_memory_space_constraint(value, pltpu.HBM)


def params(mebibytes):
    return pltpu.CompilerParams(vmem_limit_bytes=mebibytes * 1024 * 1024)


def column_kernel(source_ref, count_ref, given_ref, sums_ref, tiles_ref, arrived):
    slots = given_ref.shape[0]
    chunk = slots // arrived.shape[0]
    copies = []
    for c in range(arrived.shape[0]):
        span = pl.ds(c * chunk, chunk)
        copies.append(
            pltpu.make_async_copy(given_ref.at[span], tiles_ref.at[span], arrived.at[c])
        )
        copies[c].start()
    sums_ref[...] = jnp.zeros_like(sums_ref)

    def group(g, carry):
        columns = [
            jnp.sum(tiles_ref[8 * g + u].astype(jnp.float32), axis=0, keepdims=True) for u in range(8)
        ]
        for u in range(8):
            k = 8 * g + u
            live = jnp.where(k < count_ref[0], 1.0, 0.0)
            sums_ref[pl.ds(source_ref[k] % sums_ref.shape[0], 1), :] += columns[u] * live
        return carry

    for c in range(arrived.shape[0]):
        copies[c].wait()
        last = jnp.minimum((c + 1) * chunk, count_ref[0])
        lax.fori_loop(c * chunk // 8, (last + 7) // 8, group, 0)


def encode(value):
    exponent = jnp.floor(jnp.log2(jnp.maximum(value, 1e-30))) + 1.0
    mantissa = (value * jnp.exp2(24.0 - exponent) + 0.5).astype(jnp.int32)
    mantissa = jnp.minimum(mantissa, (1 << 24) - 1)
    upper = (exponent.astype(jnp.int32) + 127) * 256 + (mantissa >> 16)
    return (jnp.concatenate([upper, mantissa & 65535]) - 32768).astype(jnp.int16)


def decode(code):
    code = code.astype(jnp.int32) + 32768
    each = code.shape[0] // 2
    upper, lower = code[:each], code[each:]
    mantissa = ((upper & 255) * 65536 + lower).astype(jnp.float32)
    return mantissa * jnp.exp2(((upper >> 8) - (127 + 24)).astype(jnp.float32))


def seed_kernel(first_ref, ids_ref, counts_ref, pages_ref):
    total, lanes = ids_ref.shape
    pages = counts_ref.shape[0]
    first = first_ref[0]
    chunk = 256
    counts_ref[...] = jnp.zeros_like(counts_ref)

    def fold(value, reduce):
        parts = [value[i : i + 8] for i in range(0, value.shape[0], 8)]
        while len(parts) > 1:
            parts = [reduce(p, q) for p, q in zip(parts[::2], parts[1::2])]
        return parts[0]

    def rows(i):
        return pl.ds(pl.multiple_of(i * chunk, chunk), chunk)

    def prepare(i, best):
        page = ids_ref[rows(i), :] - first
        page = jnp.where((page >= 0) & (page < pages), page, FAR)
        pages_ref[rows(i), :] = page
        return jnp.minimum(best, fold(page, jnp.minimum))

    def more(carry):
        return carry[1] < pages

    def walk(carry):
        page_now, _ = carry

        def step(i, inner):
            best, seen = inner
            page = pages_ref[rows(i), :]
            found = jnp.where(page > page_now, page, FAR)
            same = jnp.where(page == page_now, 1.0, 0.0)
            return jnp.minimum(best, fold(found, jnp.minimum)), seen + fold(same, jnp.add)

        best, seen = lax.fori_loop(0, total // chunk, step, (far, jnp.zeros((8, lanes), jnp.float32)))
        seen = jnp.sum(seen, axis=0, keepdims=True)

        def place(i, inner):
            here = lax.broadcasted_iota(jnp.int32, (chunk, lanes), 0) + i * chunk
            counts_ref[rows(i), :] += jnp.where(here == page_now, seen, 0.0)
            return inner

        lax.fori_loop(0, pages // chunk, place, 0)
        later = jnp.min(best, axis=0, keepdims=True)
        return later, jnp.min(later)

    far = jnp.full((8, lanes), FAR, jnp.int32)
    best = lax.fori_loop(0, total // chunk, prepare, far)
    start = jnp.min(best, axis=0, keepdims=True)
    lax.while_loop(more, walk, (start, jnp.min(start)))


def fetch(own_ref, sib_ref, tiles, arrived):
    slots = own_ref.shape[0]
    copies = [
        pltpu.make_async_copy(own_ref, tiles.at[pl.ds(0, slots)], arrived.at[0]),
        pltpu.make_async_copy(sib_ref, tiles.at[pl.ds(slots, slots)], arrived.at[1]),
    ]
    for copy in copies:
        copy.start()
    return copies


def products(facts_refs, copies, tiles, panel, total):
    unroll = 16
    slots = tiles.shape[0] // 2
    dummy = total.shape[0] - 1
    for which, facts_ref in enumerate(facts_refs):
        copies[which].wait()
        pairs = facts_ref[3, 0]

        def group(g, carry, base=which * slots, facts_ref=facts_ref, pairs=pairs):
            for u in range(unroll):
                pair = g * unroll + u
                at = 2 * pair
                target = jnp.where(pair < pairs, facts_ref[2, at], dummy)
                left = jnp.concatenate(
                    [tiles[base + facts_ref[0, at]], tiles[base + facts_ref[0, at + 1]]], axis=1
                )
                right = jnp.concatenate(
                    [panel[facts_ref[1, at]], panel[facts_ref[1, at + 1]]], axis=0
                )
                total[target] += jnp.dot(left, right, preferred_element_type=jnp.float32)
            return carry

        lax.fori_loop(0, (pairs + unroll - 1) // unroll, group, 0)


def single_products(slot_refs, count_ref, core_ref, copies, tiles, panel, total):
    unroll = 16
    slots = tiles.shape[0] // 2
    dummy = total.shape[0] - 1
    per = 2 * BT
    band = panel.shape[0] - 1
    for which in range(2):
        copies[which].wait()
        rows_ref, cols_ref = slot_refs[2 * which : 2 * which + 2]
        owner = core_ref[0] if which == 0 else 1 - core_ref[0]

        def group(g, carry, which=which, rows_ref=rows_ref, cols_ref=cols_ref, owner=owner):
            for u in range(unroll):
                k = g * unroll + u
                target = rows_ref[k] // band * per + owner * BT + rows_ref[k] % BT
                target = jnp.where(k < count_ref[which], target, dummy)
                total[target] += jnp.dot(
                    tiles[which * slots + k],
                    panel[cols_ref[k] % band],
                    preferred_element_type=jnp.float32,
                )
            return carry

        lax.fori_loop(0, (count_ref[which] + unroll - 1) // unroll, group, 0)


def round_parts(total, out_ref):
    receivers = out_ref.shape[0]
    per = (out_ref.shape[1] - 16) // TILE

    def send(r, carry):
        exponents = []
        for t in range(per):
            block = total[r * per + t]
            top = jnp.maximum(jnp.max(block, axis=0, keepdims=True), 1e-30)
            exponent = jnp.floor(jnp.log2(top)) + 1.0
            exponents.append(exponent)
            code = block * jnp.exp2(16.0 - exponent) + 0.5
            code = jnp.clip(code.astype(jnp.int32), 0, 65535) - 32768
            out_ref[r, t * TILE : (t + 1) * TILE, :] = code.astype(jnp.int16)
        rows = exponents + [jnp.zeros((16 - per, LANES), jnp.float32)]
        tail = jnp.concatenate(rows, axis=0).astype(jnp.int32).astype(jnp.int16)
        out_ref[r, per * TILE : per * TILE + 16, :] = tail
        return carry

    lax.fori_loop(0, receivers, send, 0)


def first_kernel(pieces, far, *refs):
    slot_refs, (count_ref, core_ref, chip_ref, sums_ref, own_ref, sib_ref) = refs[:4], refs[4:10]
    piece_refs = list(refs[10 : 10 + pieces])
    out_ref, inverse_ref, panel, total, tiles, arrived, ordered, brought, near = refs[10 + pieces :]
    brings = {}
    for i in range(far):
        p = pieces - far + i
        inside = brought.at[i, pl.ds(0, piece_refs[p].shape[0])]
        brings[p] = pltpu.make_async_copy(piece_refs[p], inside, near.at[i])
        brings[p].start()
        piece_refs[p] = inside
    copies = fetch(own_ref, sib_ref, tiles, arrived)
    total[...] = jnp.zeros_like(total)
    groups, per, _ = sums_ref.shape
    ordered[...] = jnp.zeros_like(ordered)
    for p in range(pieces):
        ordered[p * per : (p + 1) * per, :] = sums_ref[chip_ref[p]]
    inverse = (1.0 / jnp.maximum(ordered[...], 1.0)).T
    for p in range(pieces):
        if p in brings:
            brings[p].wait()
        for t in range(per):
            column = inverse[:, p * per + t : p * per + t + 1]
            code = piece_refs[p][t * TILE : (t + 1) * TILE, :].astype(jnp.float32)
            score = (code + HALF) * ((HIGH - LOW) / STEPS) + LOW
            panel[chip_ref[p] * per + t] = (score * column).astype(jnp.bfloat16)
            if p == 0:
                inverse_ref[t * TILE : (t + 1) * TILE, :] = jnp.broadcast_to(column, (TILE, LANES))
    single_products(slot_refs, count_ref, core_ref, copies, tiles, panel, total)
    round_parts(total, out_ref)


def later_kernel(pieces, rows, own_facts, sib_facts, chip_ref, own_ref, sib_ref, *refs):
    piece_refs = refs[:pieces]
    out_ref, panel, total, tiles, arrived = refs[pieces:]
    copies = fetch(own_ref, sib_ref, tiles, arrived)
    total[...] = jnp.zeros_like(total)
    per = rows // TILE
    for p in range(pieces):
        for t in range(per):
            panel[chip_ref[p] * per + t] = piece_refs[p][t * TILE : (t + 1) * TILE, :]
    panel[pieces * per] = jnp.zeros((TILE, LANES), jnp.bfloat16)
    products((own_facts, sib_facts), copies, tiles, panel, total)
    round_parts(total, out_ref)


def current_kernel(scaled, parts_ref, restart_ref, inverse_ref, out_ref):
    senders = parts_ref.shape[0]
    per = (parts_ref.shape[1] - 16) // TILE
    for t in range(per):
        rows = slice(t * TILE, (t + 1) * TILE)
        summed = jnp.zeros((TILE, LANES), jnp.float32)
        for r in range(senders):
            tail = parts_ref[r, per * TILE : per * TILE + 16, :].astype(jnp.float32)
            scale = jnp.exp2(tail[t : t + 1, :] - 16.0)
            summed += (parts_ref[r, rows, :].astype(jnp.float32) + HALF) * scale
        current = damping * summed + teleport * restart_ref[rows, :]
        if scaled:
            current = current * inverse_ref[rows, :]
        out_ref[rows, :] = current.astype(out_ref.dtype)


def per_device(scores, tile_values, tile_rows, tile_cols, tile_count, seed_ids):
    grid_rows = lax.axis_size("row")
    grid_cols = lax.axis_size("col")
    row_index = lax.axis_index("row")
    col_index = lax.axis_index("col")
    depth = grid_cols // 4
    high, z, core = col_index // (2 * depth), col_index // 2 % depth, col_index % 2
    own_rows = scores.shape[0]
    columns = scores.shape[1]
    slots = tile_values.shape[0]
    seed_total = seed_ids.shape[1]
    band_tiles = grid_cols * BT
    chips = grid_cols // 2
    per = 2 * BT

    def by_col(value, move):
        pairs = []
        for c in range(grid_cols):
            y, at, k = move(c // (2 * depth), c // 2 % depth, c % 2)
            pairs.append((c, (y * depth + at) * 2 + k))
        return lax.ppermute(value, "col", pairs)

    def sibling(value):
        return by_col(value, lambda y, at, k: (y, at, 1 - k))

    def along(value, step):
        return by_col(value, lambda y, at, k: (y, (at + step) % depth, k))

    def across(value):
        return by_col(value, lambda y, at, k: (1 - y, at, k))

    tie = lax.optimization_barrier

    def gather(block, sums=None):
        rows = block.shape[0]
        other = across(block)
        if sums is not None:
            block = jnp.concatenate([block, encode(sums)])
        pieces, names = [block, other], [(0, 0), (1, 0)]
        a, b, c, d = block, block, other, other
        for step in range(1, depth // 2):
            a, b = along(a, 1), along(b, -1)
            c, d = along(c, 1), along(d, -1)
            pieces += [a, b, c, d]
            names += [(0, -step), (0, step), (1, -step), (1, step)]
        a = along(a, 1)
        if sums is not None:
            plane = [p for p, (y, _) in zip(pieces, names) if y == 0] + [a]
            found = sum(decode(p[rows:]) for p in plane[1:]) + sums
            sums = found + across(found)
        pieces += [a, along(d, -1)]
        names += [(0, depth // 2), (1, depth // 2)]
        return pieces, names, sums

    half = columns // 2
    code = ((scores - LOW) * (STEPS / (HIGH - LOW)) + 0.5).astype(jnp.int32)
    code = (jnp.clip(code, 0, 65535) - 32768).astype(jnp.int16)
    mine = lax.dynamic_slice_in_dim(code, core * half, half, 1)
    theirs = sibling(lax.dynamic_slice_in_dim(code, (1 - core) * half, half, 1))
    block = jnp.where(
        core == 0, jnp.concatenate([mine, theirs]), jnp.concatenate([theirs, mine])
    )
    slots_here = jnp.stack([tile_rows, tile_cols, jnp.broadcast_to(tile_count, (slots,))])
    slots_there = sibling(slots_here)
    sib_tiles = sibling(tile_values)
    sums = pl.pallas_call(
        column_kernel,
        out_shape=jax.ShapeDtypeStruct((band_tiles, TILE), jnp.float32),
        in_specs=[smem(), smem(), anywhere()],
        out_specs=vmem(),
        scratch_shapes=[VMEM(tile_values.shape, tile_values.dtype), pltpu.SemaphoreType.DMA((4,))],
        compiler_params=params(8),
        name="column_sums",
    )(tile_cols, tile_count, in_hbm(tile_values))

    sums = sums + sibling(sums)

    target_total = grid_rows * per

    def order_tiles(tile_rows, tile_cols, tile_count):
        sources = tile_cols - row_index * band_tiles
        targets = tile_rows // band_tiles * per + core * BT + tile_rows % BT
        slot_ids = jnp.arange(slots, dtype=jnp.int32)
        live = slot_ids < tile_count[0]
        target_ids = jnp.arange(target_total, dtype=jnp.int32)
        at_target = (targets[:, None] == target_ids[None, :]) & live[:, None]
        filled = (jnp.sum(at_target.astype(jnp.int32), axis=0) + 1) // 2 * 2
        before = target_ids[:, None] < target_ids[None, :]
        start = jnp.sum(jnp.where(before, filled[:, None], 0), axis=0)
        alike = (targets[:, None] == targets[None, :]) & (slot_ids[None, :] < slot_ids[:, None])
        place = jnp.sum(alike.astype(jnp.int32), axis=1)
        place = place + jnp.sum(jnp.where(at_target, start[None, :], 0), axis=1)
        long = slots + target_total
        moved = (place[:, None] == jnp.arange(long)[None, :]) & live[:, None]

        def spread(value):
            return jnp.sum(jnp.where(moved, value[:, None], 0), axis=0)

        facts = jnp.stack(
            [
                spread(slot_ids),
                spread(sources - band_tiles) + band_tiles,
                spread(targets),
                jnp.broadcast_to(jnp.sum(filled) // 2, (long,)),
            ]
        )
        return facts

    first_page = (row_index * grid_cols + col_index - core) * own_rows
    ids = lax.dynamic_slice_in_dim(seed_ids, core * half, half, 0).T
    restart = pl.pallas_call(
        seed_kernel,
        out_shape=jax.ShapeDtypeStruct((2 * own_rows, half), jnp.float32),
        in_specs=[smem(), vmem()],
        out_specs=vmem(),
        scratch_shapes=[VMEM(ids.shape, jnp.int32)],
        compiler_params=params(4),
        name="seed_counts",
    )(first_page.reshape(1), ids)

    def multiply(pieces, names, sums, facts):
        order = jnp.stack([(high ^ y) * depth + (z + d) % depth for y, d in names])
        n = len(pieces)
        rows = per * TILE
        parts = jax.ShapeDtypeStruct((grid_rows, rows + 16, half), jnp.int16)
        scratch = [
            VMEM((band_tiles + 1, TILE, half), jnp.bfloat16),
            VMEM((target_total + 1, TILE, half), jnp.float32),
            VMEM((2 * slots, TILE, TILE), tile_values.dtype),
            pltpu.SemaphoreType.DMA((2,)),
        ]
        tiles = (in_hbm(tile_values), in_hbm(sib_tiles))
        if sums is not None:
            far = 6
            pieces = pieces[: n - far] + [in_hbm(piece) for piece in pieces[n - far :]]
            longest = max(piece.shape[0] for piece in pieces)
            counts = jnp.concatenate([tile_count, slots_there[2, :1]])
            return pl.pallas_call(
                lambda *refs: first_kernel(n, far, *refs),
                out_shape=(parts, jax.ShapeDtypeStruct((rows, half), jnp.float32)),
                in_specs=[smem()] * 7
                + [vmem()]
                + [anywhere()] * 2
                + [vmem()] * (n - far)
                + [anywhere()] * far,
                out_specs=(vmem(), vmem()),
                scratch_shapes=scratch
                + [
                    VMEM((TILE, TILE), jnp.float32),
                    VMEM((far, longest, half), jnp.int16),
                    pltpu.SemaphoreType.DMA((far,)),
                ],
                compiler_params=params(20),
                name="first_products",
            )(
                tile_rows, tile_cols, slots_there[0], slots_there[1], counts, core.reshape(1),
                order, sums.reshape(chips, per, TILE), *tiles, *pieces,
            )
        return pl.pallas_call(
            lambda *refs: later_kernel(n, rows, *refs),
            out_shape=parts,
            in_specs=[smem()] * 3 + [anywhere()] * 2 + [vmem()] * n,
            out_specs=vmem(),
            scratch_shapes=scratch,
            compiler_params=params(20),
            name="later_products",
        )(*facts, order, *tiles, *pieces)

    def update(parts, inverse, scaled):
        return pl.pallas_call(
            lambda *refs: current_kernel(scaled, *refs),
            out_shape=jax.ShapeDtypeStruct(
                (per * TILE, half), jnp.bfloat16 if scaled else jnp.float32
            ),
            in_specs=[vmem()] * 3,
            out_specs=vmem(),
            compiler_params=params(6),
            name="current",
        )(parts, restart, inverse)

    pieces, names, sums = gather(block, sums)
    parts, inverse = multiply(pieces, names, sums, None)
    parts, raw = tie((parts, (tile_rows, tile_cols, tile_count)))
    facts = order_tiles(*raw)
    parts = lax.all_to_all(parts, "row", 0, 0, tiled=True)
    parts, facts = tie((parts, facts))
    facts = (facts, sibling(facts))
    panel = update(parts, inverse, True)
    pieces, names, _ = gather(panel)
    parts = multiply(pieces, names, None, facts)
    parts = lax.all_to_all(parts, "row", 0, 0, tiled=True)
    current = update(parts, inverse, False)
    mine = lax.dynamic_slice_in_dim(current, core * own_rows, own_rows, 0)
    theirs = sibling(lax.dynamic_slice_in_dim(current, (1 - core) * own_rows, own_rows, 0))
    return jnp.where(
        core == 0,
        jnp.concatenate([mine, theirs], axis=1),
        jnp.concatenate([theirs, mine], axis=1),
    )


def solution(mesh):
    placed = (
        P(("row", "col"), None),
        P(("row", "col"), None, None),
        P(("row", "col")),
        P(("row", "col")),
        P(("row", "col")),
        P(),
    )
    return jax.shard_map(
        per_device, mesh=mesh, in_specs=placed, out_specs=P(("row", "col"), None), check_vma=False
    )
```

```python
import jax
import jax.numpy as jnp
from jax import lax
from jax.experimental import pallas as pl
from jax.experimental.pallas import tpu as pltpu
from jax.sharding import PartitionSpec as P

BT = 2
TILE = 128
LANES = 128
damping = 0.85
teleport = 0.15
LOW, HIGH = 0.2, 2.0
STEPS = 65535.0
HALF = 32768.0
FAR = 1 << 30
VMEM = pltpu.VMEM
SMEM = pltpu.SMEM


def vmem(*_):
    return pl.BlockSpec(memory_space=VMEM)


def smem(*_):
    return pl.BlockSpec(memory_space=SMEM)


def anywhere(*_):
    return pl.BlockSpec(memory_space=pl.ANY)


def in_hbm(value):
    return pltpu.with_memory_space_constraint(value, pltpu.HBM)


def params(mebibytes):
    return pltpu.CompilerParams(vmem_limit_bytes=mebibytes * 1024 * 1024)


def column_kernel(source_ref, count_ref, given_ref, sums_ref, tiles_ref, arrived):
    slots = given_ref.shape[0]
    chunk = slots // arrived.shape[0]
    copies = []
    for c in range(arrived.shape[0]):
        span = pl.ds(c * chunk, chunk)
        copies.append(
            pltpu.make_async_copy(given_ref.at[span], tiles_ref.at[span], arrived.at[c])
        )
        copies[c].start()
    sums_ref[...] = jnp.zeros_like(sums_ref)

    def group(g, carry):
        columns = [
            jnp.sum(tiles_ref[8 * g + u].astype(jnp.float32), axis=0, keepdims=True) for u in range(8)
        ]
        for u in range(8):
            k = 8 * g + u
            live = jnp.where(k < count_ref[0], 1.0, 0.0)
            sums_ref[pl.ds(source_ref[k] % sums_ref.shape[0], 1), :] += columns[u] * live
        return carry

    for c in range(arrived.shape[0]):
        copies[c].wait()
        last = jnp.minimum((c + 1) * chunk, count_ref[0])
        lax.fori_loop(c * chunk // 8, (last + 7) // 8, group, 0)


def encode(value):
    exponent = jnp.floor(jnp.log2(jnp.maximum(value, 1e-30))) + 1.0
    mantissa = (value * jnp.exp2(24.0 - exponent) + 0.5).astype(jnp.int32)
    mantissa = jnp.minimum(mantissa, (1 << 24) - 1)
    upper = (exponent.astype(jnp.int32) + 127) * 256 + (mantissa >> 16)
    return (jnp.concatenate([upper, mantissa & 65535]) - 32768).astype(jnp.int16)


def decode(code):
    code = code.astype(jnp.int32) + 32768
    each = code.shape[0] // 2
    upper, lower = code[:each], code[each:]
    mantissa = ((upper & 255) * 65536 + lower).astype(jnp.float32)
    return mantissa * jnp.exp2(((upper >> 8) - (127 + 24)).astype(jnp.float32))


def seed_kernel(where_ref, all_ref, counts_ref, ids_ref, pages_ref, arrived):
    total, lanes = pages_ref.shape
    pages = counts_ref.shape[0]
    first = where_ref[0]
    mine = pl.ds(pl.multiple_of(where_ref[1] * lanes, lanes), lanes)
    copy = pltpu.make_async_copy(all_ref.at[mine], ids_ref, arrived)
    copy.start()
    chunk = 256
    counts_ref[...] = jnp.zeros_like(counts_ref)

    def fold(value, reduce):
        parts = [value[i : i + 8] for i in range(0, value.shape[0], 8)]
        while len(parts) > 1:
            parts = [reduce(p, q) for p, q in zip(parts[::2], parts[1::2])]
        return parts[0]

    def rows(i):
        return pl.ds(pl.multiple_of(i * chunk, chunk), chunk)

    def more(carry):
        return carry[1] < pages

    def walk(carry):
        page_now, _ = carry

        def step(i, inner):
            best, seen = inner
            page = pages_ref[rows(i), :]
            found = jnp.where(page > page_now, page, FAR)
            same = jnp.where(page == page_now, 1.0, 0.0)
            return jnp.minimum(best, fold(found, jnp.minimum)), seen + fold(same, jnp.add)

        best, seen = lax.fori_loop(0, total // chunk, step, (far, jnp.zeros((8, lanes), jnp.float32)))
        seen = jnp.sum(seen, axis=0, keepdims=True)

        def place(i, inner):
            here = lax.broadcasted_iota(jnp.int32, (chunk, lanes), 0) + i * chunk
            counts_ref[rows(i), :] += jnp.where(here == page_now, seen, 0.0)
            return inner

        lax.fori_loop(0, pages // chunk, place, 0)
        later = jnp.min(best, axis=0, keepdims=True)
        return later, jnp.min(later)

    far = jnp.full((8, lanes), FAR, jnp.int32)
    best = far
    copy.wait()
    for i in range(0, total, lanes):
        page = ids_ref[:, i : i + lanes] - first
        page = jnp.where((page >= 0) & (page < pages), page, FAR)
        page = page.astype(jnp.float32).T.astype(jnp.int32)
        pages_ref[i : i + lanes, :] = page
        best = jnp.minimum(best, fold(page, jnp.minimum))
    start = jnp.min(best, axis=0, keepdims=True)
    lax.while_loop(more, walk, (start, jnp.min(start)))


def fetch(own_ref, sib_ref, tiles, arrived):
    slots = own_ref.shape[0]
    copies = [
        pltpu.make_async_copy(own_ref, tiles.at[pl.ds(0, slots)], arrived.at[0]),
        pltpu.make_async_copy(sib_ref, tiles.at[pl.ds(slots, slots)], arrived.at[1]),
    ]
    for copy in copies:
        copy.start()
    return copies


def products(facts_refs, copies, tiles, panel, total):
    unroll = 16
    slots = tiles.shape[0] // 2
    dummy = total.shape[0] - 1
    for which, facts_ref in enumerate(facts_refs):
        copies[which].wait()
        pairs = facts_ref[3, 0]

        def group(g, carry, base=which * slots, facts_ref=facts_ref, pairs=pairs):
            for u in range(unroll):
                pair = g * unroll + u
                at = 2 * pair
                target = jnp.where(pair < pairs, facts_ref[2, at], dummy)
                left = jnp.concatenate(
                    [tiles[base + facts_ref[0, at]], tiles[base + facts_ref[0, at + 1]]], axis=1
                )
                right = jnp.concatenate(
                    [panel[facts_ref[1, at]], panel[facts_ref[1, at + 1]]], axis=0
                )
                total[target] += jnp.dot(left, right, preferred_element_type=jnp.float32)
            return carry

        lax.fori_loop(0, (pairs + unroll - 1) // unroll, group, 0)


def single_products(slot_refs, count_ref, core_ref, copies, tiles, panel, total):
    unroll = 16
    slots = tiles.shape[0] // 2
    dummy = total.shape[0] - 1
    per = 2 * BT
    band = panel.shape[0] - 1
    for which in range(2):
        copies[which].wait()
        rows_ref, cols_ref = slot_refs[2 * which : 2 * which + 2]
        owner = core_ref[0] if which == 0 else 1 - core_ref[0]

        def group(g, carry, which=which, rows_ref=rows_ref, cols_ref=cols_ref, owner=owner):
            for u in range(unroll):
                k = g * unroll + u
                target = rows_ref[k] // band * per + owner * BT + rows_ref[k] % BT
                target = jnp.where(k < count_ref[which], target, dummy)
                total[target] += jnp.dot(
                    tiles[which * slots + k],
                    panel[cols_ref[k] % band],
                    preferred_element_type=jnp.float32,
                )
            return carry

        lax.fori_loop(0, (count_ref[which] + unroll - 1) // unroll, group, 0)


def round_parts(total, out_ref):
    receivers = out_ref.shape[0]
    per = (out_ref.shape[1] - 16) // TILE

    def send(r, carry):
        exponents = []
        for t in range(per):
            block = total[r * per + t]
            top = jnp.maximum(jnp.max(block, axis=0, keepdims=True), 1e-30)
            exponent = jnp.floor(jnp.log2(top)) + 1.0
            exponents.append(exponent)
            code = block * jnp.exp2(16.0 - exponent) + 0.5
            code = jnp.clip(code.astype(jnp.int32), 0, 65535) - 32768
            out_ref[r, t * TILE : (t + 1) * TILE, :] = code.astype(jnp.int16)
        rows = exponents + [jnp.zeros((16 - per, LANES), jnp.float32)]
        tail = jnp.concatenate(rows, axis=0).astype(jnp.int32).astype(jnp.int16)
        out_ref[r, per * TILE : per * TILE + 16, :] = tail
        return carry

    lax.fori_loop(0, receivers, send, 0)


def first_kernel(pieces, far, *refs):
    slot_refs, (count_ref, core_ref, chip_ref, sums_ref, own_ref, sib_ref) = refs[:4], refs[4:10]
    piece_refs = list(refs[10 : 10 + pieces])
    out_ref, inverse_ref, panel, total, tiles, arrived, ordered, brought, near = refs[10 + pieces :]
    brings = {}
    for i in range(far):
        p = pieces - far + i
        inside = brought.at[i, pl.ds(0, piece_refs[p].shape[0])]
        brings[p] = pltpu.make_async_copy(piece_refs[p], inside, near.at[i])
        brings[p].start()
        piece_refs[p] = inside
    copies = fetch(own_ref, sib_ref, tiles, arrived)
    total[...] = jnp.zeros_like(total)
    groups, per, _ = sums_ref.shape
    ordered[...] = jnp.zeros_like(ordered)
    for p in range(pieces):
        ordered[p * per : (p + 1) * per, :] = sums_ref[chip_ref[p]]
    inverse = (1.0 / jnp.maximum(ordered[...], 1.0)).T
    for p in range(pieces):
        if p in brings:
            brings[p].wait()
        for t in range(per):
            column = inverse[:, p * per + t : p * per + t + 1]
            code = piece_refs[p][t * TILE : (t + 1) * TILE, :].astype(jnp.float32)
            score = (code + HALF) * ((HIGH - LOW) / STEPS) + LOW
            panel[chip_ref[p] * per + t] = (score * column).astype(jnp.bfloat16)
            if p == 0:
                inverse_ref[t * TILE : (t + 1) * TILE, :] = jnp.broadcast_to(column, (TILE, LANES))
    single_products(slot_refs, count_ref, core_ref, copies, tiles, panel, total)
    round_parts(total, out_ref)


def later_kernel(pieces, rows, own_facts, sib_facts, chip_ref, own_ref, sib_ref, *refs):
    piece_refs = refs[:pieces]
    out_ref, panel, total, tiles, arrived = refs[pieces:]
    copies = fetch(own_ref, sib_ref, tiles, arrived)
    total[...] = jnp.zeros_like(total)
    per = rows // TILE
    for p in range(pieces):
        for t in range(per):
            panel[chip_ref[p] * per + t] = piece_refs[p][t * TILE : (t + 1) * TILE, :]
    panel[pieces * per] = jnp.zeros((TILE, LANES), jnp.bfloat16)
    products((own_facts, sib_facts), copies, tiles, panel, total)
    round_parts(total, out_ref)


def current_kernel(scaled, parts_ref, restart_ref, inverse_ref, out_ref):
    senders = parts_ref.shape[0]
    per = (parts_ref.shape[1] - 16) // TILE
    for t in range(per):
        rows = slice(t * TILE, (t + 1) * TILE)
        summed = jnp.zeros((TILE, LANES), jnp.float32)
        for r in range(senders):
            tail = parts_ref[r, per * TILE : per * TILE + 16, :].astype(jnp.float32)
            scale = jnp.exp2(tail[t : t + 1, :] - 16.0)
            summed += (parts_ref[r, rows, :].astype(jnp.float32) + HALF) * scale
        current = damping * summed + teleport * restart_ref[rows, :]
        if scaled:
            current = current * inverse_ref[rows, :]
        out_ref[rows, :] = current.astype(out_ref.dtype)


def per_device(scores, tile_values, tile_rows, tile_cols, tile_count, seed_ids):
    grid_rows = lax.axis_size("row")
    grid_cols = lax.axis_size("col")
    row_index = lax.axis_index("row")
    col_index = lax.axis_index("col")
    depth = grid_cols // 4
    high, z, core = col_index // (2 * depth), col_index // 2 % depth, col_index % 2
    own_rows = scores.shape[0]
    columns = scores.shape[1]
    slots = tile_values.shape[0]
    seed_total = seed_ids.shape[1]
    band_tiles = grid_cols * BT
    chips = grid_cols // 2
    per = 2 * BT

    def by_col(value, move):
        pairs = []
        for c in range(grid_cols):
            y, at, k = move(c // (2 * depth), c // 2 % depth, c % 2)
            pairs.append((c, (y * depth + at) * 2 + k))
        return lax.ppermute(value, "col", pairs)

    def sibling(value):
        return by_col(value, lambda y, at, k: (y, at, 1 - k))

    def along(value, step):
        return by_col(value, lambda y, at, k: (y, (at + step) % depth, k))

    def across(value):
        return by_col(value, lambda y, at, k: (1 - y, at, k))

    tie = lax.optimization_barrier

    def gather(block, sums=None):
        rows = block.shape[0]
        a, b = along(block, 1), along(block, -1)
        if sums is None:
            other = across(block)
        else:
            other = across(jnp.concatenate([block, encode(sums)]))
            a, other = tie((a, other))
            sums = sums + decode(other[rows:])
            other = jnp.concatenate([other[:rows], encode(sums)])
        pieces, names = [block, other], [(0, 0), (1, 0)]
        c, d = other, other
        for step in range(1, depth // 2):
            if step > 1:
                a, b = along(a, 1), along(b, -1)
            c, d = along(c, 1), along(d, -1)
            pieces += [a, b, c, d]
            names += [(0, -step), (0, step), (1, -step), (1, step)]
            if sums is not None:
                sums = sums + (decode(c[rows:]) + decode(d[rows:]))
        a, d = along(a, 1), along(d, -1)
        pieces += [a, d]
        names += [(0, depth // 2), (1, depth // 2)]
        if sums is not None:
            sums = sums + decode(d[rows:])
        return pieces, names, sums

    half = columns // 2
    code = ((scores - LOW) * (STEPS / (HIGH - LOW)) + 0.5).astype(jnp.int32)
    code = (jnp.clip(code, 0, 65535) - 32768).astype(jnp.int16)
    mine = lax.dynamic_slice_in_dim(code, core * half, half, 1)
    theirs = sibling(lax.dynamic_slice_in_dim(code, (1 - core) * half, half, 1))
    block = jnp.where(
        core == 0, jnp.concatenate([mine, theirs]), jnp.concatenate([theirs, mine])
    )
    slots_here = jnp.stack([tile_rows, tile_cols, jnp.broadcast_to(tile_count, (slots,))])
    slots_there = sibling(slots_here)
    sib_tiles = sibling(tile_values)
    sums = pl.pallas_call(
        column_kernel,
        out_shape=jax.ShapeDtypeStruct((band_tiles, TILE), jnp.float32),
        in_specs=[smem(), smem(), anywhere()],
        out_specs=vmem(),
        scratch_shapes=[VMEM(tile_values.shape, tile_values.dtype), pltpu.SemaphoreType.DMA((4,))],
        compiler_params=params(8),
        name="column_sums",
    )(tile_cols, tile_count, in_hbm(tile_values))

    part = band_tiles // 2
    given = sibling(lax.dynamic_slice_in_dim(sums, (1 - core) * part, part, 0))
    sums = given + lax.dynamic_slice_in_dim(sums, core * part, part, 0)

    target_total = grid_rows * per

    def order_tiles(tile_rows, tile_cols, tile_count):
        sources = tile_cols - row_index * band_tiles
        targets = tile_rows // band_tiles * per + core * BT + tile_rows % BT
        slot_ids = jnp.arange(slots, dtype=jnp.int32)
        live = slot_ids < tile_count[0]
        target_ids = jnp.arange(target_total, dtype=jnp.int32)
        at_target = (targets[:, None] == target_ids[None, :]) & live[:, None]
        filled = (jnp.sum(at_target.astype(jnp.int32), axis=0) + 1) // 2 * 2
        before = target_ids[:, None] < target_ids[None, :]
        start = jnp.sum(jnp.where(before, filled[:, None], 0), axis=0)
        alike = (targets[:, None] == targets[None, :]) & (slot_ids[None, :] < slot_ids[:, None])
        place = jnp.sum(alike.astype(jnp.int32), axis=1)
        place = place + jnp.sum(jnp.where(at_target, start[None, :], 0), axis=1)
        long = slots + target_total
        moved = (place[:, None] == jnp.arange(long)[None, :]) & live[:, None]

        def spread(value):
            return jnp.sum(jnp.where(moved, value[:, None], 0), axis=0)

        facts = jnp.stack(
            [
                spread(slot_ids),
                spread(sources - band_tiles) + band_tiles,
                spread(targets),
                jnp.broadcast_to(jnp.sum(filled) // 2, (long,)),
            ]
        )
        return facts

    def count_seeds(seed_ids):
        first_page = (row_index * grid_cols + col_index - core) * own_rows
        return pl.pallas_call(
            seed_kernel,
            out_shape=jax.ShapeDtypeStruct((2 * own_rows, half), jnp.float32),
            in_specs=[smem(), anywhere()],
            out_specs=vmem(),
            scratch_shapes=[
                VMEM((half, seed_total), jnp.int32),
                VMEM((seed_total, half), jnp.int32),
                pltpu.SemaphoreType.DMA,
            ],
            compiler_params=params(6),
            name="seed_counts",
        )(jnp.stack([first_page, core]), seed_ids)

    def multiply(pieces, names, sums, facts):
        order = jnp.stack([(high ^ y) * depth + (z + d) % depth for y, d in names])
        n = len(pieces)
        rows = per * TILE
        parts = jax.ShapeDtypeStruct((grid_rows, rows + 16, half), jnp.int16)
        scratch = [
            VMEM((band_tiles + 1, TILE, half), jnp.bfloat16),
            VMEM((target_total + 1, TILE, half), jnp.float32),
            VMEM((2 * slots, TILE, TILE), tile_values.dtype),
            pltpu.SemaphoreType.DMA((2,)),
        ]
        tiles = (in_hbm(tile_values), in_hbm(sib_tiles))
        if sums is not None:
            far = 6
            pieces = pieces[: n - far] + [in_hbm(piece) for piece in pieces[n - far :]]
            longest = max(piece.shape[0] for piece in pieces)
            counts = jnp.concatenate([tile_count, slots_there[2, :1]])
            return pl.pallas_call(
                lambda *refs: first_kernel(n, far, *refs),
                out_shape=(parts, jax.ShapeDtypeStruct((rows, half), jnp.float32)),
                in_specs=[smem()] * 7
                + [vmem()]
                + [anywhere()] * 2
                + [vmem()] * (n - far)
                + [anywhere()] * far,
                out_specs=(vmem(), vmem()),
                scratch_shapes=scratch
                + [
                    VMEM((TILE, TILE), jnp.float32),
                    VMEM((far, longest, half), jnp.int16),
                    pltpu.SemaphoreType.DMA((far,)),
                ],
                compiler_params=params(20),
                name="first_products",
            )(
                tile_rows, tile_cols, slots_there[0], slots_there[1], counts, core.reshape(1),
                order, sums.reshape(chips, per, TILE), *tiles, *pieces,
            )
        return pl.pallas_call(
            lambda *refs: later_kernel(n, rows, *refs),
            out_shape=parts,
            in_specs=[smem()] * 3 + [anywhere()] * 2 + [vmem()] * n,
            out_specs=vmem(),
            scratch_shapes=scratch,
            compiler_params=params(20),
            name="later_products",
        )(*facts, order, *tiles, *pieces)

    def update(parts, restart, inverse, scaled):
        return pl.pallas_call(
            lambda *refs: current_kernel(scaled, *refs),
            out_shape=jax.ShapeDtypeStruct(
                (per * TILE, half), jnp.bfloat16 if scaled else jnp.float32
            ),
            in_specs=[vmem()] * 3,
            out_specs=vmem(),
            compiler_params=params(6),
            name="current",
        )(parts, restart, inverse)

    pieces, names, found = gather(block, sums)
    other = sibling(found)
    sums = jnp.where(
        core == 0, jnp.concatenate([found, other]), jnp.concatenate([other, found])
    )
    parts, inverse = multiply(pieces, names, sums, None)
    parts, raw, lists = tie((parts, (tile_rows, tile_cols, tile_count), seed_ids))
    restart = count_seeds(lists)
    facts = order_tiles(*raw)
    parts = lax.all_to_all(parts, "row", 0, 0, tiled=True)
    parts, restart, facts = tie((parts, restart, facts))
    facts = (facts, sibling(facts))
    panel = update(parts, restart, inverse, True)
    pieces, names, _ = gather(panel)
    parts = multiply(pieces, names, None, facts)
    parts = lax.all_to_all(parts, "row", 0, 0, tiled=True)
    current = update(parts, restart, inverse, False)
    mine = lax.dynamic_slice_in_dim(current, core * own_rows, own_rows, 0)
    theirs = sibling(lax.dynamic_slice_in_dim(current, (1 - core) * own_rows, own_rows, 0))
    return jnp.where(
        core == 0,
        jnp.concatenate([mine, theirs], axis=1),
        jnp.concatenate([theirs, mine], axis=1),
    )


def solution(mesh):
    placed = (
        P(("row", "col"), None),
        P(("row", "col"), None, None),
        P(("row", "col")),
        P(("row", "col")),
        P(("row", "col")),
        P(),
    )
    return jax.shard_map(
        per_device, mesh=mesh, in_specs=placed, out_specs=P(("row", "col"), None), check_vma=False
    )
```

```python
import jax
import jax.numpy as jnp
from jax import lax
from jax.experimental import pallas as pl
from jax.experimental.pallas import tpu as pltpu
from jax.sharding import PartitionSpec as P

BT = 2
TILE = 128
LANES = 128
damping = 0.85
teleport = 0.15
LOW, HIGH = 0.2, 2.0
STEPS = 65535.0
HALF = 32768.0
FAR = 1 << 30
VMEM = pltpu.VMEM
SMEM = pltpu.SMEM


def vmem(*_):
    return pl.BlockSpec(memory_space=VMEM)


def smem(*_):
    return pl.BlockSpec(memory_space=SMEM)


def anywhere(*_):
    return pl.BlockSpec(memory_space=pl.ANY)


def in_hbm(value):
    return pltpu.with_memory_space_constraint(value, pltpu.HBM)


def params(mebibytes):
    return pltpu.CompilerParams(vmem_limit_bytes=mebibytes * 1024 * 1024)


def column_kernel(source_ref, count_ref, given_ref, sums_ref, tiles_ref, arrived):
    slots = given_ref.shape[0]
    chunk = slots // arrived.shape[0]
    copies = []
    for c in range(arrived.shape[0]):
        span = pl.ds(c * chunk, chunk)
        copies.append(
            pltpu.make_async_copy(given_ref.at[span], tiles_ref.at[span], arrived.at[c])
        )
        copies[c].start()
    sums_ref[...] = jnp.zeros_like(sums_ref)

    def group(g, carry):
        columns = [
            jnp.sum(tiles_ref[8 * g + u].astype(jnp.float32), axis=0, keepdims=True) for u in range(8)
        ]
        for u in range(8):
            k = 8 * g + u
            live = jnp.where(k < count_ref[0], 1.0, 0.0)
            sums_ref[pl.ds(source_ref[k] % sums_ref.shape[0], 1), :] += columns[u] * live
        return carry

    for c in range(arrived.shape[0]):
        copies[c].wait()
        last = jnp.minimum((c + 1) * chunk, count_ref[0])
        lax.fori_loop(c * chunk // 8, (last + 7) // 8, group, 0)


def encode(value):
    exponent = jnp.floor(jnp.log2(jnp.maximum(value, 1e-30))) + 1.0
    mantissa = (value * jnp.exp2(24.0 - exponent) + 0.5).astype(jnp.int32)
    mantissa = jnp.minimum(mantissa, (1 << 24) - 1)
    upper = (exponent.astype(jnp.int32) + 127) * 256 + (mantissa >> 16)
    return (jnp.concatenate([upper, mantissa & 65535]) - 32768).astype(jnp.int16)


def decode(code):
    code = code.astype(jnp.int32) + 32768
    each = code.shape[0] // 2
    upper, lower = code[:each], code[each:]
    mantissa = ((upper & 255) * 65536 + lower).astype(jnp.float32)
    return mantissa * jnp.exp2(((upper >> 8) - (127 + 24)).astype(jnp.float32))


def seed_kernel(where_ref, all_ref, counts_ref, ids_ref, pages_ref, arrived):
    total, lanes = pages_ref.shape
    pages = counts_ref.shape[0]
    first = where_ref[0]
    mine = pl.ds(pl.multiple_of(where_ref[1] * lanes, lanes), lanes)
    copy = pltpu.make_async_copy(all_ref.at[mine], ids_ref, arrived)
    copy.start()
    chunk = 256
    counts_ref[...] = jnp.zeros_like(counts_ref)

    def fold(value, reduce):
        parts = [value[i : i + 8] for i in range(0, value.shape[0], 8)]
        while len(parts) > 1:
            parts = [reduce(p, q) for p, q in zip(parts[::2], parts[1::2])]
        return parts[0]

    def rows(i):
        return pl.ds(pl.multiple_of(i * chunk, chunk), chunk)

    def more(carry):
        return carry[1] < pages

    def walk(carry):
        page_now, _ = carry

        def step(i, inner):
            best, seen = inner
            page = pages_ref[rows(i), :]
            found = jnp.where(page > page_now, page, FAR)
            same = jnp.where(page == page_now, 1.0, 0.0)
            return jnp.minimum(best, fold(found, jnp.minimum)), seen + fold(same, jnp.add)

        best, seen = lax.fori_loop(0, total // chunk, step, (far, jnp.zeros((8, lanes), jnp.float32)))
        seen = jnp.sum(seen, axis=0, keepdims=True)

        def place(i, inner):
            here = lax.broadcasted_iota(jnp.int32, (chunk, lanes), 0) + i * chunk
            counts_ref[rows(i), :] += jnp.where(here == page_now, seen, 0.0)
            return inner

        lax.fori_loop(0, pages // chunk, place, 0)
        later = jnp.min(best, axis=0, keepdims=True)
        return later, jnp.min(later)

    far = jnp.full((8, lanes), FAR, jnp.int32)
    best = far
    copy.wait()
    for i in range(0, total, lanes):
        page = ids_ref[:, i : i + lanes] - first
        page = jnp.where((page >= 0) & (page < pages), page, FAR)
        page = page.astype(jnp.float32).T.astype(jnp.int32)
        pages_ref[i : i + lanes, :] = page
        best = jnp.minimum(best, fold(page, jnp.minimum))
    start = jnp.min(best, axis=0, keepdims=True)
    lax.while_loop(more, walk, (start, jnp.min(start)))


def fetch(own_ref, sib_ref, tiles, arrived):
    slots = own_ref.shape[0]
    copies = [
        pltpu.make_async_copy(own_ref, tiles.at[pl.ds(0, slots)], arrived.at[0]),
        pltpu.make_async_copy(sib_ref, tiles.at[pl.ds(slots, slots)], arrived.at[1]),
    ]
    for copy in copies:
        copy.start()
    return copies


def products(facts_refs, copies, tiles, panel, total):
    unroll = 16
    slots = tiles.shape[0] // 2
    dummy = total.shape[0] - 1
    for which, facts_ref in enumerate(facts_refs):
        copies[which].wait()
        pairs = facts_ref[3, 0]

        def group(g, carry, base=which * slots, facts_ref=facts_ref, pairs=pairs):
            for u in range(unroll):
                pair = g * unroll + u
                at = 2 * pair
                target = jnp.where(pair < pairs, facts_ref[2, at], dummy)
                left = jnp.concatenate(
                    [tiles[base + facts_ref[0, at]], tiles[base + facts_ref[0, at + 1]]], axis=1
                )
                right = jnp.concatenate(
                    [panel[facts_ref[1, at]], panel[facts_ref[1, at + 1]]], axis=0
                )
                total[target] += jnp.dot(left, right, preferred_element_type=jnp.float32)
            return carry

        lax.fori_loop(0, (pairs + unroll - 1) // unroll, group, 0)


def round_parts(total, out_ref):
    receivers = out_ref.shape[0]
    per = (out_ref.shape[1] - 16) // TILE

    def send(r, carry):
        exponents = []
        for t in range(per):
            block = total[r * per + t]
            top = jnp.maximum(jnp.max(block, axis=0, keepdims=True), 1e-30)
            exponent = jnp.floor(jnp.log2(top)) + 1.0
            exponents.append(exponent)
            code = block * jnp.exp2(16.0 - exponent) + 0.5
            code = jnp.clip(code.astype(jnp.int32), 0, 65535) - 32768
            out_ref[r, t * TILE : (t + 1) * TILE, :] = code.astype(jnp.int16)
        rows = exponents + [jnp.zeros((16 - per, LANES), jnp.float32)]
        tail = jnp.concatenate(rows, axis=0).astype(jnp.int32).astype(jnp.int16)
        out_ref[r, per * TILE : per * TILE + 16, :] = tail
        return carry

    lax.fori_loop(0, receivers, send, 0)


def first_kernel(pieces, far, *refs):
    own_facts, sib_facts, chip_ref, sums_ref, own_ref, sib_ref = refs[:6]
    piece_refs = list(refs[6 : 6 + pieces])
    out_ref, inverse_ref, panel, total, tiles, arrived, ordered, brought, near = refs[6 + pieces :]
    brings = {}
    for i in range(far):
        p = pieces - far + i
        inside = brought.at[i, pl.ds(0, piece_refs[p].shape[0])]
        brings[p] = pltpu.make_async_copy(piece_refs[p], inside, near.at[i])
        brings[p].start()
        piece_refs[p] = inside
    copies = fetch(own_ref, sib_ref, tiles, arrived)
    total[...] = jnp.zeros_like(total)
    groups, per, _ = sums_ref.shape
    ordered[...] = jnp.zeros_like(ordered)
    for p in range(pieces):
        ordered[p * per : (p + 1) * per, :] = sums_ref[chip_ref[p]]
    inverse = (1.0 / jnp.maximum(ordered[...], 1.0)).T
    for p in range(pieces):
        if p in brings:
            brings[p].wait()
        for t in range(per):
            column = inverse[:, p * per + t : p * per + t + 1]
            code = piece_refs[p][t * TILE : (t + 1) * TILE, :].astype(jnp.float32)
            score = (code + HALF) * ((HIGH - LOW) / STEPS) + LOW
            panel[chip_ref[p] * per + t] = (score * column).astype(jnp.bfloat16)
            if p == 0:
                inverse_ref[t * TILE : (t + 1) * TILE, :] = jnp.broadcast_to(column, (TILE, LANES))
    panel[pieces * per] = jnp.zeros((TILE, LANES), jnp.bfloat16)
    products((own_facts, sib_facts), copies, tiles, panel, total)
    round_parts(total, out_ref)


def later_kernel(pieces, rows, own_facts, sib_facts, chip_ref, own_ref, sib_ref, *refs):
    piece_refs = refs[:pieces]
    out_ref, panel, total, tiles, arrived = refs[pieces:]
    copies = fetch(own_ref, sib_ref, tiles, arrived)
    total[...] = jnp.zeros_like(total)
    per = rows // TILE
    for p in range(pieces):
        for t in range(per):
            panel[chip_ref[p] * per + t] = piece_refs[p][t * TILE : (t + 1) * TILE, :]
    panel[pieces * per] = jnp.zeros((TILE, LANES), jnp.bfloat16)
    products((own_facts, sib_facts), copies, tiles, panel, total)
    round_parts(total, out_ref)


def current_kernel(scaled, parts_ref, restart_ref, inverse_ref, out_ref):
    senders = parts_ref.shape[0]
    per = (parts_ref.shape[1] - 16) // TILE
    for t in range(per):
        rows = slice(t * TILE, (t + 1) * TILE)
        summed = jnp.zeros((TILE, LANES), jnp.float32)
        for r in range(senders):
            tail = parts_ref[r, per * TILE : per * TILE + 16, :].astype(jnp.float32)
            scale = jnp.exp2(tail[t : t + 1, :] - 16.0)
            summed += (parts_ref[r, rows, :].astype(jnp.float32) + HALF) * scale
        current = damping * summed + teleport * restart_ref[rows, :]
        if scaled:
            current = current * inverse_ref[rows, :]
        out_ref[rows, :] = current.astype(out_ref.dtype)


def per_device(scores, tile_values, tile_rows, tile_cols, tile_count, seed_ids):
    grid_rows = lax.axis_size("row")
    grid_cols = lax.axis_size("col")
    row_index = lax.axis_index("row")
    col_index = lax.axis_index("col")
    depth = grid_cols // 4
    high, z, core = col_index // (2 * depth), col_index // 2 % depth, col_index % 2
    own_rows = scores.shape[0]
    columns = scores.shape[1]
    slots = tile_values.shape[0]
    seed_total = seed_ids.shape[1]
    band_tiles = grid_cols * BT
    chips = grid_cols // 2
    per = 2 * BT

    def by_col(value, move):
        pairs = []
        for c in range(grid_cols):
            y, at, k = move(c // (2 * depth), c // 2 % depth, c % 2)
            pairs.append((c, (y * depth + at) * 2 + k))
        return lax.ppermute(value, "col", pairs)

    def sibling(value):
        return by_col(value, lambda y, at, k: (y, at, 1 - k))

    def along(value, step):
        return by_col(value, lambda y, at, k: (y, (at + step) % depth, k))

    def across(value):
        return by_col(value, lambda y, at, k: (1 - y, at, k))

    tie = lax.optimization_barrier

    def gather(block, sums=None, later=None):
        rows = block.shape[0]
        beside = None
        if sums is not None:
            block = jnp.concatenate([block, encode(sums)])
        other = across(block)
        pieces, names = [block, other], [(0, 0), (1, 0)]
        a, b, c, d = block, block, other, other
        for step in range(1, depth // 2):
            a, b = along(a, 1), along(b, -1)
            c, d = along(c, 1), along(d, -1)
            if later is not None and step == depth // 2 - 1:
                a, d, raw = tie((a, d, (tile_rows, tile_cols, tile_count)))
                beside = later(*raw)
            pieces += [a, b, c, d]
            names += [(0, -step), (0, step), (1, -step), (1, step)]
        pieces += [along(a, 1), along(d, -1)]
        names += [(0, depth // 2), (1, depth // 2)]
        if sums is not None:
            for piece in pieces[1:]:
                sums = sums + decode(piece[rows:])
        return pieces, names, sums, beside

    half = columns // 2
    code = ((scores - LOW) * (STEPS / (HIGH - LOW)) + 0.5).astype(jnp.int32)
    code = (jnp.clip(code, 0, 65535) - 32768).astype(jnp.int16)
    mine = lax.dynamic_slice_in_dim(code, core * half, half, 1)
    theirs = sibling(lax.dynamic_slice_in_dim(code, (1 - core) * half, half, 1))
    block = jnp.where(
        core == 0, jnp.concatenate([mine, theirs]), jnp.concatenate([theirs, mine])
    )
    sib_tiles = sibling(tile_values)
    sums = pl.pallas_call(
        column_kernel,
        out_shape=jax.ShapeDtypeStruct((band_tiles, TILE), jnp.float32),
        in_specs=[smem(), smem(), anywhere()],
        out_specs=vmem(),
        scratch_shapes=[VMEM(tile_values.shape, tile_values.dtype), pltpu.SemaphoreType.DMA((4,))],
        compiler_params=params(8),
        name="column_sums",
    )(tile_cols, tile_count, in_hbm(tile_values))

    part = band_tiles // 2
    given = sibling(lax.dynamic_slice_in_dim(sums, (1 - core) * part, part, 0))
    sums = given + lax.dynamic_slice_in_dim(sums, core * part, part, 0)

    target_total = grid_rows * per

    def order_tiles(tile_rows, tile_cols, tile_count):
        sources = tile_cols - row_index * band_tiles
        targets = tile_rows // band_tiles * per + core * BT + tile_rows % BT
        slot_ids = jnp.arange(slots, dtype=jnp.int32)
        live = slot_ids < tile_count[0]
        target_ids = jnp.arange(target_total, dtype=jnp.int32)
        at_target = (targets[:, None] == target_ids[None, :]) & live[:, None]
        filled = (jnp.sum(at_target.astype(jnp.int32), axis=0) + 1) // 2 * 2
        before = target_ids[:, None] < target_ids[None, :]
        start = jnp.sum(jnp.where(before, filled[:, None], 0), axis=0)
        alike = (targets[:, None] == targets[None, :]) & (slot_ids[None, :] < slot_ids[:, None])
        place = jnp.sum(alike.astype(jnp.int32), axis=1)
        place = place + jnp.sum(jnp.where(at_target, start[None, :], 0), axis=1)
        long = slots + target_total
        moved = (place[:, None] == jnp.arange(long)[None, :]) & live[:, None]

        def spread(value):
            return jnp.sum(jnp.where(moved, value[:, None], 0), axis=0)

        facts = jnp.stack(
            [
                spread(slot_ids),
                spread(sources - band_tiles) + band_tiles,
                spread(targets),
                jnp.broadcast_to(jnp.sum(filled) // 2, (long,)),
            ]
        )
        return facts

    def count_seeds(seed_ids):
        first_page = (row_index * grid_cols + col_index - core) * own_rows
        return pl.pallas_call(
            seed_kernel,
            out_shape=jax.ShapeDtypeStruct((2 * own_rows, half), jnp.float32),
            in_specs=[smem(), anywhere()],
            out_specs=vmem(),
            scratch_shapes=[
                VMEM((half, seed_total), jnp.int32),
                VMEM((seed_total, half), jnp.int32),
                pltpu.SemaphoreType.DMA,
            ],
            compiler_params=params(6),
            name="seed_counts",
        )(jnp.stack([first_page, core]), seed_ids)

    def multiply(pieces, names, sums, facts):
        order = jnp.stack([(high ^ y) * depth + (z + d) % depth for y, d in names])
        n = len(pieces)
        rows = per * TILE
        parts = jax.ShapeDtypeStruct((grid_rows, rows + 16, half), jnp.int16)
        scratch = [
            VMEM((band_tiles + 1, TILE, half), jnp.bfloat16),
            VMEM((target_total + 1, TILE, half), jnp.float32),
            VMEM((2 * slots, TILE, TILE), tile_values.dtype),
            pltpu.SemaphoreType.DMA((2,)),
        ]
        tiles = (in_hbm(tile_values), in_hbm(sib_tiles))
        if sums is not None:
            far = 6
            pieces = pieces[: n - far] + [in_hbm(piece) for piece in pieces[n - far :]]
            longest = max(piece.shape[0] for piece in pieces)
            return pl.pallas_call(
                lambda *refs: first_kernel(n, far, *refs),
                out_shape=(parts, jax.ShapeDtypeStruct((rows, half), jnp.float32)),
                in_specs=[smem()] * 3
                + [vmem()]
                + [anywhere()] * 2
                + [vmem()] * (n - far)
                + [anywhere()] * far,
                out_specs=(vmem(), vmem()),
                scratch_shapes=scratch
                + [
                    VMEM((TILE, TILE), jnp.float32),
                    VMEM((far, longest, half), jnp.int16),
                    pltpu.SemaphoreType.DMA((far,)),
                ],
                compiler_params=params(20),
                name="first_products",
            )(
                *facts, order, sums.reshape(chips, per, TILE), *tiles, *pieces
            )
        return pl.pallas_call(
            lambda *refs: later_kernel(n, rows, *refs),
            out_shape=parts,
            in_specs=[smem()] * 3 + [anywhere()] * 2 + [vmem()] * n,
            out_specs=vmem(),
            scratch_shapes=scratch,
            compiler_params=params(20),
            name="later_products",
        )(*facts, order, *tiles, *pieces)

    def update(parts, restart, inverse, scaled):
        return pl.pallas_call(
            lambda *refs: current_kernel(scaled, *refs),
            out_shape=jax.ShapeDtypeStruct(
                (per * TILE, half), jnp.bfloat16 if scaled else jnp.float32
            ),
            in_specs=[vmem()] * 3,
            out_specs=vmem(),
            compiler_params=params(6),
            name="current",
        )(parts, restart, inverse)

    pieces, names, found, facts = gather(block, sums, order_tiles)
    facts = (facts, sibling(facts))
    other = sibling(found)
    sums = jnp.where(
        core == 0, jnp.concatenate([found, other]), jnp.concatenate([other, found])
    )
    parts, inverse = multiply(pieces, names, sums, facts)
    parts, lists = tie((parts, seed_ids))
    restart = count_seeds(lists)
    parts = lax.all_to_all(parts, "row", 0, 0, tiled=True)
    panel = update(parts, restart, inverse, True)
    pieces, names, _, _ = gather(panel)
    parts = multiply(pieces, names, None, facts)
    parts = lax.all_to_all(parts, "row", 0, 0, tiled=True)
    current = update(parts, restart, inverse, False)
    mine = lax.dynamic_slice_in_dim(current, core * own_rows, own_rows, 0)
    theirs = sibling(lax.dynamic_slice_in_dim(current, (1 - core) * own_rows, own_rows, 0))
    return jnp.where(
        core == 0,
        jnp.concatenate([mine, theirs], axis=1),
        jnp.concatenate([theirs, mine], axis=1),
    )


def solution(mesh):
    placed = (
        P(("row", "col"), None),
        P(("row", "col"), None, None),
        P(("row", "col")),
        P(("row", "col")),
        P(("row", "col")),
        P(),
    )
    return jax.shard_map(
        per_device, mesh=mesh, in_specs=placed, out_specs=P(("row", "col"), None), check_vma=False
    )
```

```python
import jax
import jax.numpy as jnp
from jax import lax
from jax.experimental import pallas as pl
from jax.experimental.pallas import tpu as pltpu
from jax.sharding import PartitionSpec as P

BT = 2
TILE = 128
LANES = 128
damping = 0.85
teleport = 0.15
LOW, HIGH = 0.2, 2.0
STEPS = 65535.0
HALF = 32768.0
FAR = 1 << 30
VMEM = pltpu.VMEM
SMEM = pltpu.SMEM


def vmem(*_):
    return pl.BlockSpec(memory_space=VMEM)


def smem(*_):
    return pl.BlockSpec(memory_space=SMEM)


def anywhere(*_):
    return pl.BlockSpec(memory_space=pl.ANY)


def in_hbm(value):
    return pltpu.with_memory_space_constraint(value, pltpu.HBM)


def params(mebibytes):
    return pltpu.CompilerParams(vmem_limit_bytes=mebibytes * 1024 * 1024)


def column_kernel(source_ref, count_ref, given_ref, sums_ref, tiles_ref, arrived):
    slots = given_ref.shape[0]
    chunk = slots // arrived.shape[0]
    copies = []
    for c in range(arrived.shape[0]):
        span = pl.ds(c * chunk, chunk)
        copies.append(
            pltpu.make_async_copy(given_ref.at[span], tiles_ref.at[span], arrived.at[c])
        )
        copies[c].start()
    sums_ref[...] = jnp.zeros_like(sums_ref)

    def group(g, carry):
        columns = [
            jnp.sum(tiles_ref[8 * g + u].astype(jnp.float32), axis=0, keepdims=True) for u in range(8)
        ]
        for u in range(8):
            k = 8 * g + u
            live = jnp.where(k < count_ref[0], 1.0, 0.0)
            sums_ref[pl.ds(source_ref[k] % sums_ref.shape[0], 1), :] += columns[u] * live
        return carry

    for c in range(arrived.shape[0]):
        copies[c].wait()
        last = jnp.minimum((c + 1) * chunk, count_ref[0])
        lax.fori_loop(c * chunk // 8, (last + 7) // 8, group, 0)


def encode(value):
    exponent = jnp.floor(jnp.log2(jnp.maximum(value, 1e-30))) + 1.0
    mantissa = (value * jnp.exp2(24.0 - exponent) + 0.5).astype(jnp.int32)
    mantissa = jnp.minimum(mantissa, (1 << 24) - 1)
    upper = (exponent.astype(jnp.int32) + 127) * 256 + (mantissa >> 16)
    return (jnp.concatenate([upper, mantissa & 65535]) - 32768).astype(jnp.int16)


def decode(code):
    code = code.astype(jnp.int32) + 32768
    each = code.shape[0] // 2
    upper, lower = code[:each], code[each:]
    mantissa = ((upper & 255) * 65536 + lower).astype(jnp.float32)
    return mantissa * jnp.exp2(((upper >> 8) - (127 + 24)).astype(jnp.float32))


def seed_kernel(where_ref, all_ref, counts_ref, ids_ref, pages_ref, arrived):
    total, lanes = pages_ref.shape
    pages = counts_ref.shape[0]
    first = where_ref[0]
    mine = pl.ds(pl.multiple_of(where_ref[1] * lanes, lanes), lanes)
    copy = pltpu.make_async_copy(all_ref.at[mine], ids_ref, arrived)
    copy.start()
    chunk = 256
    counts_ref[...] = jnp.zeros_like(counts_ref)

    def fold(value, reduce):
        parts = [value[i : i + 8] for i in range(0, value.shape[0], 8)]
        while len(parts) > 1:
            parts = [reduce(p, q) for p, q in zip(parts[::2], parts[1::2])]
        return parts[0]

    def rows(i):
        return pl.ds(pl.multiple_of(i * chunk, chunk), chunk)

    def more(carry):
        return carry[1] < pages

    def walk(carry):
        page_now, _ = carry

        def step(i, inner):
            best, seen = inner
            page = pages_ref[rows(i), :]
            found = jnp.where(page > page_now, page, FAR)
            same = jnp.where(page == page_now, 1.0, 0.0)
            return jnp.minimum(best, fold(found, jnp.minimum)), seen + fold(same, jnp.add)

        best, seen = lax.fori_loop(0, total // chunk, step, (far, jnp.zeros((8, lanes), jnp.float32)))
        seen = jnp.sum(seen, axis=0, keepdims=True)

        def place(i, inner):
            here = lax.broadcasted_iota(jnp.int32, (chunk, lanes), 0) + i * chunk
            counts_ref[rows(i), :] += jnp.where(here == page_now, seen, 0.0)
            return inner

        lax.fori_loop(0, pages // chunk, place, 0)
        later = jnp.min(best, axis=0, keepdims=True)
        return later, jnp.min(later)

    far = jnp.full((8, lanes), FAR, jnp.int32)
    best = far
    copy.wait()
    for i in range(0, total, lanes):
        page = ids_ref[:, i : i + lanes] - first
        page = jnp.where((page >= 0) & (page < pages), page, FAR)
        page = page.astype(jnp.float32).T.astype(jnp.int32)
        pages_ref[i : i + lanes, :] = page
        best = jnp.minimum(best, fold(page, jnp.minimum))
    start = jnp.min(best, axis=0, keepdims=True)
    lax.while_loop(more, walk, (start, jnp.min(start)))


def fetch(own_ref, sib_ref, tiles, arrived):
    slots = own_ref.shape[0]
    copies = [
        pltpu.make_async_copy(own_ref, tiles.at[pl.ds(0, slots)], arrived.at[0]),
        pltpu.make_async_copy(sib_ref, tiles.at[pl.ds(slots, slots)], arrived.at[1]),
    ]
    for copy in copies:
        copy.start()
    return copies


def products(facts_refs, copies, tiles, panel, total):
    unroll = 16
    slots = tiles.shape[0] // 2
    dummy = total.shape[0] - 1
    for which, facts_ref in enumerate(facts_refs):
        copies[which].wait()
        pairs = facts_ref[3, 0]

        def group(g, carry, base=which * slots, facts_ref=facts_ref, pairs=pairs):
            for u in range(unroll):
                pair = g * unroll + u
                at = 2 * pair
                target = jnp.where(pair < pairs, facts_ref[2, at], dummy)
                left = jnp.concatenate(
                    [tiles[base + facts_ref[0, at]], tiles[base + facts_ref[0, at + 1]]], axis=1
                )
                right = jnp.concatenate(
                    [panel[facts_ref[1, at]], panel[facts_ref[1, at + 1]]], axis=0
                )
                total[target] += jnp.dot(left, right, preferred_element_type=jnp.float32)
            return carry

        lax.fori_loop(0, (pairs + unroll - 1) // unroll, group, 0)


def single_products(slot_refs, count_ref, core_ref, copies, tiles, panel, total):
    unroll = 24
    slots = tiles.shape[0] // 2
    dummy = total.shape[0] - 1
    per = 2 * BT
    band = panel.shape[0] - 1
    for which in range(2):
        copies[which].wait()
        rows_ref, cols_ref = slot_refs[2 * which : 2 * which + 2]
        owner = core_ref[0] if which == 0 else 1 - core_ref[0]

        def group(g, carry, which=which, rows_ref=rows_ref, cols_ref=cols_ref, owner=owner):
            for u in range(unroll):
                k = g * unroll + u
                target = rows_ref[k] // band * per + owner * BT + rows_ref[k] % BT
                target = jnp.where(k < count_ref[which], target, dummy)
                total[target] += jnp.dot(
                    tiles[which * slots + k],
                    panel[cols_ref[k] % band],
                    preferred_element_type=jnp.float32,
                )
            return carry

        lax.fori_loop(0, (count_ref[which] + unroll - 1) // unroll, group, 0)


def round_parts(total, out_ref):
    receivers = out_ref.shape[0]
    per = (out_ref.shape[1] - 16) // TILE

    def send(r, carry):
        exponents = []
        for t in range(per):
            block = total[r * per + t]
            top = jnp.maximum(jnp.max(block, axis=0, keepdims=True), 1e-30)
            exponent = jnp.floor(jnp.log2(top)) + 1.0
            exponents.append(exponent)
            code = block * jnp.exp2(16.0 - exponent) + 0.5
            code = jnp.clip(code.astype(jnp.int32), 0, 65535) - 32768
            out_ref[r, t * TILE : (t + 1) * TILE, :] = code.astype(jnp.int16)
        rows = exponents + [jnp.zeros((16 - per, LANES), jnp.float32)]
        tail = jnp.concatenate(rows, axis=0).astype(jnp.int32).astype(jnp.int16)
        out_ref[r, per * TILE : per * TILE + 16, :] = tail
        return carry

    lax.fori_loop(0, receivers, send, 0)


def first_kernel(pieces, far, *refs):
    slot_refs, (count_ref, core_ref, chip_ref, sums_ref, own_ref, sib_ref) = refs[:4], refs[4:10]
    piece_refs = list(refs[10 : 10 + pieces])
    out_ref, inverse_ref, panel, total, tiles, arrived, ordered, brought, near = refs[10 + pieces :]
    brings = {}
    for i in range(far):
        p = pieces - far + i
        inside = brought.at[i, pl.ds(0, piece_refs[p].shape[0])]
        brings[p] = pltpu.make_async_copy(piece_refs[p], inside, near.at[i])
        brings[p].start()
        piece_refs[p] = inside
    copies = fetch(own_ref, sib_ref, tiles, arrived)
    total[...] = jnp.zeros_like(total)
    groups, per, _ = sums_ref.shape
    ordered[...] = jnp.zeros_like(ordered)
    for p in range(pieces):
        ordered[p * per : (p + 1) * per, :] = sums_ref[chip_ref[p]]
    inverse = (1.0 / jnp.maximum(ordered[...], 1.0)).T
    for p in range(pieces):
        if p in brings:
            brings[p].wait()
        for t in range(per):
            column = inverse[:, p * per + t : p * per + t + 1]
            code = piece_refs[p][t * TILE : (t + 1) * TILE, :].astype(jnp.float32)
            score = (code + HALF) * ((HIGH - LOW) / STEPS) + LOW
            panel[chip_ref[p] * per + t] = (score * column).astype(jnp.bfloat16)
            if p == 0:
                inverse_ref[t * TILE : (t + 1) * TILE, :] = jnp.broadcast_to(column, (TILE, LANES))
    single_products(slot_refs, count_ref, core_ref, copies, tiles, panel, total)
    round_parts(total, out_ref)


def later_kernel(pieces, rows, own_facts, sib_facts, chip_ref, own_ref, sib_ref, *refs):
    piece_refs = refs[:pieces]
    out_ref, panel, total, tiles, arrived = refs[pieces:]
    copies = fetch(own_ref, sib_ref, tiles, arrived)
    total[...] = jnp.zeros_like(total)
    per = rows // TILE
    for p in range(pieces):
        for t in range(per):
            panel[chip_ref[p] * per + t] = piece_refs[p][t * TILE : (t + 1) * TILE, :]
    panel[pieces * per] = jnp.zeros((TILE, LANES), jnp.bfloat16)
    products((own_facts, sib_facts), copies, tiles, panel, total)
    round_parts(total, out_ref)


def current_kernel(scaled, parts_ref, restart_ref, inverse_ref, out_ref):
    senders = parts_ref.shape[0]
    per = (parts_ref.shape[1] - 16) // TILE
    for t in range(per):
        rows = slice(t * TILE, (t + 1) * TILE)
        summed = jnp.zeros((TILE, LANES), jnp.float32)
        for r in range(senders):
            tail = parts_ref[r, per * TILE : per * TILE + 16, :].astype(jnp.float32)
            scale = jnp.exp2(tail[t : t + 1, :] - 16.0)
            summed += (parts_ref[r, rows, :].astype(jnp.float32) + HALF) * scale
        current = damping * summed + teleport * restart_ref[rows, :]
        if scaled:
            current = current * inverse_ref[rows, :]
        out_ref[rows, :] = current.astype(out_ref.dtype)


def per_device(scores, tile_values, tile_rows, tile_cols, tile_count, seed_ids):
    grid_rows = lax.axis_size("row")
    grid_cols = lax.axis_size("col")
    row_index = lax.axis_index("row")
    col_index = lax.axis_index("col")
    depth = grid_cols // 4
    high, z, core = col_index // (2 * depth), col_index // 2 % depth, col_index % 2
    own_rows = scores.shape[0]
    columns = scores.shape[1]
    slots = tile_values.shape[0]
    seed_total = seed_ids.shape[1]
    band_tiles = grid_cols * BT
    chips = grid_cols // 2
    per = 2 * BT

    def by_col(value, move):
        pairs = []
        for c in range(grid_cols):
            y, at, k = move(c // (2 * depth), c // 2 % depth, c % 2)
            pairs.append((c, (y * depth + at) * 2 + k))
        return lax.ppermute(value, "col", pairs)

    def sibling(value):
        return by_col(value, lambda y, at, k: (y, at, 1 - k))

    def along(value, step):
        return by_col(value, lambda y, at, k: (y, (at + step) % depth, k))

    def across(value):
        return by_col(value, lambda y, at, k: (1 - y, at, k))

    tie = lax.optimization_barrier

    def gather(block, sums=None):
        rows = block.shape[0]
        if sums is not None:
            block = jnp.concatenate([block, encode(sums)])
        other = across(block)
        pieces, names = [block, other], [(0, 0), (1, 0)]
        a, b, c, d = block, block, other, other
        for step in range(1, depth // 2):
            a, b = along(a, 1), along(b, -1)
            c, d = along(c, 1), along(d, -1)
            pieces += [a, b, c, d]
            names += [(0, -step), (0, step), (1, -step), (1, step)]
        pieces += [along(a, 1), along(d, -1)]
        names += [(0, depth // 2), (1, depth // 2)]
        if sums is not None:
            for piece in pieces[1:]:
                sums = sums + decode(piece[rows:])
        return pieces, names, sums

    half = columns // 2
    code = ((scores - LOW) * (STEPS / (HIGH - LOW)) + 0.5).astype(jnp.int32)
    code = (jnp.clip(code, 0, 65535) - 32768).astype(jnp.int16)
    mine = lax.dynamic_slice_in_dim(code, core * half, half, 1)
    theirs = sibling(lax.dynamic_slice_in_dim(code, (1 - core) * half, half, 1))
    block = jnp.where(
        core == 0, jnp.concatenate([mine, theirs]), jnp.concatenate([theirs, mine])
    )
    slots_here = jnp.stack([tile_rows, tile_cols, jnp.broadcast_to(tile_count, (slots,))])
    slots_there = sibling(slots_here)
    sib_tiles = sibling(tile_values)
    sums = pl.pallas_call(
        column_kernel,
        out_shape=jax.ShapeDtypeStruct((band_tiles, TILE), jnp.float32),
        in_specs=[smem(), smem(), anywhere()],
        out_specs=vmem(),
        scratch_shapes=[VMEM(tile_values.shape, tile_values.dtype), pltpu.SemaphoreType.DMA((4,))],
        compiler_params=params(8),
        name="column_sums",
    )(tile_cols, tile_count, in_hbm(tile_values))

    part = band_tiles // 2
    given = sibling(lax.dynamic_slice_in_dim(sums, (1 - core) * part, part, 0))
    sums = given + lax.dynamic_slice_in_dim(sums, core * part, part, 0)

    target_total = grid_rows * per

    def order_tiles(tile_rows, tile_cols, tile_count):
        sources = tile_cols - row_index * band_tiles
        targets = tile_rows // band_tiles * per + core * BT + tile_rows % BT
        slot_ids = jnp.arange(slots, dtype=jnp.int32)
        live = slot_ids < tile_count[0]
        target_ids = jnp.arange(target_total, dtype=jnp.int32)
        at_target = (targets[:, None] == target_ids[None, :]) & live[:, None]
        filled = (jnp.sum(at_target.astype(jnp.int32), axis=0) + 1) // 2 * 2
        before = target_ids[:, None] < target_ids[None, :]
        start = jnp.sum(jnp.where(before, filled[:, None], 0), axis=0)
        alike = (targets[:, None] == targets[None, :]) & (slot_ids[None, :] < slot_ids[:, None])
        place = jnp.sum(alike.astype(jnp.int32), axis=1)
        place = place + jnp.sum(jnp.where(at_target, start[None, :], 0), axis=1)
        long = slots + target_total
        moved = (place[:, None] == jnp.arange(long)[None, :]) & live[:, None]

        def spread(value):
            return jnp.sum(jnp.where(moved, value[:, None], 0), axis=0)

        facts = jnp.stack(
            [
                spread(slot_ids),
                spread(sources - band_tiles) + band_tiles,
                spread(targets),
                jnp.broadcast_to(jnp.sum(filled) // 2, (long,)),
            ]
        )
        return facts

    def count_seeds(seed_ids):
        first_page = (row_index * grid_cols + col_index - core) * own_rows
        return pl.pallas_call(
            seed_kernel,
            out_shape=jax.ShapeDtypeStruct((2 * own_rows, half), jnp.float32),
            in_specs=[smem(), anywhere()],
            out_specs=vmem(),
            scratch_shapes=[
                VMEM((half, seed_total), jnp.int32),
                VMEM((seed_total, half), jnp.int32),
                pltpu.SemaphoreType.DMA,
            ],
            compiler_params=params(6),
            name="seed_counts",
        )(jnp.stack([first_page, core]), seed_ids)

    def multiply(pieces, names, sums, facts):
        order = jnp.stack([(high ^ y) * depth + (z + d) % depth for y, d in names])
        n = len(pieces)
        rows = per * TILE
        parts = jax.ShapeDtypeStruct((grid_rows, rows + 16, half), jnp.int16)
        scratch = [
            VMEM((band_tiles + 1, TILE, half), jnp.bfloat16),
            VMEM((target_total + 1, TILE, half), jnp.float32),
            VMEM((2 * slots, TILE, TILE), tile_values.dtype),
            pltpu.SemaphoreType.DMA((2,)),
        ]
        tiles = (in_hbm(tile_values), in_hbm(sib_tiles))
        if sums is not None:
            far = 6
            pieces = pieces[: n - far] + [in_hbm(piece) for piece in pieces[n - far :]]
            longest = max(piece.shape[0] for piece in pieces)
            counts = jnp.concatenate([tile_count, slots_there[2, :1]])
            return pl.pallas_call(
                lambda *refs: first_kernel(n, far, *refs),
                out_shape=(parts, jax.ShapeDtypeStruct((rows, half), jnp.float32)),
                in_specs=[smem()] * 7
                + [vmem()]
                + [anywhere()] * 2
                + [vmem()] * (n - far)
                + [anywhere()] * far,
                out_specs=(vmem(), vmem()),
                scratch_shapes=scratch
                + [
                    VMEM((TILE, TILE), jnp.float32),
                    VMEM((far, longest, half), jnp.int16),
                    pltpu.SemaphoreType.DMA((far,)),
                ],
                compiler_params=params(20),
                name="first_products",
            )(
                tile_rows, tile_cols, slots_there[0], slots_there[1], counts, core.reshape(1),
                order, sums.reshape(chips, per, TILE), *tiles, *pieces,
            )
        return pl.pallas_call(
            lambda *refs: later_kernel(n, rows, *refs),
            out_shape=parts,
            in_specs=[smem()] * 3 + [anywhere()] * 2 + [vmem()] * n,
            out_specs=vmem(),
            scratch_shapes=scratch,
            compiler_params=params(20),
            name="later_products",
        )(*facts, order, *tiles, *pieces)

    def update(parts, restart, inverse, scaled):
        return pl.pallas_call(
            lambda *refs: current_kernel(scaled, *refs),
            out_shape=jax.ShapeDtypeStruct(
                (per * TILE, half), jnp.bfloat16 if scaled else jnp.float32
            ),
            in_specs=[vmem()] * 3,
            out_specs=vmem(),
            compiler_params=params(6),
            name="current",
        )(parts, restart, inverse)

    pieces, names, found = gather(block, sums)
    other = sibling(found)
    sums = jnp.where(
        core == 0, jnp.concatenate([found, other]), jnp.concatenate([other, found])
    )
    parts, inverse = multiply(pieces, names, sums, None)
    parts, raw, lists = tie((parts, (tile_rows, tile_cols, tile_count), seed_ids))
    restart = count_seeds(lists)
    facts = order_tiles(*raw)
    parts = lax.all_to_all(parts, "row", 0, 0, tiled=True)
    parts, restart, facts = tie((parts, restart, facts))
    facts = (facts, sibling(facts))
    panel = update(parts, restart, inverse, True)
    pieces, names, _ = gather(panel)
    parts = multiply(pieces, names, None, facts)
    parts = lax.all_to_all(parts, "row", 0, 0, tiled=True)
    current = update(parts, restart, inverse, False)
    mine = lax.dynamic_slice_in_dim(current, core * own_rows, own_rows, 0)
    theirs = sibling(lax.dynamic_slice_in_dim(current, (1 - core) * own_rows, own_rows, 0))
    return jnp.where(
        core == 0,
        jnp.concatenate([mine, theirs], axis=1),
        jnp.concatenate([theirs, mine], axis=1),
    )


def solution(mesh):
    placed = (
        P(("row", "col"), None),
        P(("row", "col"), None, None),
        P(("row", "col")),
        P(("row", "col")),
        P(("row", "col")),
        P(),
    )
    return jax.shard_map(
        per_device, mesh=mesh, in_specs=placed, out_specs=P(("row", "col"), None), check_vma=False
    )
```

```python
import jax
import jax.numpy as jnp
from jax import lax
from jax.experimental import pallas as pl
from jax.experimental.pallas import tpu as pltpu
from jax.sharding import PartitionSpec as P

BT = 2
TILE = 128
LANES = 128
damping = 0.85
teleport = 0.15
LOW, HIGH = 0.2, 2.0
STEPS = 65535.0
HALF = 32768.0
FAR = 1 << 30
VMEM = pltpu.VMEM
SMEM = pltpu.SMEM


def vmem(*_):
    return pl.BlockSpec(memory_space=VMEM)


def smem(*_):
    return pl.BlockSpec(memory_space=SMEM)


def anywhere(*_):
    return pl.BlockSpec(memory_space=pl.ANY)


def in_hbm(value):
    return pltpu.with_memory_space_constraint(value, pltpu.HBM)


def params(mebibytes):
    return pltpu.CompilerParams(vmem_limit_bytes=mebibytes * 1024 * 1024)


def column_kernel(source_ref, count_ref, given_ref, sums_ref, tiles_ref, arrived):
    slots = given_ref.shape[0]
    chunk = slots // arrived.shape[0]
    copies = []
    for c in range(arrived.shape[0]):
        span = pl.ds(c * chunk, chunk)
        copies.append(
            pltpu.make_async_copy(given_ref.at[span], tiles_ref.at[span], arrived.at[c])
        )
        copies[c].start()
    sums_ref[...] = jnp.zeros_like(sums_ref)

    def group(g, carry):
        columns = [
            jnp.sum(tiles_ref[8 * g + u].astype(jnp.float32), axis=0, keepdims=True) for u in range(8)
        ]
        for u in range(8):
            k = 8 * g + u
            live = jnp.where(k < count_ref[0], 1.0, 0.0)
            sums_ref[pl.ds(source_ref[k] % sums_ref.shape[0], 1), :] += columns[u] * live
        return carry

    for c in range(arrived.shape[0]):
        copies[c].wait()
        last = jnp.minimum((c + 1) * chunk, count_ref[0])
        lax.fori_loop(c * chunk // 8, (last + 7) // 8, group, 0)


def encode(value):
    exponent = jnp.floor(jnp.log2(jnp.maximum(value, 1e-30))) + 1.0
    mantissa = (value * jnp.exp2(24.0 - exponent) + 0.5).astype(jnp.int32)
    mantissa = jnp.minimum(mantissa, (1 << 24) - 1)
    upper = (exponent.astype(jnp.int32) + 127) * 256 + (mantissa >> 16)
    return (jnp.concatenate([upper, mantissa & 65535]) - 32768).astype(jnp.int16)


def decode(code):
    code = code.astype(jnp.int32) + 32768
    each = code.shape[0] // 2
    upper, lower = code[:each], code[each:]
    mantissa = ((upper & 255) * 65536 + lower).astype(jnp.float32)
    return mantissa * jnp.exp2(((upper >> 8) - (127 + 24)).astype(jnp.float32))


def seed_kernel(where_ref, all_ref, counts_ref, ids_ref, pages_ref, arrived):
    total, lanes = pages_ref.shape
    pages = counts_ref.shape[0]
    first = where_ref[0]
    mine = pl.ds(pl.multiple_of(where_ref[1] * lanes, lanes), lanes)
    copy = pltpu.make_async_copy(all_ref.at[mine], ids_ref, arrived)
    copy.start()
    chunk = 256
    counts_ref[...] = jnp.zeros_like(counts_ref)

    def fold(value, reduce):
        parts = [value[i : i + 8] for i in range(0, value.shape[0], 8)]
        while len(parts) > 1:
            parts = [reduce(p, q) for p, q in zip(parts[::2], parts[1::2])]
        return parts[0]

    def rows(i):
        return pl.ds(pl.multiple_of(i * chunk, chunk), chunk)

    def more(carry):
        return carry[1] < pages

    def walk(carry):
        page_now, _ = carry

        def step(i, inner):
            best, seen = inner
            page = pages_ref[rows(i), :]
            found = jnp.where(page > page_now, page, FAR)
            same = jnp.where(page == page_now, 1.0, 0.0)
            return jnp.minimum(best, fold(found, jnp.minimum)), seen + fold(same, jnp.add)

        best, seen = lax.fori_loop(0, total // chunk, step, (far, jnp.zeros((8, lanes), jnp.float32)))
        seen = jnp.sum(seen, axis=0, keepdims=True)

        def place(i, inner):
            here = lax.broadcasted_iota(jnp.int32, (chunk, lanes), 0) + i * chunk
            counts_ref[rows(i), :] += jnp.where(here == page_now, seen, 0.0)
            return inner

        lax.fori_loop(0, pages // chunk, place, 0)
        later = jnp.min(best, axis=0, keepdims=True)
        return later, jnp.min(later)

    far = jnp.full((8, lanes), FAR, jnp.int32)
    best = far
    copy.wait()
    for i in range(0, total, lanes):
        page = ids_ref[:, i : i + lanes] - first
        page = jnp.where((page >= 0) & (page < pages), page, FAR)
        page = page.astype(jnp.float32).T.astype(jnp.int32)
        pages_ref[i : i + lanes, :] = page
        best = jnp.minimum(best, fold(page, jnp.minimum))
    start = jnp.min(best, axis=0, keepdims=True)
    lax.while_loop(more, walk, (start, jnp.min(start)))


def fetch(own_ref, sib_ref, tiles, arrived):
    slots = own_ref.shape[0]
    copies = [
        pltpu.make_async_copy(own_ref, tiles.at[pl.ds(0, slots)], arrived.at[0]),
        pltpu.make_async_copy(sib_ref, tiles.at[pl.ds(slots, slots)], arrived.at[1]),
    ]
    for copy in copies:
        copy.start()
    return copies


def single_products(slot_refs, count_ref, core_ref, copies, tiles, panel, total):
    unroll = 24
    slots = tiles.shape[0] // 2
    dummy = total.shape[0] - 1
    per = 2 * BT
    band = panel.shape[0] - 1
    for which in range(2):
        copies[which].wait()
        rows_ref, cols_ref = slot_refs[2 * which : 2 * which + 2]
        owner = core_ref[0] if which == 0 else 1 - core_ref[0]

        def group(g, carry, which=which, rows_ref=rows_ref, cols_ref=cols_ref, owner=owner):
            for u in range(unroll):
                k = g * unroll + u
                target = rows_ref[k] // band * per + owner * BT + rows_ref[k] % BT
                target = jnp.where(k < count_ref[which], target, dummy)
                total[target] += jnp.dot(
                    tiles[which * slots + k],
                    panel[cols_ref[k] % band],
                    preferred_element_type=jnp.float32,
                )
            return carry

        lax.fori_loop(0, (count_ref[which] + unroll - 1) // unroll, group, 0)


def round_parts(total, out_ref):
    receivers = out_ref.shape[0]
    per = (out_ref.shape[1] - 16) // TILE

    def send(r, carry):
        exponents = []
        for t in range(per):
            block = total[r * per + t]
            top = jnp.maximum(jnp.max(block, axis=0, keepdims=True), 1e-30)
            exponent = jnp.floor(jnp.log2(top)) + 1.0
            exponents.append(exponent)
            code = block * jnp.exp2(16.0 - exponent) + 0.5
            code = jnp.clip(code.astype(jnp.int32), 0, 65535) - 32768
            out_ref[r, t * TILE : (t + 1) * TILE, :] = code.astype(jnp.int16)
        rows = exponents + [jnp.zeros((16 - per, LANES), jnp.float32)]
        tail = jnp.concatenate(rows, axis=0).astype(jnp.int32).astype(jnp.int16)
        out_ref[r, per * TILE : per * TILE + 16, :] = tail
        return carry

    lax.fori_loop(0, receivers, send, 0)


def first_kernel(pieces, far, *refs):
    slot_refs, (count_ref, core_ref, chip_ref, sums_ref, own_ref, sib_ref) = refs[:4], refs[4:10]
    piece_refs = list(refs[10 : 10 + pieces])
    out_ref, inverse_ref, panel, total, tiles, arrived, ordered, brought, near = refs[10 + pieces :]
    brings = {}
    for i in range(far):
        p = pieces - far + i
        inside = brought.at[i, pl.ds(0, piece_refs[p].shape[0])]
        brings[p] = pltpu.make_async_copy(piece_refs[p], inside, near.at[i])
        brings[p].start()
        piece_refs[p] = inside
    copies = fetch(own_ref, sib_ref, tiles, arrived)
    total[...] = jnp.zeros_like(total)
    groups, per, _ = sums_ref.shape
    ordered[...] = jnp.zeros_like(ordered)
    for p in range(pieces):
        ordered[p * per : (p + 1) * per, :] = sums_ref[chip_ref[p]]
    inverse = (1.0 / jnp.maximum(ordered[...], 1.0)).T
    for p in range(pieces):
        if p in brings:
            brings[p].wait()
        for t in range(per):
            column = inverse[:, p * per + t : p * per + t + 1]
            code = piece_refs[p][t * TILE : (t + 1) * TILE, :].astype(jnp.float32)
            score = (code + HALF) * ((HIGH - LOW) / STEPS) + LOW
            panel[chip_ref[p] * per + t] = (score * column).astype(jnp.bfloat16)
            if p == 0:
                inverse_ref[t * TILE : (t + 1) * TILE, :] = jnp.broadcast_to(column, (TILE, LANES))
    single_products(slot_refs, count_ref, core_ref, copies, tiles, panel, total)
    round_parts(total, out_ref)


def later_kernel(pieces, rows, *refs):
    slot_refs, (count_ref, core_ref, chip_ref, own_ref, sib_ref) = refs[:4], refs[4:9]
    piece_refs = refs[9 : 9 + pieces]
    out_ref, panel, total, tiles, arrived = refs[9 + pieces :]
    copies = fetch(own_ref, sib_ref, tiles, arrived)
    total[...] = jnp.zeros_like(total)
    per = rows // TILE
    for p in range(pieces):
        for t in range(per):
            panel[chip_ref[p] * per + t] = piece_refs[p][t * TILE : (t + 1) * TILE, :]
    single_products(slot_refs, count_ref, core_ref, copies, tiles, panel, total)
    round_parts(total, out_ref)


def current_kernel(scaled, parts_ref, restart_ref, inverse_ref, out_ref):
    senders = parts_ref.shape[0]
    per = (parts_ref.shape[1] - 16) // TILE
    for t in range(per):
        rows = slice(t * TILE, (t + 1) * TILE)
        summed = jnp.zeros((TILE, LANES), jnp.float32)
        for r in range(senders):
            tail = parts_ref[r, per * TILE : per * TILE + 16, :].astype(jnp.float32)
            scale = jnp.exp2(tail[t : t + 1, :] - 16.0)
            summed += (parts_ref[r, rows, :].astype(jnp.float32) + HALF) * scale
        current = damping * summed + teleport * restart_ref[rows, :]
        if scaled:
            current = current * inverse_ref[rows, :]
        out_ref[rows, :] = current.astype(out_ref.dtype)


def per_device(scores, tile_values, tile_rows, tile_cols, tile_count, seed_ids):
    grid_rows = lax.axis_size("row")
    grid_cols = lax.axis_size("col")
    row_index = lax.axis_index("row")
    col_index = lax.axis_index("col")
    depth = grid_cols // 4
    high, z, core = col_index // (2 * depth), col_index // 2 % depth, col_index % 2
    own_rows = scores.shape[0]
    columns = scores.shape[1]
    slots = tile_values.shape[0]
    seed_total = seed_ids.shape[1]
    band_tiles = grid_cols * BT
    chips = grid_cols // 2
    per = 2 * BT

    def by_col(value, move):
        pairs = []
        for c in range(grid_cols):
            y, at, k = move(c // (2 * depth), c // 2 % depth, c % 2)
            pairs.append((c, (y * depth + at) * 2 + k))
        return lax.ppermute(value, "col", pairs)

    def sibling(value):
        return by_col(value, lambda y, at, k: (y, at, 1 - k))

    def along(value, step):
        return by_col(value, lambda y, at, k: (y, (at + step) % depth, k))

    def across(value):
        return by_col(value, lambda y, at, k: (1 - y, at, k))

    tie = lax.optimization_barrier

    def gather(block, sums=None):
        rows = block.shape[0]
        if sums is not None:
            block = jnp.concatenate([block, encode(sums)])
        other = across(block)
        pieces, names = [block, other], [(0, 0), (1, 0)]
        a, b, c, d = block, block, other, other
        for step in range(1, depth // 2):
            a, b = along(a, 1), along(b, -1)
            c, d = along(c, 1), along(d, -1)
            pieces += [a, b, c, d]
            names += [(0, -step), (0, step), (1, -step), (1, step)]
        pieces += [along(a, 1), along(d, -1)]
        names += [(0, depth // 2), (1, depth // 2)]
        if sums is not None:
            for piece in pieces[1:]:
                sums = sums + decode(piece[rows:])
        return pieces, names, sums

    half = columns // 2
    code = ((scores - LOW) * (STEPS / (HIGH - LOW)) + 0.5).astype(jnp.int32)
    code = (jnp.clip(code, 0, 65535) - 32768).astype(jnp.int16)
    mine = lax.dynamic_slice_in_dim(code, core * half, half, 1)
    theirs = sibling(lax.dynamic_slice_in_dim(code, (1 - core) * half, half, 1))
    block = jnp.where(
        core == 0, jnp.concatenate([mine, theirs]), jnp.concatenate([theirs, mine])
    )
    slots_here = jnp.stack([tile_rows, tile_cols, jnp.broadcast_to(tile_count, (slots,))])
    slots_there = sibling(slots_here)
    sib_tiles = sibling(tile_values)
    sums = pl.pallas_call(
        column_kernel,
        out_shape=jax.ShapeDtypeStruct((band_tiles, TILE), jnp.float32),
        in_specs=[smem(), smem(), anywhere()],
        out_specs=vmem(),
        scratch_shapes=[VMEM(tile_values.shape, tile_values.dtype), pltpu.SemaphoreType.DMA((4,))],
        compiler_params=params(8),
        name="column_sums",
    )(tile_cols, tile_count, in_hbm(tile_values))

    part = band_tiles // 2
    given = sibling(lax.dynamic_slice_in_dim(sums, (1 - core) * part, part, 0))
    sums = given + lax.dynamic_slice_in_dim(sums, core * part, part, 0)

    target_total = grid_rows * per

    def count_seeds(seed_ids):
        first_page = (row_index * grid_cols + col_index - core) * own_rows
        return pl.pallas_call(
            seed_kernel,
            out_shape=jax.ShapeDtypeStruct((2 * own_rows, half), jnp.float32),
            in_specs=[smem(), anywhere()],
            out_specs=vmem(),
            scratch_shapes=[
                VMEM((half, seed_total), jnp.int32),
                VMEM((seed_total, half), jnp.int32),
                pltpu.SemaphoreType.DMA,
            ],
            compiler_params=params(6),
            name="seed_counts",
        )(jnp.stack([first_page, core]), seed_ids)

    def multiply(pieces, names, sums):
        order = jnp.stack([(high ^ y) * depth + (z + d) % depth for y, d in names])
        n = len(pieces)
        rows = per * TILE
        parts = jax.ShapeDtypeStruct((grid_rows, rows + 16, half), jnp.int16)
        scratch = [
            VMEM((band_tiles + 1, TILE, half), jnp.bfloat16),
            VMEM((target_total + 1, TILE, half), jnp.float32),
            VMEM((2 * slots, TILE, TILE), tile_values.dtype),
            pltpu.SemaphoreType.DMA((2,)),
        ]
        tiles = (in_hbm(tile_values), in_hbm(sib_tiles))
        counts = jnp.concatenate([tile_count, slots_there[2, :1]])
        where = (tile_rows, tile_cols, slots_there[0], slots_there[1], counts, core.reshape(1), order)
        if sums is not None:
            far = 6
            pieces = pieces[: n - far] + [in_hbm(piece) for piece in pieces[n - far :]]
            longest = max(piece.shape[0] for piece in pieces)
            return pl.pallas_call(
                lambda *refs: first_kernel(n, far, *refs),
                out_shape=(parts, jax.ShapeDtypeStruct((rows, half), jnp.float32)),
                in_specs=[smem()] * 7
                + [vmem()]
                + [anywhere()] * 2
                + [vmem()] * (n - far)
                + [anywhere()] * far,
                out_specs=(vmem(), vmem()),
                scratch_shapes=scratch
                + [
                    VMEM((TILE, TILE), jnp.float32),
                    VMEM((far, longest, half), jnp.int16),
                    pltpu.SemaphoreType.DMA((far,)),
                ],
                compiler_params=params(20),
                name="first_products",
            )(
                *where, sums.reshape(chips, per, TILE), *tiles, *pieces
            )
        return pl.pallas_call(
            lambda *refs: later_kernel(n, rows, *refs),
            out_shape=parts,
            in_specs=[smem()] * 7 + [anywhere()] * 2 + [vmem()] * n,
            out_specs=vmem(),
            scratch_shapes=scratch,
            compiler_params=params(20),
            name="later_products",
        )(*where, *tiles, *pieces)

    def update(parts, restart, inverse, scaled):
        return pl.pallas_call(
            lambda *refs: current_kernel(scaled, *refs),
            out_shape=jax.ShapeDtypeStruct(
                (per * TILE, half), jnp.bfloat16 if scaled else jnp.float32
            ),
            in_specs=[vmem()] * 3,
            out_specs=vmem(),
            compiler_params=params(6),
            name="current",
        )(parts, restart, inverse)

    pieces, names, found = gather(block, sums)
    other = sibling(found)
    sums = jnp.where(
        core == 0, jnp.concatenate([found, other]), jnp.concatenate([other, found])
    )
    parts, inverse = multiply(pieces, names, sums)
    parts, lists = tie((parts, seed_ids))
    restart = count_seeds(lists)
    parts = lax.all_to_all(parts, "row", 0, 0, tiled=True)
    panel = update(parts, restart, inverse, True)
    pieces, names, _ = gather(panel)
    parts = multiply(pieces, names, None)
    parts = lax.all_to_all(parts, "row", 0, 0, tiled=True)
    current = update(parts, restart, inverse, False)
    mine = lax.dynamic_slice_in_dim(current, core * own_rows, own_rows, 0)
    theirs = sibling(lax.dynamic_slice_in_dim(current, (1 - core) * own_rows, own_rows, 0))
    return jnp.where(
        core == 0,
        jnp.concatenate([mine, theirs], axis=1),
        jnp.concatenate([theirs, mine], axis=1),
    )


def solution(mesh):
    placed = (
        P(("row", "col"), None),
        P(("row", "col"), None, None),
        P(("row", "col")),
        P(("row", "col")),
        P(("row", "col")),
        P(),
    )
    return jax.shard_map(
        per_device, mesh=mesh, in_specs=placed, out_specs=P(("row", "col"), None), check_vma=False
    )
```

```python
import jax
import jax.numpy as jnp
from jax import lax
from jax.experimental import pallas as pl
from jax.experimental.pallas import tpu as pltpu
from jax.sharding import PartitionSpec as P

BT = 2
TILE = 128
LANES = 128
damping = 0.85
teleport = 0.15
LOW, HIGH = 0.2, 2.0
STEPS = 65535.0
HALF = 32768.0
FAR = 1 << 30
VMEM = pltpu.VMEM
SMEM = pltpu.SMEM


def vmem(*_):
    return pl.BlockSpec(memory_space=VMEM)


def smem(*_):
    return pl.BlockSpec(memory_space=SMEM)


def anywhere(*_):
    return pl.BlockSpec(memory_space=pl.ANY)


def in_hbm(value):
    return pltpu.with_memory_space_constraint(value, pltpu.HBM)


def params(mebibytes):
    return pltpu.CompilerParams(vmem_limit_bytes=mebibytes * 1024 * 1024)


def column_kernel(source_ref, count_ref, given_ref, sums_ref, tiles_ref, arrived):
    slots = given_ref.shape[0]
    chunk = slots // arrived.shape[0]
    copies = []
    for c in range(arrived.shape[0]):
        span = pl.ds(c * chunk, chunk)
        copies.append(
            pltpu.make_async_copy(given_ref.at[span], tiles_ref.at[span], arrived.at[c])
        )
        copies[c].start()
    sums_ref[...] = jnp.zeros_like(sums_ref)

    def group(g, carry):
        columns = [
            jnp.sum(tiles_ref[8 * g + u].astype(jnp.float32), axis=0, keepdims=True) for u in range(8)
        ]
        for u in range(8):
            k = 8 * g + u
            live = jnp.where(k < count_ref[0], 1.0, 0.0)
            sums_ref[pl.ds(source_ref[k] % sums_ref.shape[0], 1), :] += columns[u] * live
        return carry

    for c in range(arrived.shape[0]):
        copies[c].wait()
        last = jnp.minimum((c + 1) * chunk, count_ref[0])
        lax.fori_loop(c * chunk // 8, (last + 7) // 8, group, 0)


def encode(value):
    exponent = jnp.floor(jnp.log2(jnp.maximum(value, 1e-30))) + 1.0
    mantissa = (value * jnp.exp2(24.0 - exponent) + 0.5).astype(jnp.int32)
    mantissa = jnp.minimum(mantissa, (1 << 24) - 1)
    upper = (exponent.astype(jnp.int32) + 127) * 256 + (mantissa >> 16)
    return (jnp.concatenate([upper, mantissa & 65535]) - 32768).astype(jnp.int16)


def decode(code):
    code = code.astype(jnp.int32) + 32768
    each = code.shape[0] // 2
    upper, lower = code[:each], code[each:]
    mantissa = ((upper & 255) * 65536 + lower).astype(jnp.float32)
    return mantissa * jnp.exp2(((upper >> 8) - (127 + 24)).astype(jnp.float32))


def seed_kernel(where_ref, all_ref, counts_ref, ids_ref, pages_ref, arrived):
    total, lanes = pages_ref.shape
    pages = counts_ref.shape[0]
    first = where_ref[0]
    mine = pl.ds(pl.multiple_of(where_ref[1] * lanes, lanes), lanes)
    copy = pltpu.make_async_copy(all_ref.at[mine], ids_ref, arrived)
    copy.start()
    chunk = 256
    counts_ref[...] = jnp.zeros_like(counts_ref)

    def fold(value, reduce):
        parts = [value[i : i + 8] for i in range(0, value.shape[0], 8)]
        while len(parts) > 1:
            parts = [reduce(p, q) for p, q in zip(parts[::2], parts[1::2])]
        return parts[0]

    def rows(i):
        return pl.ds(pl.multiple_of(i * chunk, chunk), chunk)

    def more(carry):
        return carry[1] < pages

    def walk(carry):
        page_now, _ = carry

        def step(i, inner):
            best, seen = inner
            page = pages_ref[rows(i), :]
            found = jnp.where(page > page_now, page, FAR)
            same = jnp.where(page == page_now, 1.0, 0.0)
            return jnp.minimum(best, fold(found, jnp.minimum)), seen + fold(same, jnp.add)

        best, seen = lax.fori_loop(0, total // chunk, step, (far, jnp.zeros((8, lanes), jnp.float32)))
        seen = jnp.sum(seen, axis=0, keepdims=True)

        def place(i, inner):
            here = lax.broadcasted_iota(jnp.int32, (chunk, lanes), 0) + i * chunk
            counts_ref[rows(i), :] += jnp.where(here == page_now, seen, 0.0)
            return inner

        lax.fori_loop(0, pages // chunk, place, 0)
        later = jnp.min(best, axis=0, keepdims=True)
        return later, jnp.min(later)

    far = jnp.full((8, lanes), FAR, jnp.int32)
    best = far
    copy.wait()
    for i in range(0, total, lanes):
        page = ids_ref[:, i : i + lanes] - first
        page = jnp.where((page >= 0) & (page < pages), page, FAR)
        page = page.astype(jnp.float32).T.astype(jnp.int32)
        pages_ref[i : i + lanes, :] = page
        best = jnp.minimum(best, fold(page, jnp.minimum))
    start = jnp.min(best, axis=0, keepdims=True)
    lax.while_loop(more, walk, (start, jnp.min(start)))


def fetch(own_ref, sib_ref, tiles, arrived):
    slots = own_ref.shape[0]
    copies = [
        pltpu.make_async_copy(own_ref, tiles.at[pl.ds(0, slots)], arrived.at[0]),
        pltpu.make_async_copy(sib_ref, tiles.at[pl.ds(slots, slots)], arrived.at[1]),
    ]
    for copy in copies:
        copy.start()
    return copies


def single_products(slot_refs, count_ref, core_ref, copies, tiles, panel, total):
    unroll = 32
    slots = tiles.shape[0] // 2
    dummy = total.shape[0] - 1
    per = 2 * BT
    band = panel.shape[0] - 1
    for which in range(2):
        copies[which].wait()
        rows_ref, cols_ref = slot_refs[2 * which : 2 * which + 2]
        owner = core_ref[0] if which == 0 else 1 - core_ref[0]

        def group(g, carry, which=which, rows_ref=rows_ref, cols_ref=cols_ref, owner=owner):
            for u in range(unroll):
                k = g * unroll + u
                target = rows_ref[k] // band * per + owner * BT + rows_ref[k] % BT
                target = jnp.where(k < count_ref[which], target, dummy)
                total[target] += jnp.dot(
                    tiles[which * slots + k],
                    panel[cols_ref[k] % band],
                    preferred_element_type=jnp.float32,
                )
            return carry

        lax.fori_loop(0, (count_ref[which] + unroll - 1) // unroll, group, 0)


def round_parts(total, out_ref):
    receivers = out_ref.shape[0]
    per = (out_ref.shape[1] - 16) // TILE

    def send(r, carry):
        exponents = []
        for t in range(per):
            block = total[r * per + t]
            top = jnp.maximum(jnp.max(block, axis=0, keepdims=True), 1e-30)
            exponent = jnp.floor(jnp.log2(top)) + 1.0
            exponents.append(exponent)
            code = block * jnp.exp2(16.0 - exponent) + 0.5
            code = jnp.clip(code.astype(jnp.int32), 0, 65535) - 32768
            out_ref[r, t * TILE : (t + 1) * TILE, :] = code.astype(jnp.int16)
        rows = exponents + [jnp.zeros((16 - per, LANES), jnp.float32)]
        tail = jnp.concatenate(rows, axis=0).astype(jnp.int32).astype(jnp.int16)
        out_ref[r, per * TILE : per * TILE + 16, :] = tail
        return carry

    lax.fori_loop(0, receivers, send, 0)


def first_kernel(pieces, far, *refs):
    slot_refs, (count_ref, core_ref, chip_ref, sums_ref, own_ref, sib_ref) = refs[:4], refs[4:10]
    piece_refs = list(refs[10 : 10 + pieces])
    out_ref, inverse_ref, panel, total, tiles, arrived, ordered, brought, near = refs[10 + pieces :]
    brings = {}
    for i in range(far):
        p = pieces - far + i
        inside = brought.at[i, pl.ds(0, piece_refs[p].shape[0])]
        brings[p] = pltpu.make_async_copy(piece_refs[p], inside, near.at[i])
        brings[p].start()
        piece_refs[p] = inside
    copies = fetch(own_ref, sib_ref, tiles, arrived)
    total[...] = jnp.zeros_like(total)
    groups, per, _ = sums_ref.shape
    ordered[...] = jnp.zeros_like(ordered)
    for p in range(pieces):
        ordered[p * per : (p + 1) * per, :] = sums_ref[chip_ref[p]]
    inverse = (1.0 / jnp.maximum(ordered[...], 1.0)).T
    for p in range(pieces):
        if p in brings:
            brings[p].wait()
        for t in range(per):
            column = inverse[:, p * per + t : p * per + t + 1]
            code = piece_refs[p][t * TILE : (t + 1) * TILE, :].astype(jnp.float32)
            score = (code + HALF) * ((HIGH - LOW) / STEPS) + LOW
            panel[chip_ref[p] * per + t] = (score * column).astype(jnp.bfloat16)
            if p == 0:
                inverse_ref[t * TILE : (t + 1) * TILE, :] = jnp.broadcast_to(column, (TILE, LANES))
    single_products(slot_refs, count_ref, core_ref, copies, tiles, panel, total)
    round_parts(total, out_ref)


def later_kernel(pieces, rows, *refs):
    slot_refs, (count_ref, core_ref, chip_ref, own_ref, sib_ref) = refs[:4], refs[4:9]
    piece_refs = refs[9 : 9 + pieces]
    out_ref, panel, total, tiles, arrived = refs[9 + pieces :]
    copies = fetch(own_ref, sib_ref, tiles, arrived)
    total[...] = jnp.zeros_like(total)
    per = rows // TILE
    for p in range(pieces):
        for t in range(per):
            panel[chip_ref[p] * per + t] = piece_refs[p][t * TILE : (t + 1) * TILE, :]
    single_products(slot_refs, count_ref, core_ref, copies, tiles, panel, total)
    round_parts(total, out_ref)


def current_kernel(scaled, parts_ref, restart_ref, inverse_ref, out_ref):
    senders = parts_ref.shape[0]
    per = (parts_ref.shape[1] - 16) // TILE
    for t in range(per):
        rows = slice(t * TILE, (t + 1) * TILE)
        summed = jnp.zeros((TILE, LANES), jnp.float32)
        for r in range(senders):
            tail = parts_ref[r, per * TILE : per * TILE + 16, :].astype(jnp.float32)
            scale = jnp.exp2(tail[t : t + 1, :] - 16.0)
            summed += (parts_ref[r, rows, :].astype(jnp.float32) + HALF) * scale
        current = damping * summed + teleport * restart_ref[rows, :]
        if scaled:
            current = current * inverse_ref[rows, :]
        out_ref[rows, :] = current.astype(out_ref.dtype)


def per_device(scores, tile_values, tile_rows, tile_cols, tile_count, seed_ids):
    grid_rows = lax.axis_size("row")
    grid_cols = lax.axis_size("col")
    row_index = lax.axis_index("row")
    col_index = lax.axis_index("col")
    depth = grid_cols // 4
    high, z, core = col_index // (2 * depth), col_index // 2 % depth, col_index % 2
    own_rows = scores.shape[0]
    columns = scores.shape[1]
    slots = tile_values.shape[0]
    seed_total = seed_ids.shape[1]
    band_tiles = grid_cols * BT
    chips = grid_cols // 2
    per = 2 * BT

    def by_col(value, move):
        pairs = []
        for c in range(grid_cols):
            y, at, k = move(c // (2 * depth), c // 2 % depth, c % 2)
            pairs.append((c, (y * depth + at) * 2 + k))
        return lax.ppermute(value, "col", pairs)

    def sibling(value):
        return by_col(value, lambda y, at, k: (y, at, 1 - k))

    def along(value, step):
        return by_col(value, lambda y, at, k: (y, (at + step) % depth, k))

    def across(value):
        return by_col(value, lambda y, at, k: (1 - y, at, k))

    tie = lax.optimization_barrier

    def gather(block, sums=None):
        rows = block.shape[0]
        if sums is not None:
            block = jnp.concatenate([block, encode(sums)])
        other = across(block)
        pieces, names = [block, other], [(0, 0), (1, 0)]
        a, b, c, d = block, block, other, other
        for step in range(1, depth // 2):
            a, b = along(a, 1), along(b, -1)
            c, d = along(c, 1), along(d, -1)
            pieces += [a, b, c, d]
            names += [(0, -step), (0, step), (1, -step), (1, step)]
        pieces += [along(a, 1), along(d, -1)]
        names += [(0, depth // 2), (1, depth // 2)]
        if sums is not None:
            for piece in pieces[1:]:
                sums = sums + decode(piece[rows:])
        return pieces, names, sums

    half = columns // 2
    code = ((scores - LOW) * (STEPS / (HIGH - LOW)) + 0.5).astype(jnp.int32)
    code = (jnp.clip(code, 0, 65535) - 32768).astype(jnp.int16)
    mine = lax.dynamic_slice_in_dim(code, core * half, half, 1)
    theirs = sibling(lax.dynamic_slice_in_dim(code, (1 - core) * half, half, 1))
    block = jnp.where(
        core == 0, jnp.concatenate([mine, theirs]), jnp.concatenate([theirs, mine])
    )
    slots_here = jnp.stack([tile_rows, tile_cols, jnp.broadcast_to(tile_count, (slots,))])
    slots_there = sibling(slots_here)
    sib_tiles = sibling(tile_values)
    sums = pl.pallas_call(
        column_kernel,
        out_shape=jax.ShapeDtypeStruct((band_tiles, TILE), jnp.float32),
        in_specs=[smem(), smem(), anywhere()],
        out_specs=vmem(),
        scratch_shapes=[VMEM(tile_values.shape, tile_values.dtype), pltpu.SemaphoreType.DMA((4,))],
        compiler_params=params(8),
        name="column_sums",
    )(tile_cols, tile_count, in_hbm(tile_values))

    part = band_tiles // 2
    given = sibling(lax.dynamic_slice_in_dim(sums, (1 - core) * part, part, 0))
    sums = given + lax.dynamic_slice_in_dim(sums, core * part, part, 0)

    target_total = grid_rows * per

    def count_seeds(seed_ids):
        first_page = (row_index * grid_cols + col_index - core) * own_rows
        return pl.pallas_call(
            seed_kernel,
            out_shape=jax.ShapeDtypeStruct((2 * own_rows, half), jnp.float32),
            in_specs=[smem(), anywhere()],
            out_specs=vmem(),
            scratch_shapes=[
                VMEM((half, seed_total), jnp.int32),
                VMEM((seed_total, half), jnp.int32),
                pltpu.SemaphoreType.DMA,
            ],
            compiler_params=params(6),
            name="seed_counts",
        )(jnp.stack([first_page, core]), seed_ids)

    def multiply(pieces, names, sums):
        order = jnp.stack([(high ^ y) * depth + (z + d) % depth for y, d in names])
        n = len(pieces)
        rows = per * TILE
        parts = jax.ShapeDtypeStruct((grid_rows, rows + 16, half), jnp.int16)
        scratch = [
            VMEM((band_tiles + 1, TILE, half), jnp.bfloat16),
            VMEM((target_total + 1, TILE, half), jnp.float32),
            VMEM((2 * slots, TILE, TILE), tile_values.dtype),
            pltpu.SemaphoreType.DMA((2,)),
        ]
        tiles = (in_hbm(tile_values), in_hbm(sib_tiles))
        counts = jnp.concatenate([tile_count, slots_there[2, :1]])
        where = (tile_rows, tile_cols, slots_there[0], slots_there[1], counts, core.reshape(1), order)
        if sums is not None:
            far = 6
            pieces = pieces[: n - far] + [in_hbm(piece) for piece in pieces[n - far :]]
            longest = max(piece.shape[0] for piece in pieces)
            return pl.pallas_call(
                lambda *refs: first_kernel(n, far, *refs),
                out_shape=(parts, jax.ShapeDtypeStruct((rows, half), jnp.float32)),
                in_specs=[smem()] * 7
                + [vmem()]
                + [anywhere()] * 2
                + [vmem()] * (n - far)
                + [anywhere()] * far,
                out_specs=(vmem(), vmem()),
                scratch_shapes=scratch
                + [
                    VMEM((TILE, TILE), jnp.float32),
                    VMEM((far, longest, half), jnp.int16),
                    pltpu.SemaphoreType.DMA((far,)),
                ],
                compiler_params=params(20),
                name="first_products",
            )(
                *where, sums.reshape(chips, per, TILE), *tiles, *pieces
            )
        return pl.pallas_call(
            lambda *refs: later_kernel(n, rows, *refs),
            out_shape=parts,
            in_specs=[smem()] * 7 + [anywhere()] * 2 + [vmem()] * n,
            out_specs=vmem(),
            scratch_shapes=scratch,
            compiler_params=params(20),
            name="later_products",
        )(*where, *tiles, *pieces)

    def update(parts, restart, inverse, scaled):
        return pl.pallas_call(
            lambda *refs: current_kernel(scaled, *refs),
            out_shape=jax.ShapeDtypeStruct(
                (per * TILE, half), jnp.bfloat16 if scaled else jnp.float32
            ),
            in_specs=[vmem()] * 3,
            out_specs=vmem(),
            compiler_params=params(6),
            name="current",
        )(parts, restart, inverse)

    pieces, names, found = gather(block, sums)
    other = sibling(found)
    sums = jnp.where(
        core == 0, jnp.concatenate([found, other]), jnp.concatenate([other, found])
    )
    parts, inverse = multiply(pieces, names, sums)
    parts, lists = tie((parts, seed_ids))
    restart = count_seeds(lists)
    parts = lax.all_to_all(parts, "row", 0, 0, tiled=True)
    panel = update(parts, restart, inverse, True)
    pieces, names, _ = gather(panel)
    parts = multiply(pieces, names, None)
    parts = lax.all_to_all(parts, "row", 0, 0, tiled=True)
    current = update(parts, restart, inverse, False)
    mine = lax.dynamic_slice_in_dim(current, core * own_rows, own_rows, 0)
    theirs = sibling(lax.dynamic_slice_in_dim(current, (1 - core) * own_rows, own_rows, 0))
    return jnp.where(
        core == 0,
        jnp.concatenate([mine, theirs], axis=1),
        jnp.concatenate([theirs, mine], axis=1),
    )


def solution(mesh):
    placed = (
        P(("row", "col"), None),
        P(("row", "col"), None, None),
        P(("row", "col")),
        P(("row", "col")),
        P(("row", "col")),
        P(),
    )
    return jax.shard_map(
        per_device, mesh=mesh, in_specs=placed, out_specs=P(("row", "col"), None), check_vma=False
    )
```
